32 devices in a mesh: grp: 4 (over x, core), shard: 8 (over z, y).
Axes of the slice: x: 2, y: 2, z: 4, core: 2. Of those that a mesh axis runs over, the one named last changes fastest.
Arguments:
- tokens: bfloat16 [4096, 1024], P(('grp', 'shard')), may hold values from -6 to 6
- cotangent: bfloat16 [4096, 1024], P(('grp', 'shard')), may hold values from -6 to 6
- item_ids: int32 [4096], P('grp'), may hold values from 0 to 2, as said below
- live_mask: int32 [4096], P('grp'), may hold values from 0 to 1, as said below
- qkv_weight: bfloat16 [1024, 3072], P('shard'), may hold values from -0.1875 to 0.1875
- out_weight: bfloat16 [1024, 1024], P('shard'), may hold values from -3 to 3
- up_weight: bfloat16 [1024, 4096], P('shard'), may hold values from -0.1875 to 0.1875
- down_weight: bfloat16 [4096, 1024], P('shard'), may hold values from -0.09375 to 0.09375
- norm_weight: bfloat16 [4, 1024], P(None, 'shard'), may hold values from -1.2 to 1.4, as said below
- qkv_master: float32 [1024, 3072], P(('grp', 'shard')), may hold values from -0.1875 to 0.1875
- qkv_first: float32 [1024, 3072], P(('grp', 'shard')), may hold values from -0.0546875 to 0.0546875
- qkv_second: float32 [1024, 3072], P(('grp', 'shard')), may hold values from 8.789063e-05 to 0.0003515625
- out_master: float32 [1024, 1024], P(('grp', 'shard')), may hold values from -3 to 3
- out_first: float32 [1024, 1024], P(('grp', 'shard')), may hold values from -0.0078125 to 0.0078125
- out_second: float32 [1024, 1024], P(('grp', 'shard')), may hold values from 2.1457672e-06 to 8.583069e-06
- up_master: float32 [1024, 4096], P(('grp', 'shard')), may hold values from -0.1875 to 0.1875
- up_first: float32 [1024, 4096], P(('grp', 'shard')), may hold values from -0.0390625 to 0.0390625
- up_second: float32 [1024, 4096], P(('grp', 'shard')), may hold values from 4.8828126e-05 to 0.0001953125
- down_master: float32 [4096, 1024], P(('grp', 'shard')), may hold values from -0.09375 to 0.09375
- down_first: float32 [4096, 1024], P(('grp', 'shard')), may hold values from -0.078125 to 0.078125
- down_second: float32 [4096, 1024], P(('grp', 'shard')), may hold values from 0.00015625 to 0.000625
- norm_master: float32 [4, 1024], P(None, ('grp', 'shard')), may hold values from -1.2 to 1.4, as said below
- norm_first: float32 [4, 1024], P(None, ('grp', 'shard')), may hold values from -0.75 to 0.75
- norm_second: float32 [4, 1024], P(None, ('grp', 'shard')), may hold values from 0.015625 to 0.0625
Outputs:
- block_out: float32 [4096, 1024], P(('grp', 'shard'))
- input_grad: float32 [4096, 1024], P(('grp', 'shard'))
- qkv_grad: float32 [1024, 3072], P(('grp', 'shard'))
- qkv_moment: float32 [1024, 3072], P(('grp', 'shard'))
- qkv_square: float32 [1024, 3072], P(('grp', 'shard'))
- qkv_fresh: float32 [1024, 3072], P(('grp', 'shard'))
- qkv_copy: bfloat16 [1024, 3072], P(('grp', 'shard'))
- out_grad: float32 [1024, 1024], P(('grp', 'shard'))
- out_moment: float32 [1024, 1024], P(('grp', 'shard'))
- out_square: float32 [1024, 1024], P(('grp', 'shard'))
- out_fresh: float32 [1024, 1024], P(('grp', 'shard'))
- out_copy: bfloat16 [1024, 1024], P(('grp', 'shard'))
- up_grad: float32 [1024, 4096], P(('grp', 'shard'))
- up_moment: float32 [1024, 4096], P(('grp', 'shard'))
- up_square: float32 [1024, 4096], P(('grp', 'shard'))
- up_fresh: float32 [1024, 4096], P(('grp', 'shard'))
- up_copy: bfloat16 [1024, 4096], P(('grp', 'shard'))
- down_grad: float32 [4096, 1024], P(('grp', 'shard'))
- down_moment: float32 [4096, 1024], P(('grp', 'shard'))
- down_square: float32 [4096, 1024], P(('grp', 'shard'))
- down_fresh: float32 [4096, 1024], P(('grp', 'shard'))
- down_copy: bfloat16 [4096, 1024], P(('grp', 'shard'))
- norm_grad: float32 [4, 1024], P(None, ('grp', 'shard'))
- norm_moment: float32 [4, 1024], P(None, ('grp', 'shard'))
- norm_square: float32 [4, 1024], P(None, ('grp', 'shard'))
- norm_fresh: float32 [4, 1024], P(None, ('grp', 'shard'))
- norm_copy: bfloat16 [4, 1024], P(None, ('grp', 'shard'))
The draws below stay inside these ranges and needn't reach their ends.
Inputs may be any that keep to these rules, and one draw needn't show every extreme that they name: `item_ids`: within each group of 1024 consecutive rows the item number never falls; item 1 starts at one of rows 1 to 63 of the group and ends in its last 64 rows, items 0 and 2 fill the rest. `live_mask`: the first row of every item is 1. `norm_weight`: rows 0 and 2 are gains, rows 1 and 3 biases. `norm_master`: rows 0 and 2 are gains, rows 1 and 3 biases.
All inputs are finite; a program needn't handle non-finite values.
Results may differ from the reference program's by a relative error of at most 0.018.
Values may be sent and summed in bfloat16 or wider, within the bound.
A program may use at most 256 MiB of HBM per device.

```python
import math
import jax
import jax.numpy as jnp
from jax import lax

D = 1024
HEADS = 16
HEAD_DIM = 64
FF = 4096
TOK_DEV = 128
STEP = 5
GROUPS = 4
G_TOK = 1024
TOKENS = 4096


def norm_rows(key):
    gain_key, shift_key = jax.random.split(key)
    gains = jax.random.uniform(gain_key, (2, D), jnp.float32, 0.6, 1.4)
    shifts = jnp.clip(0.3 * jax.random.normal(shift_key, (2, D), jnp.float32), -1.2, 1.2)
    return jnp.stack([gains[0], shifts[0], gains[1], shifts[1]])


def item_bounds(key):
    head_key, tail_key = jax.random.split(key)
    begins = jax.random.randint(head_key, (GROUPS,), 1, TOK_DEV // 2)
    ends = G_TOK - jax.random.randint(tail_key, (GROUPS,), 1, TOK_DEV // 2)
    return (begins, ends)


def draw_norm_weight(key, part):
    key = jax.random.fold_in(key, 11)
    return norm_rows(key).astype(jnp.bfloat16)


def draw_norm_master(key, part):
    key = jax.random.fold_in(key, 12)
    return norm_rows(key)


def draw_item_ids(key, part):
    begins, ends = item_bounds(key)
    position = jnp.arange(G_TOK, dtype=jnp.int32)[None, :]
    items = (position >= begins[:, None]).astype(jnp.int32) + (position >= ends[:, None]).astype(jnp.int32)
    return items.reshape(-1)


def draw_live_mask(key, part):
    begins, ends = item_bounds(key)
    key = jax.random.fold_in(key, 22)
    position = jnp.arange(G_TOK, dtype=jnp.int32)[None, :]
    group_index = jnp.arange(GROUPS, dtype=jnp.int32)[:, None]
    ticket = jax.random.randint(key, (GROUPS, G_TOK), 0, 3 * (GROUPS - 1))
    keep = ticket < GROUPS - 1 + 2 * group_index
    leading = (position == 0) | (position == begins[:, None]) | (position == ends[:, None])
    return (keep | leading).astype(jnp.int32).reshape(-1)


def shard_levels(stream_key, extent, cuts, low, largest):
    loudness, own = 1.0, jax.random.fold_in(stream_key, 6)
    for axis_at, parts in cuts:
        draws = jnp.exp(jax.random.uniform(jax.random.fold_in(own, axis_at), (parts,), jnp.float32, low / len(cuts), largest / len(cuts)))
        loudness = loudness * jnp.repeat(draws, extent[axis_at] // parts).reshape([-1 if axis == axis_at else 1 for axis in range(len(extent))])
    return loudness


def gaussian(rng, shape, width, limit, shards=(), kind=jnp.bfloat16):
    loudness = shard_levels(rng, shape, shards, -0.22, 0.18) if shards else 1.0
    drawn = jax.random.normal(rng, shape, jnp.float32) * width * loudness
    return jnp.minimum(jnp.maximum(drawn, -limit), limit).astype(kind)


def setup_inputs(seed: int = 0) -> dict:
    streams_of = jax.random.split(jax.random.key(seed), 25)
    return {
        "tokens": gaussian(streams_of[0], (TOKENS, D), 1.0, 6.0, ((0, 32),)),
        "cotangent": gaussian(streams_of[1], (TOKENS, D), 1.0, 6.0, ((0, 32),)),
        "item_ids": draw_item_ids(jax.random.fold_in(streams_of[24], 71), 0),
        "live_mask": draw_live_mask(jax.random.fold_in(streams_of[24], 71), 0),
        "qkv_weight": gaussian(streams_of[4], (D, 3 * D), D ** -0.5, 0.1875, ((0, 8),)),
        "out_weight": gaussian(streams_of[5], (D, D), (G_TOK ** 0.5 / 64), 3.0, ((0, 8),)),
        "up_weight": gaussian(streams_of[6], (D, FF), D ** -0.5, 0.1875, ((0, 8),)),
        "down_weight": gaussian(streams_of[7], (FF, D), FF ** -0.5, 0.09375, ((0, 8),)),
        "norm_weight": draw_norm_weight(jax.random.fold_in(streams_of[24], 71), 0),
        "qkv_master": gaussian(streams_of[9], (D, 3 * D), D ** -0.5, 0.1875, ((0, 32),), jnp.float32),
        "qkv_first": gaussian(streams_of[10], (D, 3 * D), (0.6 / TOKENS ** 0.5), 0.0546875, ((0, 32),), jnp.float32),
        "qkv_second": jnp.clip(jnp.exp(math.log(0.0003515625) - 1.3862944 * jax.random.uniform(streams_of[11], (D, 3 * D), jnp.float32) ** shard_levels(streams_of[11], (D, 3 * D), ((0, 32),), -0.2, 0.2)), 8.789062849245965e-05, 0.0003515625),
        "out_master": gaussian(streams_of[12], (D, D), (G_TOK ** 0.5 / 64), 3.0, ((0, 32),), jnp.float32),
        "out_first": gaussian(streams_of[13], (D, D), (3.0 / (G_TOK * TOKENS) ** 0.5), 0.0078125, ((0, 32),), jnp.float32),
        "out_second": jnp.clip(jnp.exp(math.log(8.58306884765625e-06) - 1.3862944 * jax.random.uniform(streams_of[14], (D, D), jnp.float32) ** shard_levels(streams_of[14], (D, D), ((0, 32),), -0.2, 0.2)), 2.1457672119140625e-06, 8.58306884765625e-06),
        "up_master": gaussian(streams_of[15], (D, FF), D ** -0.5, 0.1875, ((0, 32),), jnp.float32),
        "up_first": gaussian(streams_of[16], (D, FF), (0.45 / TOKENS ** 0.5), 0.0390625, ((0, 32),), jnp.float32),
        "up_second": jnp.clip(jnp.exp(math.log(0.0001953125) - 1.3862944 * jax.random.uniform(streams_of[17], (D, FF), jnp.float32) ** shard_levels(streams_of[17], (D, FF), ((0, 32),), -0.2, 0.2)), 4.882812572759576e-05, 0.0001953125),
        "down_master": gaussian(streams_of[18], (FF, D), FF ** -0.5, 0.09375, ((0, 32),), jnp.float32),
        "down_first": gaussian(streams_of[19], (FF, D), (0.8 / TOKENS ** 0.5), 0.078125, ((0, 32),), jnp.float32),
        "down_second": jnp.clip(jnp.exp(math.log(0.000625) - 1.3862944 * jax.random.uniform(streams_of[20], (FF, D), jnp.float32) ** shard_levels(streams_of[20], (FF, D), ((0, 32),), -0.2, 0.2)), 0.00015625, 0.000625),
        "norm_master": draw_norm_master(jax.random.fold_in(streams_of[24], 71), 0),
        "norm_first": gaussian(streams_of[22], (4, D), (0.5 * D ** 0.5 / (64 * GROUPS ** 0.5)), 0.75, ((1, 32),), jnp.float32),
        "norm_second": jnp.clip(jnp.exp(math.log(0.0625) - 1.3862944 * jax.random.uniform(streams_of[23], (4, D), jnp.float32) ** shard_levels(streams_of[23], (4, D), ((1, 32),), -0.2, 0.2)), 0.015625, 0.0625),
    }


highest = lax.Precision.HIGHEST

@jax.custom_vjp
def low(v):
    return lax.optimization_barrier(v.astype(jnp.bfloat16)).astype(jnp.float32)

@jax.custom_vjp
def low_back(v):
    return v

def low_keep(v):
    return (low(v), None)

def low_pass(kept, grad):
    return (grad,)

def back_keep(v):
    return (v, None)

def back_low(kept, grad):
    return (low(grad),)
low.defvjp(low_keep, low_pass)
low_back.defvjp(back_keep, back_low)

def matmul(left, right):
    return jnp.dot(left, right, preferred_element_type=jnp.float32, precision=highest)

def layer_norm(values, gain, shift):
    mean = lax.optimization_barrier(jnp.mean(values, -1, keepdims=True))
    centred = values - mean
    variance = lax.optimization_barrier(jnp.mean(centred * centred, -1, keepdims=True))
    return centred * lax.rsqrt(variance + 1e-06) * gain + shift

def group_attention(projected, group_items, group_live):
    queries = projected[:, :D].reshape(G_TOK, HEADS, HEAD_DIM)
    key_heads = projected[:, D:2 * D].reshape(G_TOK, HEADS, HEAD_DIM)
    value_heads = projected[:, 2 * D:].reshape(G_TOK, HEADS, HEAD_DIM)
    block_rows = math.gcd(G_TOK, 512)

    def one_block(first_row):
        query_block = lax.dynamic_slice_in_dim(queries, first_row, block_rows, 0)
        item_block = lax.dynamic_slice_in_dim(group_items, first_row, block_rows, 0)
        scores = jnp.einsum('qhd,khd->hqk', query_block, key_heads, precision=highest) * 0.125
        scores = low_back(scores)
        allowed = (item_block[:, None] == group_items[None, :]) & (group_live[None, :] > 0)
        scores = jnp.where(allowed[None], scores, -1e+30)
        peak = lax.optimization_barrier(jnp.max(scores, -1, keepdims=True))
        expo = jnp.exp(scores - peak)
        probs = low(expo / lax.optimization_barrier(jnp.sum(expo, -1, keepdims=True)))
        return jnp.einsum('hqk,khd->qhd', probs, value_heads, precision=highest)
    firsts = jnp.arange(G_TOK // block_rows, dtype=jnp.int32) * block_rows
    blocks = lax.map(jax.checkpoint(one_block), firsts)
    return blocks.reshape(G_TOK, D)

def adamw(summed, live_total, master, old_first, old_second, step_rate, shrink):
    gradient = summed / live_total
    moment = 0.5 * old_first + 0.5 * gradient
    square = 0.5 * old_second + 0.5 * gradient * gradient
    correction = 1.0 - 0.5 ** STEP
    updated = master - step_rate * (moment / correction / (jnp.sqrt(square / correction) + 1e-08) + shrink * master)
    return (gradient, moment, square, updated, updated.astype(jnp.bfloat16))

def reference(tokens, cotangent, item_ids, live_mask, qkv_weight, out_weight, up_weight, down_weight, norm_weight, qkv_master, qkv_first, qkv_second, out_master, out_first, out_second, up_master, up_first, up_second, down_master, down_first, down_second, norm_master, norm_first, norm_second):
    live_f = live_mask.astype(jnp.float32)

    def forward(qkv_mat, out_mat, up_mat, down_mat, norm_mat, inputs):

        def one_group(packed):
            group_in, group_items, group_live = packed
            first_low = low(layer_norm(group_in, norm_mat[0], norm_mat[1]))
            projected = low_back(low(matmul(first_low, qkv_mat)))
            attended = low_back(low(group_attention(projected, group_items, group_live)))
            mixed = group_in + low_back(matmul(attended, out_mat))
            second_low = low(layer_norm(mixed, norm_mat[2], norm_mat[3]))
            expanded = low_back(matmul(second_low, up_mat))
            activated = low(jax.nn.gelu(expanded, approximate=False))
            return mixed + low_back(matmul(activated, down_mat))
        packed = (inputs.reshape(GROUPS, G_TOK, D), item_ids.reshape(GROUPS, G_TOK), live_f.reshape(GROUPS, G_TOK))
        return lax.map(jax.checkpoint(one_group), packed).reshape(TOKENS, D)
    block_out, pull = jax.vjp(forward, qkv_weight.astype(jnp.float32), out_weight.astype(jnp.float32), up_weight.astype(jnp.float32), down_weight.astype(jnp.float32), norm_weight.astype(jnp.float32), tokens.astype(jnp.float32))
    grads = pull(cotangent.astype(jnp.float32) * live_f[:, None])
    live_total = jnp.sum(live_f)
    qkv_grad, qkv_moment, qkv_square, qkv_fresh, qkv_copy = adamw(grads[0], live_total, qkv_master, qkv_first, qkv_second, D ** (-0.5), 0.1)
    out_grad, out_moment, out_square, out_fresh, out_copy = adamw(grads[1], live_total, out_master, out_first, out_second, G_TOK ** 0.5 / 64, 0.1)
    up_grad, up_moment, up_square, up_fresh, up_copy = adamw(grads[2], live_total, up_master, up_first, up_second, D ** (-0.5), 0.1)
    down_grad, down_moment, down_square, down_fresh, down_copy = adamw(grads[3], live_total, down_master, down_first, down_second, FF ** (-0.5), 0.1)
    norm_grad, norm_moment, norm_square, norm_fresh, norm_copy = adamw(grads[4], live_total, norm_master, norm_first, norm_second, 0.4, 0.0)
    return (block_out, grads[5], qkv_grad, qkv_moment, qkv_square, qkv_fresh, qkv_copy, out_grad, out_moment, out_square, out_fresh, out_copy, up_grad, up_moment, up_square, up_fresh, up_copy, down_grad, down_moment, down_square, down_fresh, down_copy, norm_grad, norm_moment, norm_square, norm_fresh, norm_copy)
```

```python
import math

import jax
import jax.numpy as jnp
from jax import lax
from jax.experimental import pallas as pl
from jax.experimental.pallas import tpu as pltpu
from jax.sharding import PartitionSpec as P

HEADS = 16
HEAD_DIM = 64
STEP = 5


eps_norm = 1e-06
score_scale = 0.125


def exact_gelu(inputs):
    return jax.nn.gelu(inputs, approximate=False)


def outer_sum(left, right):
    return lax.dot_general(
        left, right, (((0,), (0,)), ((), ())), preferred_element_type=jnp.float32
    )


def back_dot(gradient, weight):
    return lax.dot_general(
        gradient, weight, (((1,), (1,)), ((), ())), preferred_element_type=jnp.float32
    )


def norm_forward(values, gain, shift):
    mean = jnp.mean(values, -1, keepdims=True)
    centred = values - mean
    variance = jnp.mean(centred * centred, -1, keepdims=True)
    inverse = lax.rsqrt(variance + eps_norm)
    normed = centred * inverse
    return (normed * gain + shift, normed, inverse)


def norm_backward(upstream, normed, inverse, gain):
    scaled = upstream * gain
    mean_one = jnp.mean(scaled, -1, keepdims=True)
    mean_two = jnp.mean(scaled * normed, -1, keepdims=True)
    return (
        inverse * (scaled - mean_one - normed * mean_two),
        jnp.sum(upstream * normed, 0),
        jnp.sum(upstream, 0),
    )


def block_scores(queries, query_items, key_heads, key_items, key_live):
    scores = (
        jnp.einsum("qhd,khd->qhk", queries, key_heads, preferred_element_type=jnp.float32)
        * score_scale
    )
    allowed = (query_items[:, None] == key_items[None, :]) & (key_live[None, :] > 0)
    return (scores, allowed[:, None, :])


def score_grads(
    queries, query_items, grad_out, log_total, grad_dot, key_heads, value_heads, key_items, key_live
):
    scores, allowed = block_scores(queries, query_items, key_heads, key_items, key_live)
    attention = jnp.where(allowed, jnp.exp(scores - log_total[..., None]), 0.0)
    grad_attention = jnp.einsum(
        "qhd,khd->qhk", grad_out, value_heads, preferred_element_type=jnp.float32
    )
    grad_scores = (attention * (grad_attention - grad_dot[..., None])).astype(jnp.bfloat16)
    return (grad_scores, attention.astype(jnp.bfloat16))


def key_terms(grad_scores, attention_low, queries, grad_out):
    grad_key = (
        jnp.einsum("qhk,qhd->khd", grad_scores, queries, preferred_element_type=jnp.float32)
        * score_scale
    )
    grad_value = jnp.einsum(
        "qhk,qhd->khd", attention_low, grad_out, preferred_element_type=jnp.float32
    )
    return (grad_key, grad_value)


def query_term(grad_scores, key_heads):
    return (
        jnp.einsum("qhk,khd->qhd", grad_scores, key_heads, preferred_element_type=jnp.float32)
        * score_scale
    )


def key_blocks(shard_piece, item_ids, live_mask):
    piece_rows = shard_piece.shape[0]
    block_rows = math.gcd(piece_rows, 512)
    block_count = piece_rows // block_rows
    heads = shard_piece.reshape(block_count, block_rows, 2, HEADS, HEAD_DIM)
    key_items = item_ids.reshape(block_count, block_rows)
    key_live = live_mask.reshape(block_count, block_rows)
    return (heads[:, :, 0], heads[:, :, 1], key_items, key_live, block_rows)


def attend_fold(queries, query_items, item_ids, live_mask, carried, shard_piece):
    key_heads, value_heads, key_items, key_live, block_rows = key_blocks(
        shard_piece, item_ids, live_mask
    )

    def attend_advance(running, current):
        running_max, running_sum, weighted_sum = running
        key_block, value_block, item_block, live_block = current
        scores, allowed = block_scores(queries, query_items, key_block, item_block, live_block)
        new_max = jnp.maximum(running_max, jnp.max(jnp.where(allowed, scores, -1e30), -1))
        attention = jnp.where(allowed, jnp.exp(scores - new_max[..., None]), 0.0)
        factor = jnp.exp(running_max - new_max)
        running_sum = running_sum * factor + jnp.sum(attention, -1)
        weighted_sum = weighted_sum * factor[..., None] + jnp.einsum(
            "qhk,khd->qhd",
            attention.astype(jnp.bfloat16),
            value_block,
            preferred_element_type=jnp.float32,
        )
        return ((new_max, running_sum, weighted_sum), None)

    carried, _ = lax.scan(attend_advance, carried, (key_heads, value_heads, key_items, key_live))
    return carried


def summed_fold(queries, query_items, grad_out, log_total, grad_dot, item_ids, live_mask):

    def fold_keys(carried, shard_piece, first_row):
        grad_query, grad_pairs = carried
        key_heads, value_heads, key_items, key_live, block_rows = key_blocks(
            shard_piece, item_ids, live_mask
        )

        def fold_advance(running, current):
            key_block, value_block, item_block, live_block = current
            grad_scores, attention_low = score_grads(
                queries,
                query_items,
                grad_out,
                log_total,
                grad_dot,
                key_block,
                value_block,
                item_block,
                live_block,
            )
            grad_key, grad_value = key_terms(grad_scores, attention_low, queries, grad_out)
            paired = jnp.concatenate(
                [grad_key.reshape(block_rows, -1), grad_value.reshape(block_rows, -1)], 1
            )
            return (running + query_term(grad_scores, key_block), paired)

        grad_query, pieces = lax.scan(
            fold_advance, grad_query, (key_heads, value_heads, key_items, key_live)
        )
        grad_pairs = pieces.reshape(shard_piece.shape[0], -1)
        return (grad_query, grad_pairs)

    return fold_keys


def adamw(summed, live_total, master, old_first, old_second, step_rate, shrink):
    gradient = summed / live_total
    moment = 0.5 * old_first + 0.5 * gradient
    square = 0.5 * old_second + 0.5 * gradient * gradient
    correction = 1.0 - 0.5**STEP
    updated = master - step_rate * (
        moment / correction / (jnp.sqrt(square / correction) + 1e-08) + shrink * master
    )
    return (gradient, moment, square, updated, updated.astype(jnp.bfloat16))


def body(
    tokens,
    cotangent,
    item_ids,
    live_mask,
    qkv_weight,
    out_weight,
    up_weight,
    down_weight,
    norm_weight,
    qkv_master,
    qkv_first,
    qkv_second,
    out_master,
    out_first,
    out_second,
    up_master,
    up_first,
    up_second,
    down_master,
    down_first,
    down_second,
    norm_master,
    norm_first,
    norm_second,
):
    local_rows = tokens.shape[0]
    model_width = tokens.shape[1]
    group_rows = item_ids.shape[0]
    offset = lax.axis_index("shard") * local_rows
    qkv_full, out_full, up_full, down_full, norm_full = (
        lax.all_gather(qkv_weight, "shard", axis=0, tiled=True),
        lax.all_gather(out_weight, "shard", axis=0, tiled=True),
        lax.all_gather(up_weight, "shard", axis=0, tiled=True),
        lax.all_gather(down_weight, "shard", axis=0, tiled=True),
        lax.all_gather(norm_weight, "shard", axis=1, tiled=True),
    )
    hidden = up_full.shape[1]
    norm_values = norm_full.astype(jnp.float32)
    live_rows = lax.dynamic_slice_in_dim(live_mask, offset, local_rows)
    query_items = lax.dynamic_slice_in_dim(item_ids, offset, local_rows)
    group_count = jnp.sum(live_mask).astype(jnp.float32)
    total_count = lax.psum(group_count, "grp")
    inputs = tokens.astype(jnp.float32)
    first_norm, normed_one, inverse_one = norm_forward(inputs, norm_values[0], norm_values[1])
    first_low = first_norm.astype(jnp.bfloat16)
    projected = jnp.dot(first_low, qkv_full, preferred_element_type=jnp.float32).astype(
        jnp.bfloat16
    )
    query_flat = projected[:, :model_width]
    queries = query_flat.reshape(local_rows, HEADS, HEAD_DIM)
    key_values = projected[:, model_width:]
    start_state = (
        jnp.full((local_rows, HEADS), -1e30, jnp.float32),
        jnp.zeros((local_rows, HEADS), jnp.float32),
        jnp.zeros((local_rows, HEADS, HEAD_DIM), jnp.float32),
    )
    running_max, running_sum, weighted_sum = attend_fold(
        queries,
        query_items,
        item_ids,
        live_mask,
        start_state,
        lax.all_gather(key_values, "shard", axis=0, tiled=True),
    )
    attended = weighted_sum / running_sum[..., None]
    log_total = running_max + jnp.log(running_sum)
    attended_low = attended.reshape(local_rows, model_width).astype(jnp.bfloat16)
    mixed = inputs + jnp.dot(attended_low, out_full, preferred_element_type=jnp.float32)
    second_norm, normed_two, inverse_two = norm_forward(mixed, norm_values[2], norm_values[3])
    second_low = second_norm.astype(jnp.bfloat16)
    expanded = jnp.dot(second_low, up_full, preferred_element_type=jnp.float32)
    activated, gelu_pull = jax.vjp(exact_gelu, expanded)
    activated_low = activated.astype(jnp.bfloat16)
    block_out = mixed + jnp.dot(activated_low, down_full, preferred_element_type=jnp.float32)
    upstream = cotangent.astype(jnp.float32) * live_rows.astype(jnp.float32)[:, None]
    upstream_low = upstream.astype(jnp.bfloat16)
    down_term = outer_sum(activated_low, upstream_low)
    (grad_expanded,) = gelu_pull(back_dot(upstream_low, down_full))
    expanded_low = grad_expanded.astype(jnp.bfloat16)
    up_term = outer_sum(second_low, expanded_low)
    grad_mixed, gain_two, shift_two = norm_backward(
        back_dot(expanded_low, up_full), normed_two, inverse_two, norm_values[2]
    )
    grad_mixed = grad_mixed + upstream
    mixed_low = grad_mixed.astype(jnp.bfloat16)
    out_term = outer_sum(attended_low, mixed_low)
    grad_flat = back_dot(mixed_low, out_full).astype(jnp.bfloat16)
    grad_attended = grad_flat.reshape(local_rows, HEADS, HEAD_DIM)
    grad_dot = jnp.sum(grad_attended.astype(jnp.float32) * attended, -1)
    zero_query = jnp.zeros((local_rows, HEADS, HEAD_DIM), jnp.float32)
    fold_back = summed_fold(
        queries, query_items, grad_attended, log_total, grad_dot, item_ids, live_mask
    )
    start_back = (zero_query, jnp.zeros((group_rows, 2 * model_width), jnp.float32))
    folded = fold_back(
        start_back, lax.all_gather(key_values, "shard", axis=0, tiled=True), jnp.int32(0)
    )
    grad_query, grad_pairs = folded
    grad_kv = lax.psum_scatter(
        grad_pairs.astype(jnp.bfloat16), "shard", scatter_dimension=0, tiled=True
    ).astype(jnp.float32)
    grad_projected = jnp.concatenate(
        [grad_query.reshape(local_rows, model_width), grad_kv], 1
    ).astype(jnp.bfloat16)
    qkv_term = outer_sum(first_low, grad_projected)
    grad_first, gain_one, shift_one = norm_backward(
        back_dot(grad_projected, qkv_full), normed_one, inverse_one, norm_values[0]
    )
    input_grad = grad_first + grad_mixed
    norm_term = jnp.stack([gain_one, shift_one, gain_two, shift_two])
    qkv_sum, out_sum, up_sum, down_sum, norm_sum = (
        lax.psum_scatter(qkv_term, ("grp", "shard"), scatter_dimension=0, tiled=True),
        lax.psum_scatter(out_term, ("grp", "shard"), scatter_dimension=0, tiled=True),
        lax.psum_scatter(up_term, ("grp", "shard"), scatter_dimension=0, tiled=True),
        lax.psum_scatter(down_term, ("grp", "shard"), scatter_dimension=0, tiled=True),
        lax.psum_scatter(norm_term, ("grp", "shard"), scatter_dimension=1, tiled=True),
    )
    qkv_grad, qkv_moment, qkv_square, qkv_fresh, qkv_copy = adamw(
        qkv_sum, total_count, qkv_master, qkv_first, qkv_second, model_width ** (-0.5), 0.1
    )
    out_grad, out_moment, out_square, out_fresh, out_copy = adamw(
        out_sum, total_count, out_master, out_first, out_second, math.sqrt(group_rows) / 64, 0.1
    )
    up_grad, up_moment, up_square, up_fresh, up_copy = adamw(
        up_sum, total_count, up_master, up_first, up_second, model_width ** (-0.5), 0.1
    )
    down_grad, down_moment, down_square, down_fresh, down_copy = adamw(
        down_sum, total_count, down_master, down_first, down_second, hidden ** (-0.5), 0.1
    )
    norm_grad, norm_moment, norm_square, norm_fresh, norm_copy = adamw(
        norm_sum, total_count, norm_master, norm_first, norm_second, 0.4, 0.0
    )
    return (
        block_out,
        input_grad,
        qkv_grad,
        qkv_moment,
        qkv_square,
        qkv_fresh,
        qkv_copy,
        out_grad,
        out_moment,
        out_square,
        out_fresh,
        out_copy,
        up_grad,
        up_moment,
        up_square,
        up_fresh,
        up_copy,
        down_grad,
        down_moment,
        down_square,
        down_fresh,
        down_copy,
        norm_grad,
        norm_moment,
        norm_square,
        norm_fresh,
        norm_copy,
    )


MESH = pl.DeviceIdType.MESH
F32, LOW = jnp.float32, jnp.bfloat16
VMEM = pl.BlockSpec(memory_space=pltpu.VMEM)
SHARDS, GROUPS = 8, 4
WIDTH, ROWS, HALF = 1024, 128, 64
LANES = 128
DMA = pltpu.SemaphoreType.DMA


class Place:
    def __init__(self):
        self.g, self.s = lax.axis_index("grp"), lax.axis_index("shard")
        self.z, self.y = self.s // 2, self.s % 2
        self.x, self.c = self.g // 2, self.g % 2
        self.across = (self.g, self.s + 1 - 2 * self.y)
        self.up = (self.g, self.s + 2)
        self.down = (self.g, self.s - 2)
        self.sibling = (self.g + 1 - 2 * self.c, self.s)
        self.beside = ((self.g + 2) % GROUPS, self.s)

    def at_shard(self, k):
        return (self.g, (self.s + k) % SHARDS)

    def from_shard(self, k):
        return (self.s + SHARDS - k) % SHARDS


def remote(src, dst, send, recv, device):
    return pltpu.make_async_remote_copy(
        src_ref=src, dst_ref=dst, send_sem=send, recv_sem=recv, device_id=device, device_id_type=MESH
    )


def greet(devices):
    barrier = pltpu.get_barrier_semaphore()
    for device in devices:
        pl.semaphore_signal(barrier, inc=1, device_id=device, device_id_type=MESH)
    pl.semaphore_wait(barrier, len(devices))


def rows_of(ref):
    return ref[...].reshape(-1, ref.shape[-1])


def dot(left, right):
    return lax.dot_general(left, right, (((1,), (0,)), ((), ())), preferred_element_type=F32)


def dot_nt(left, right):
    return lax.dot_general(left, right, (((1,), (1,)), ((), ())), preferred_element_type=F32)


def dot_tn(left, right):
    return lax.dot_general(left, right, (((0,), (0,)), ((), ())), preferred_element_type=F32)


def gather_sems():
    return [DMA((3, 4)), DMA((SHARDS,))]


def plane_gather(here, block, sems):
    send, recv = sems
    z, y, s = here.z, here.y, here.s

    def copy(lane, zz, yy):
        device = (here.across, here.up, here.down)[lane]
        i = zz * 2 + yy
        return remote(block(i), block(i), send.at[lane, zz], recv.at[i], device)

    def arrived(zz, yy):
        copy(0, zz, yy).wait_recv()

    @pl.when(z < 3)
    def _():
        copy(1, z, y).start()

    @pl.when(z > 0)
    def _():
        copy(2, z, y).start()

    copy(0, z, y).start()
    yield
    for step in range(1, 4):

        @pl.when(z >= step)
        def _():
            zz = z - step
            arrived(zz, y)

            @pl.when(z < 3)
            def _():
                copy(1, zz, y).start()

            copy(0, zz, y).start()

        @pl.when(z + step <= 3)
        def _():
            zz = z + step
            arrived(zz, y)

            @pl.when(z > 0)
            def _():
                copy(2, zz, y).start()

            copy(0, zz, y).start()

        yield
    for zz in range(4):
        arrived(zz, 1 - y)
        copy(0, zz, y).wait_send()

        @pl.when((zz <= z) & (z < 3))
        def _():
            copy(1, zz, y).wait_send()

        @pl.when((zz >= z) & (z > 0))
        def _():
            copy(2, zz, y).wait_send()

    yield


def sum_sems():
    return [DMA((4,)), DMA((4,)), DMA((3,)), DMA((3,))]


def sum_scratch(cols):
    return [
        pltpu.VMEM((4, ROWS, cols), LOW),
        pltpu.VMEM((3, ROWS, cols), LOW),
        pltpu.VMEM((3, ROWS, cols), LOW),
    ]


def plane_sum(here, part, total, scratch, sems):
    landed, ready, final = scratch
    y_send, y_recv, z_send, z_recv = sems
    z, y = here.z, here.y
    order = [(z + 2) % 4, 3 - z, z + 1 - 2 * (z % 2), z]
    first = [
        remote(part.at[zz * 2 + 1 - y], landed.at[i], y_send.at[i], y_recv.at[i], here.across)
        for i, zz in enumerate(order)
    ]
    second = [
        remote(ready.at[i], final.at[i], z_send.at[i], z_recv.at[i], (here.g, order[i] * 2 + y))
        for i in range(3)
    ]
    for copy in first:
        copy.start()
    yield
    for i, zz in enumerate(order):
        first[i].wait_recv()
        here_sum = part[zz * 2 + y].astype(F32) + landed[i].astype(F32)
        if i < 3:
            ready[i] = here_sum.astype(LOW)
            second[i].start()
        else:
            total[...] = here_sum
        yield
    for copy in second:
        copy.wait_recv()
    total[...] += final[0].astype(F32) + final[1].astype(F32) + final[2].astype(F32)
    for copy in first + second:
        copy.wait_send()
    yield


def cross_sems():
    return [DMA((2,)), DMA((2,)), DMA((1,)), DMA((1,))]


def cross_scratch(rows, cols):
    return [
        pltpu.VMEM((2, rows, cols), LOW),
        pltpu.VMEM((rows, cols), LOW),
        pltpu.VMEM((rows, cols), LOW),
    ]


def cross_sum(here, part, total, scratch, sems):
    landed, ready, final = scratch
    c_send, c_recv, x_send, x_recv = sems
    g, x, c = here.g, here.x, here.c
    first = [
        remote(part.at[xx * 2 + 1 - c], landed.at[xx], c_send.at[xx], c_recv.at[xx], here.sibling)
        for xx in range(2)
    ]
    second = remote(ready, final, x_send.at[0], x_recv.at[0], here.beside)
    for copy in first:
        copy.start()
    yield
    for copy in first:
        copy.wait_recv()
    ready[...] = (part[(1 - x) * 2 + c].astype(F32) + landed[1 - x].astype(F32)).astype(LOW)
    second.start()
    yield
    second.wait_recv()
    total[...] = (
        part[g].astype(F32) + landed[x].astype(F32) + final[...].astype(F32)
    ).astype(total.dtype).reshape(total.shape)
    for copy in first + [second]:
        copy.wait_send()
    yield


def trade_sems():
    return [DMA((SHARDS,)), DMA((SHARDS,))]


def plane_trade(here, mine, theirs, sems):
    send, recv = sems

    def copy(k):
        device = here.at_shard(k)
        return remote(mine.at[device[1]], theirs.at[here.s], send.at[k], recv.at[k], device)

    theirs[here.s] = mine[here.s]
    for k in range(1, SHARDS):
        copy(k).start()
    yield
    for k in range(1, SHARDS):
        copy(k).wait_recv()
    for k in range(1, SHARDS):
        copy(k).wait_send()
    yield


def run(*steps):
    for step in steps:
        for _ in step:
            pass


def centre(values):
    mean = jnp.mean(values, -1, keepdims=True)
    centred = values - mean
    variance = jnp.mean(centred * centred, -1, keepdims=True)
    inverse = lax.rsqrt(variance + eps_norm)
    return centred * inverse, inverse


def wide(norm, row):
    return jnp.concatenate([norm[j, row : row + 1, :] for j in range(SHARDS)], 1)


def head_lanes(rows):
    lane = lax.broadcasted_iota(jnp.int32, (rows, LANES), 1)
    return [lane < HEAD_DIM, lane >= HEAD_DIM]


def forward_kernel(
    tok, cot, own_items, key_items, live, own_norm, wqkv, wout, wup,
    norm, wq, wo, wu, a1, a2, dz, qkv, probs, attended, mixed, n2, r2,
    o_send, norm_send, norm_recv, wq_send, wq_recv, wq_sib, wu_send, wu_recv, wu_sib, wo_sib,
    o_ssem, o_rsem, a1_s, a1_r, wo_s, wo_r, dz_s, dz_r, a2_s, a2_r,
):
    here = Place()
    g, s, c = here.g, here.s, here.c
    greet([here.at_shard(k) for k in range(1, SHARDS)] + [here.sibling])
    half = pl.ds(pl.multiple_of(c * HALF, HALF), HALF)

    norm[s] = own_norm[...]

    def norm_copy(k):
        return remote(own_norm, norm.at[s], norm_send.at[k], norm_recv.at[k], here.at_shard(k))

    def column_copy(weight, held, send, recv, k, parts, width):
        device = here.at_shard(k)
        return [
            remote(
                weight.at[half, pl.ds(pl.multiple_of(j * WIDTH + device[1] * width, LANES), width)],
                held.at[s, c, :, pl.ds(j * width, width)],
                send.at[k],
                recv.at[k],
                device,
            )
            for j in range(parts)
        ]

    def whole(held, send, recv, k):
        return remote(
            held.at[here.from_shard(k), c], held.at[here.from_shard(k), c], send.at[k], recv.at[k], here.at_shard(k)
        )

    for k in range(1, SHARDS):
        norm_copy(k).start()
    for k in range(1, SHARDS):
        for copy in column_copy(wqkv, wq, wq_send, wq_recv, k, 3, LANES):
            copy.start()
    for j in range(3):
        wq[s, c, :, j * LANES : (j + 1) * LANES] = wqkv[
            half, pl.ds(pl.multiple_of(j * WIDTH + s * LANES, LANES), LANES)
        ]
    inputs = tok[...].astype(F32)
    n1, _ = centre(inputs)
    for k in range(1, SHARDS):
        norm_copy(k).wait_recv()
    a1[s] = (n1 * wide(norm, 0) + wide(norm, 1)).astype(LOW)
    step = plane_gather(here, lambda i: a1.at[i], (a1_s, a1_r))
    next(step)
    own = pl.ds(pl.multiple_of(s * ROWS, ROWS), ROWS)
    dz[s] = (cot[...].astype(F32) * live[own, :].astype(F32)).astype(LOW)
    for k in range(1, SHARDS):
        whole(wq, wq_send, wq_recv, k).wait_recv()
    wq_core = remote(wq.at[:, c], wq.at[:, c], wq_sib.at[0], wq_sib.at[1], here.sibling)
    wq_core.start()
    run(step)
    wq_core.wait_recv()

    wo[s, c] = wout[half, :]
    wo_step = plane_gather(here, lambda i: wo.at[i, c], (wo_s, wo_r))
    next(wo_step)

    weight = wq[...].reshape(WIDTH, 3 * LANES)

    def project(j, carry):
        qkv[j] = dot(a1[j], weight).astype(LOW)
        return carry

    lax.fori_loop(0, SHARDS, project, 0)
    keys = qkv[:, :, LANES : 2 * LANES].reshape(-1, LANES)
    values = qkv[:, :, 2 * LANES :].reshape(-1, LANES)
    mine = head_lanes(ROWS)

    def o_copy(k):
        device = here.at_shard(k)
        return remote(o_send.at[device[1]], attended.at[s], o_ssem.at[k], o_rsem.at[k], device)

    def attend(j):
        queries = qkv[j, :, :LANES]
        items = own_items[pl.ds(pl.multiple_of(j * ROWS, ROWS), ROWS), :]
        allowed = items == key_items[...]
        outs = []
        for h in range(2):
            scores = dot_nt(jnp.where(mine[h], queries, jnp.zeros_like(queries)), keys) * score_scale
            scores = jnp.where(allowed, scores, -1e30)
            peak = jnp.max(scores, -1, keepdims=True)
            expo = jnp.exp(scores - peak)
            chance = (expo / jnp.sum(expo, -1, keepdims=True)).astype(LOW)
            probs[h, j] = chance
            outs.append(dot(chance, values))
        return jnp.where(mine[0], outs[0], outs[1]).astype(LOW)

    def attend_step(k, carry):
        j = (s + k) % SHARDS
        o_send[j] = attend(j)
        o_copy(k).start()
        return carry

    lax.fori_loop(1, 3, attend_step, 0)
    next(wo_step)
    lax.fori_loop(3, 5, attend_step, 0)
    next(wo_step)
    lax.fori_loop(5, 7, attend_step, 0)
    next(wo_step)
    lax.fori_loop(7, 8, attend_step, 0)
    attended[s] = attend(s)
    run(wo_step)
    wo_core = remote(wo.at[:, c], wo.at[:, c], wo_sib.at[0], wo_sib.at[1], here.sibling)
    wo_core.start()

    for k in range(1, SHARDS):
        for copy in column_copy(wup, wu, wu_send, wu_recv, k, 1, 4 * LANES):
            copy.start()
    wu[s, c] = wup[half, pl.ds(pl.multiple_of(s * 4 * LANES, LANES), 4 * LANES)]
    dz_step = plane_gather(here, lambda i: dz.at[i], (dz_s, dz_r))
    next(dz_step)

    for k in range(1, SHARDS):
        o_copy(k).wait_recv()
    wo_core.wait_recv()
    flat = jnp.concatenate([attended[j] for j in range(SHARDS)], 1)
    h1 = inputs + dot(flat, wo[...].reshape(WIDTH, WIDTH))
    mixed[...] = h1
    normed, inverse = centre(h1)
    n2[...] = normed
    r2[...] = jnp.broadcast_to(inverse, (ROWS, LANES))
    a2[s] = (normed * wide(norm, 2) + wide(norm, 3)).astype(LOW)
    a2_step = plane_gather(here, lambda i: a2.at[i], (a2_s, a2_r))
    for _ in range(4):
        next(a2_step)
        next(dz_step)
    for k in range(1, SHARDS):
        whole(wu, wu_send, wu_recv, k).wait_recv()
    wu_core = remote(wu.at[:, c], wu.at[:, c], wu_sib.at[0], wu_sib.at[1], here.sibling)
    wu_core.start()
    run(dz_step, a2_step)
    wu_core.wait_recv()
    for k in range(1, SHARDS):
        norm_copy(k).wait_send()
        whole(wq, wq_send, wq_recv, k).wait_send()
        whole(wu, wu_send, wu_recv, k).wait_send()
        o_copy(k).wait_send()
    for copy in (wq_core, wo_core, wu_core):
        copy.wait_send()


def middle_kernel(
    a2, dz, wu, wd, wo, norm, n2, r2, live, cot, attended,
    ffn, gup, gdown, gout, grad_out, grad_mixed, norm_two,
    act, du, da2, total, do_send, lands, ready, final, y_s, y_r, z_s, z_r, o_ssem, o_rsem,
):
    here = Place()
    s = here.s
    greet([here.at_shard(k) for k in range(1, SHARDS)])
    up = wu[...].reshape(WIDTH, -1)

    def feed(j, carry):
        u = dot(a2[j], up)
        half_erf = 0.5 + 0.5 * lax.erf(u * (0.5**0.5))
        activated = (u * half_erf).astype(LOW)
        act[j] = activated
        slope = half_erf + u * jnp.exp(-0.5 * u * u) * (1.0 / math.sqrt(2.0 * math.pi))
        grad = (dot_nt(dz[j], wd[...]) * slope).astype(LOW)
        du[j] = grad
        da2[j] = dot_nt(grad, up).astype(LOW)
        return carry

    lax.fori_loop(0, SHARDS, feed, 0)
    step = plane_sum(here, da2, total, (lands, ready, final), (y_s, y_r, z_s, z_r))
    next(step)

    def rest(j, carry):
        ffn[j] = dot(act[j], wd[...]).astype(LOW)
        return carry

    lax.fori_loop(0, SHARDS, rest, 0)
    next(step)
    down = dot_tn(rows_of(act), rows_of(dz)).astype(LOW)
    gdown[...] = down.reshape(gdown.shape)
    next(step)
    gup[...] = dot_tn(rows_of(a2), rows_of(du)).astype(LOW).reshape(gup.shape)
    run(step)

    e = total[...]
    normed = n2[...]
    scaled = e * wide(norm, 2)
    mean_one = jnp.mean(scaled, -1, keepdims=True)
    mean_two = jnp.mean(scaled * normed, -1, keepdims=True)
    own = pl.ds(pl.multiple_of(s * ROWS, ROWS), ROWS)
    upstream = cot[...].astype(F32) * live[own, :].astype(F32)
    grad = r2[:, :1] * (scaled - mean_one - normed * mean_two) + upstream
    grad_mixed[...] = grad
    norm_two[0:1, :] = jnp.sum(e * normed, 0, keepdims=True)
    norm_two[1:2, :] = jnp.sum(e, 0, keepdims=True)
    low = grad.astype(LOW)
    for k in range(SHARDS):
        do_send[k] = dot_nt(low, wo[k].reshape(ROWS, WIDTH)).astype(LOW)
    trade = plane_trade(here, do_send, grad_out, (o_ssem, o_rsem))
    next(trade)
    flat = jnp.concatenate([attended[j] for j in range(SHARDS)], 1)
    gout[...] = dot_tn(flat, low).astype(LOW).reshape(gout.shape)
    run(trade)


def last_kernel(*refs):
    (
        qkv, probs, grad_out, a1, wq, norm, tok, ffn, gup, gdown, gout, norm_two, live,
        block_sum, dx, qkv_sum, up_sum, out_sum, down_sum, norm_sum,
        dqkv, da1, gq, first_total,
        *scratch,
    ) = refs
    scratch = list(scratch)

    def take(n):
        out = scratch[:n]
        del scratch[:n]
        return out

    here = Place()
    g, s = here.g, here.s
    gs = [(g + k) % GROUPS for k in range(1, GROUPS)]
    away = (s // 2, (s % 2) * 4 + g)
    home = (s // 4 + 2 * g, s % 4)
    home = (home[1], home[0])
    stays = (away[0] == g) & (away[1] == s)
    barrier = pltpu.get_barrier_semaphore()
    around = [here.at_shard(k) for k in range(1, SHARDS)] + [(k, s) for k in gs]
    for device in around:
        pl.semaphore_signal(barrier, inc=1, device_id=device, device_id_type=MESH)

    @pl.when(stays)
    def _():
        pl.semaphore_wait(barrier, len(around))

    @pl.when(jnp.logical_not(stays))
    def _():
        for device in (away, home):
            pl.semaphore_signal(barrier, inc=1, device_id=device, device_id_type=MESH)
        pl.semaphore_wait(barrier, len(around) + 2)

    ffn_scr, ffn_sem = take(3), take(4)
    d_scr, d_sem = take(3), take(4)
    cross = {}
    for name in ("up", "down", "out", "qkv"):
        cross[name] = (take(3), take(4), take(1)[0])
    trades = {}
    for name in ("up", "out", "qkv"):
        trades[name] = (take(1)[0], take(2))
    away_buf, away_sem = take(1)[0], take(1)[0]
    norm_mine, norm_land, norm_all, n_s, n_r, m_s, m_r = take(7)

    steps = plane_sum(here, ffn, block_sum, ffn_scr, ffn_sem)
    next(steps)
    up_step = cross_sum(here, gup, cross["up"][2], cross["up"][0], cross["up"][1])
    down_step = cross_sum(here, gdown, cross["down"][2], cross["down"][0], cross["down"][1])
    out_step = cross_sum(here, gout, cross["out"][2], cross["out"][0], cross["out"][1])
    next(up_step)
    next(down_step)
    next(out_step)

    keys = qkv[:, :, LANES : 2 * LANES].reshape(-1, LANES)
    values = qkv[:, :, 2 * LANES :].reshape(-1, LANES)
    mine = head_lanes(ROWS)
    dqkv[...] = jnp.zeros_like(dqkv)

    def back(j, carry):
        queries, outs = qkv[j, :, :LANES], grad_out[j]
        grad_query, grad_key, grad_value = [], [], []
        for h in range(2):
            chance_low = probs[h, j]
            chance = chance_low.astype(F32)
            grad_chance = dot_nt(jnp.where(mine[h], outs, jnp.zeros_like(outs)), values)
            inner = jnp.sum(chance * grad_chance, -1, keepdims=True)
            grad_scores = (chance * (grad_chance - inner)).astype(LOW)
            grad_query.append(dot(grad_scores, keys))
            grad_key.append(dot_tn(grad_scores, queries))
            grad_value.append(dot_tn(chance_low, outs))
        dqkv[j, :, :LANES] = jnp.where(mine[0], grad_query[0], grad_query[1]) * score_scale
        wide_mine = head_lanes(WIDTH)[0]
        gk = jnp.where(wide_mine, grad_key[0], grad_key[1]) * score_scale
        gv = jnp.where(wide_mine, grad_value[0], grad_value[1])
        dqkv[:, :, LANES : 2 * LANES] += gk.reshape(SHARDS, ROWS, LANES)
        dqkv[:, :, 2 * LANES :] += gv.reshape(SHARDS, ROWS, LANES)
        return carry

    lax.fori_loop(0, SHARDS // 2, back, 0)
    next(steps)
    next(up_step)
    next(down_step)
    next(out_step)
    lax.fori_loop(SHARDS // 2, SHARDS, back, 0)
    weight = wq[...].reshape(WIDTH, 3 * LANES)

    def spread(j, carry):
        da1[j] = dot_nt(dqkv[j].astype(LOW), weight).astype(LOW)
        return carry

    lax.fori_loop(0, SHARDS, spread, 0)
    d_step = plane_sum(here, da1, first_total, d_scr, d_sem)
    next(d_step)
    gq[...] = dot_tn(rows_of(a1), rows_of(dqkv).astype(LOW)).astype(LOW).reshape(gq.shape)
    q_step = cross_sum(here, gq, cross["qkv"][2], cross["qkv"][0], cross["qkv"][1])
    next(q_step)
    run(up_step, down_step, out_step)
    up_trade = plane_trade(here, cross["up"][2], *trades["up"])
    out_trade = plane_trade(here, cross["out"][2], *trades["out"])
    next(up_trade)
    next(out_trade)
    moved = remote(cross["down"][2], away_buf, away_sem.at[0], away_sem.at[1], away)

    @pl.when(jnp.logical_not(stays))
    def _():
        moved.start()

    next(steps)
    next(d_step)
    run(q_step)
    qkv_trade = plane_trade(here, cross["qkv"][2], *trades["qkv"])
    next(qkv_trade)
    next(d_step)
    next(steps)
    run(d_step)

    e = first_total[...]
    normed, inverse = centre(tok[...].astype(F32))
    scaled = e * wide(norm, 0)
    mean_one = jnp.mean(scaled, -1, keepdims=True)
    mean_two = jnp.mean(scaled * normed, -1, keepdims=True)
    own = pl.ds(pl.multiple_of(s * ROWS, ROWS), ROWS)
    count = jnp.sum(live[own, :].astype(F32), 0, keepdims=True)
    part = jnp.concatenate(
        [
            jnp.sum(e * normed, 0, keepdims=True),
            jnp.sum(e, 0, keepdims=True),
            norm_two[0:2, :],
            jnp.broadcast_to(count, (4, WIDTH)),
        ],
        0,
    )
    for k in range(GROUPS):
        norm_mine[k] = part[:, k * 2 * LANES : (k + 1) * 2 * LANES]

    def grp_copy(k):
        to = (g + k) % GROUPS
        return remote(norm_mine.at[to], norm_land.at[k - 1], n_s.at[k], n_r.at[k], (to, s))

    for k in range(1, GROUPS):
        grp_copy(k).start()
    dx[...] = inverse * (scaled - mean_one - normed * mean_two)
    for k in range(1, GROUPS):
        grp_copy(k).wait_recv()
    norm_all[s] = norm_mine[g] + norm_land[0] + norm_land[1] + norm_land[2]

    def all_copy(k):
        return remote(norm_all.at[s], norm_all.at[s], m_s.at[k], m_r.at[k], here.at_shard(k))

    for k in range(1, SHARDS):
        all_copy(k).start()

    run(steps, up_trade, out_trade, qkv_trade)
    up_land, out_land, qkv_land = trades["up"][0], trades["out"][0], trades["qkv"][0]
    for j in range(SHARDS):
        up_sum[:, j * 512 : (j + 1) * 512] = up_land[j].astype(F32)
        for i in range(3):
            qkv_sum[:, i * WIDTH + j * LANES : i * WIDTH + (j + 1) * LANES] = qkv_land[
                j, :, i * LANES : (i + 1) * LANES
            ].astype(F32)
    gathered = out_land[0].astype(F32)
    for j in range(1, SHARDS):
        gathered += out_land[j].astype(F32)
    out_sum[...] = gathered

    @pl.when(stays)
    def _():
        down_sum[...] = cross["down"][2][...].astype(F32)

    @pl.when(jnp.logical_not(stays))
    def _():
        moved.wait_recv()
        down_sum[...] = away_buf[...].astype(F32)
        moved.wait_send()

    for k in range(1, SHARDS):
        all_copy(k).wait_recv()
    reduced = norm_all[0]
    for j in range(1, SHARDS):
        reduced += norm_all[j]
    norm_sum[...] = reduced
    for k in range(1, GROUPS):
        grp_copy(k).wait_send()
    for k in range(1, SHARDS):
        all_copy(k).wait_send()


def params(ident):
    return pltpu.CompilerParams(
        collective_id=ident, has_side_effects=True, vmem_limit_bytes=60 * 2**20
    )


def shaped(kind, *shape):
    return jax.ShapeDtypeStruct(shape, kind)


def call(kernel, ident, outs, scratch, args):
    return pl.pallas_call(
        kernel,
        out_shape=outs,
        in_specs=[VMEM] * len(args),
        out_specs=[VMEM] * len(outs),
        scratch_shapes=scratch,
        compiler_params=params(ident),
    )(*args)


def fast_body(
    tokens, cotangent, item_ids, live_mask, qkv_weight, out_weight, up_weight, down_weight, norm_weight,
    qkv_master, qkv_first, qkv_second, out_master, out_first, out_second, up_master, up_first, up_second,
    down_master, down_first, down_second, norm_master, norm_first, norm_second,
):
    rows = item_ids.shape[0]
    own_norm = jnp.pad(norm_weight.astype(F32), ((0, 4), (0, 0)))
    key_items = jnp.where(live_mask > 0, item_ids, -1).reshape(1, rows)
    own_items = item_ids.reshape(rows, 1)
    live = live_mask.reshape(rows, 1)
    norm, wq, wo, wu, a1, a2, dz, qkv, probs, attended, mixed, n2, r2 = call(
        forward_kernel,
        0,
        [
            shaped(F32, SHARDS, 8, LANES),
            shaped(LOW, SHARDS, 2, HALF, 3 * LANES),
            shaped(LOW, SHARDS, 2, HALF, WIDTH),
            shaped(LOW, SHARDS, 2, HALF, 4 * LANES),
            shaped(LOW, SHARDS, ROWS, WIDTH),
            shaped(LOW, SHARDS, ROWS, WIDTH),
            shaped(LOW, SHARDS, ROWS, WIDTH),
            shaped(LOW, SHARDS, ROWS, 3 * LANES),
            shaped(LOW, 2, SHARDS, ROWS, WIDTH),
            shaped(LOW, SHARDS, ROWS, LANES),
            shaped(F32, ROWS, WIDTH),
            shaped(F32, ROWS, WIDTH),
            shaped(F32, ROWS, LANES),
        ],
        [pltpu.VMEM((SHARDS, ROWS, LANES), LOW)]
        + [DMA((SHARDS,))] * 4
        + [DMA((2,))]
        + [DMA((SHARDS,))] * 2
        + [DMA((2,))] * 2
        + [DMA((SHARDS,))] * 2
        + gather_sems() * 4,
        (tokens, cotangent, own_items, key_items, live, own_norm, qkv_weight, out_weight, up_weight),
    )
    ffn, gup, gdown, gout, grad_out, grad_mixed, norm_two = call(
        middle_kernel,
        1,
        [
            shaped(LOW, SHARDS, ROWS, WIDTH),
            shaped(LOW, GROUPS, 256, 512),
            shaped(LOW, GROUPS, ROWS, WIDTH),
            shaped(LOW, GROUPS, 256, WIDTH),
            shaped(LOW, SHARDS, ROWS, LANES),
            shaped(F32, ROWS, WIDTH),
            shaped(F32, 8, WIDTH),
        ],
        [
            pltpu.VMEM((SHARDS, ROWS, 512), LOW),
            pltpu.VMEM((SHARDS, ROWS, 512), LOW),
            pltpu.VMEM((SHARDS, ROWS, WIDTH), LOW),
            pltpu.VMEM((ROWS, WIDTH), F32),
            pltpu.VMEM((SHARDS, ROWS, LANES), LOW),
        ]
        + sum_scratch(WIDTH)
        + sum_sems()
        + trade_sems(),
        (a2, dz, wu, down_weight, wo, norm, n2, r2, live, cotangent, attended),
    )
    scratch = [
        pltpu.VMEM((SHARDS, ROWS, 3 * LANES), F32),
        pltpu.VMEM((SHARDS, ROWS, WIDTH), LOW),
        pltpu.VMEM((GROUPS, 256, 3 * LANES), LOW),
        pltpu.VMEM((ROWS, WIDTH), F32),
    ]
    for _ in range(2):
        scratch += sum_scratch(WIDTH) + sum_sems()
    for r, cols in ((256, 512), (ROWS, WIDTH), (256, WIDTH), (256, 3 * LANES)):
        total = (SHARDS, r // SHARDS, cols) if r == 256 else (r, cols)
        scratch += cross_scratch(r, cols) + cross_sems() + [pltpu.VMEM(total, LOW)]
    for cols in (512, WIDTH, 3 * LANES):
        scratch += [pltpu.VMEM((SHARDS, 32, cols), LOW)] + trade_sems()
    scratch += [pltpu.VMEM((ROWS, WIDTH), LOW), DMA((2,))]
    scratch += [
        pltpu.VMEM((GROUPS, 8, 256), F32),
        pltpu.VMEM((GROUPS - 1, 8, 256), F32),
        pltpu.VMEM((SHARDS, 8, 256), F32),
        DMA((GROUPS,)),
        DMA((GROUPS,)),
        DMA((SHARDS,)),
        DMA((SHARDS,)),
    ]
    block_sum, dx, qkv_sum, up_sum, out_sum, down_sum, norm_sum = call(
        last_kernel,
        2,
        [
            shaped(F32, ROWS, WIDTH),
            shaped(F32, ROWS, WIDTH),
            shaped(F32, 32, 3 * WIDTH),
            shaped(F32, 32, 4 * WIDTH),
            shaped(F32, 32, WIDTH),
            shaped(F32, ROWS, WIDTH),
            shaped(F32, 8, 256),
        ],
        scratch,
        (qkv, probs, grad_out, a1, wq, norm, tokens, ffn, gup, gdown, gout, norm_two, live),
    )
    block_out = mixed + block_sum
    input_grad = dx + grad_mixed
    columns = norm_master.shape[1]
    norm_own = lax.dynamic_slice(norm_sum, (0, lax.axis_index("shard") * columns), (8, columns))
    total_count = norm_own[4, 0]
    model_width, hidden = tokens.shape[1], up_weight.shape[1]
    return (
        block_out,
        input_grad,
        *adamw(qkv_sum, total_count, qkv_master, qkv_first, qkv_second, model_width ** (-0.5), 0.1),
        *adamw(out_sum, total_count, out_master, out_first, out_second, math.sqrt(rows) / 64, 0.1),
        *adamw(up_sum, total_count, up_master, up_first, up_second, model_width ** (-0.5), 0.1),
        *adamw(down_sum, total_count, down_master, down_first, down_second, hidden ** (-0.5), 0.1),
        *adamw(norm_own[:4], total_count, norm_master, norm_first, norm_second, 0.4, 0.0),
    )


def suits(mesh):
    return mesh.shape["grp"] == GROUPS and mesh.shape["shard"] == SHARDS


def solution(mesh):
    placed = (
        P(("grp", "shard"), None),
        P(("grp", "shard"), None),
        P("grp"),
        P("grp"),
        P("shard", None),
        P("shard", None),
        P("shard", None),
        P("shard", None),
        P(None, "shard"),
        P(("grp", "shard"), None),
        P(("grp", "shard"), None),
        P(("grp", "shard"), None),
        P(("grp", "shard"), None),
        P(("grp", "shard"), None),
        P(("grp", "shard"), None),
        P(("grp", "shard"), None),
        P(("grp", "shard"), None),
        P(("grp", "shard"), None),
        P(("grp", "shard"), None),
        P(("grp", "shard"), None),
        P(("grp", "shard"), None),
        P(None, ("grp", "shard")),
        P(None, ("grp", "shard")),
        P(None, ("grp", "shard")),
    )
    return jax.shard_map(
        fast_body if suits(mesh) else body,
        mesh=mesh,
        in_specs=placed,
        out_specs=(
            P(("grp", "shard"), None),
            P(("grp", "shard"), None),
            P(("grp", "shard"), None),
            P(("grp", "shard"), None),
            P(("grp", "shard"), None),
            P(("grp", "shard"), None),
            P(("grp", "shard"), None),
            P(("grp", "shard"), None),
            P(("grp", "shard"), None),
            P(("grp", "shard"), None),
            P(("grp", "shard"), None),
            P(("grp", "shard"), None),
            P(("grp", "shard"), None),
            P(("grp", "shard"), None),
            P(("grp", "shard"), None),
            P(("grp", "shard"), None),
            P(("grp", "shard"), None),
            P(("grp", "shard"), None),
            P(("grp", "shard"), None),
            P(("grp", "shard"), None),
            P(("grp", "shard"), None),
            P(("grp", "shard"), None),
            P(None, ("grp", "shard")),
            P(None, ("grp", "shard")),
            P(None, ("grp", "shard")),
            P(None, ("grp", "shard")),
            P(None, ("grp", "shard")),
        ),
        check_vma=False,
    )
```

```python
import math

import jax
import jax.numpy as jnp
from jax import lax
from jax.experimental import pallas as pl
from jax.experimental.pallas import tpu as pltpu
from jax.sharding import PartitionSpec as P

HEADS = 16
HEAD_DIM = 64
STEP = 5


eps_norm = 1e-06
score_scale = 0.125


def exact_gelu(inputs):
    return jax.nn.gelu(inputs, approximate=False)


def outer_sum(left, right):
    return lax.dot_general(
        left, right, (((0,), (0,)), ((), ())), preferred_element_type=jnp.float32
    )


def back_dot(gradient, weight):
    return lax.dot_general(
        gradient, weight, (((1,), (1,)), ((), ())), preferred_element_type=jnp.float32
    )


def norm_forward(values, gain, shift):
    mean = jnp.mean(values, -1, keepdims=True)
    centred = values - mean
    variance = jnp.mean(centred * centred, -1, keepdims=True)
    inverse = lax.rsqrt(variance + eps_norm)
    normed = centred * inverse
    return (normed * gain + shift, normed, inverse)


def norm_backward(upstream, normed, inverse, gain):
    scaled = upstream * gain
    mean_one = jnp.mean(scaled, -1, keepdims=True)
    mean_two = jnp.mean(scaled * normed, -1, keepdims=True)
    return (
        inverse * (scaled - mean_one - normed * mean_two),
        jnp.sum(upstream * normed, 0),
        jnp.sum(upstream, 0),
    )


def block_scores(queries, query_items, key_heads, key_items, key_live):
    scores = (
        jnp.einsum("qhd,khd->qhk", queries, key_heads, preferred_element_type=jnp.float32)
        * score_scale
    )
    allowed = (query_items[:, None] == key_items[None, :]) & (key_live[None, :] > 0)
    return (scores, allowed[:, None, :])


def score_grads(
    queries, query_items, grad_out, log_total, grad_dot, key_heads, value_heads, key_items, key_live
):
    scores, allowed = block_scores(queries, query_items, key_heads, key_items, key_live)
    attention = jnp.where(allowed, jnp.exp(scores - log_total[..., None]), 0.0)
    grad_attention = jnp.einsum(
        "qhd,khd->qhk", grad_out, value_heads, preferred_element_type=jnp.float32
    )
    grad_scores = (attention * (grad_attention - grad_dot[..., None])).astype(jnp.bfloat16)
    return (grad_scores, attention.astype(jnp.bfloat16))


def key_terms(grad_scores, attention_low, queries, grad_out):
    grad_key = (
        jnp.einsum("qhk,qhd->khd", grad_scores, queries, preferred_element_type=jnp.float32)
        * score_scale
    )
    grad_value = jnp.einsum(
        "qhk,qhd->khd", attention_low, grad_out, preferred_element_type=jnp.float32
    )
    return (grad_key, grad_value)


def query_term(grad_scores, key_heads):
    return (
        jnp.einsum("qhk,khd->qhd", grad_scores, key_heads, preferred_element_type=jnp.float32)
        * score_scale
    )


def key_blocks(shard_piece, item_ids, live_mask):
    piece_rows = shard_piece.shape[0]
    block_rows = math.gcd(piece_rows, 512)
    block_count = piece_rows // block_rows
    heads = shard_piece.reshape(block_count, block_rows, 2, HEADS, HEAD_DIM)
    key_items = item_ids.reshape(block_count, block_rows)
    key_live = live_mask.reshape(block_count, block_rows)
    return (heads[:, :, 0], heads[:, :, 1], key_items, key_live, block_rows)


def attend_fold(queries, query_items, item_ids, live_mask, carried, shard_piece):
    key_heads, value_heads, key_items, key_live, block_rows = key_blocks(
        shard_piece, item_ids, live_mask
    )

    def attend_advance(running, current):
        running_max, running_sum, weighted_sum = running
        key_block, value_block, item_block, live_block = current
        scores, allowed = block_scores(queries, query_items, key_block, item_block, live_block)
        new_max = jnp.maximum(running_max, jnp.max(jnp.where(allowed, scores, -1e30), -1))
        attention = jnp.where(allowed, jnp.exp(scores - new_max[..., None]), 0.0)
        factor = jnp.exp(running_max - new_max)
        running_sum = running_sum * factor + jnp.sum(attention, -1)
        weighted_sum = weighted_sum * factor[..., None] + jnp.einsum(
            "qhk,khd->qhd",
            attention.astype(jnp.bfloat16),
            value_block,
            preferred_element_type=jnp.float32,
        )
        return ((new_max, running_sum, weighted_sum), None)

    carried, _ = lax.scan(attend_advance, carried, (key_heads, value_heads, key_items, key_live))
    return carried


def summed_fold(queries, query_items, grad_out, log_total, grad_dot, item_ids, live_mask):

    def fold_keys(carried, shard_piece, first_row):
        grad_query, grad_pairs = carried
        key_heads, value_heads, key_items, key_live, block_rows = key_blocks(
            shard_piece, item_ids, live_mask
        )

        def fold_advance(running, current):
            key_block, value_block, item_block, live_block = current
            grad_scores, attention_low = score_grads(
                queries,
                query_items,
                grad_out,
                log_total,
                grad_dot,
                key_block,
                value_block,
                item_block,
                live_block,
            )
            grad_key, grad_value = key_terms(grad_scores, attention_low, queries, grad_out)
            paired = jnp.concatenate(
                [grad_key.reshape(block_rows, -1), grad_value.reshape(block_rows, -1)], 1
            )
            return (running + query_term(grad_scores, key_block), paired)

        grad_query, pieces = lax.scan(
            fold_advance, grad_query, (key_heads, value_heads, key_items, key_live)
        )
        grad_pairs = pieces.reshape(shard_piece.shape[0], -1)
        return (grad_query, grad_pairs)

    return fold_keys


def adamw(summed, live_total, master, old_first, old_second, step_rate, shrink):
    gradient = summed / live_total
    moment = 0.5 * old_first + 0.5 * gradient
    square = 0.5 * old_second + 0.5 * gradient * gradient
    correction = 1.0 - 0.5**STEP
    updated = master - step_rate * (
        moment / correction / (jnp.sqrt(square / correction) + 1e-08) + shrink * master
    )
    return (gradient, moment, square, updated, updated.astype(jnp.bfloat16))


def body(
    tokens,
    cotangent,
    item_ids,
    live_mask,
    qkv_weight,
    out_weight,
    up_weight,
    down_weight,
    norm_weight,
    qkv_master,
    qkv_first,
    qkv_second,
    out_master,
    out_first,
    out_second,
    up_master,
    up_first,
    up_second,
    down_master,
    down_first,
    down_second,
    norm_master,
    norm_first,
    norm_second,
):
    local_rows = tokens.shape[0]
    model_width = tokens.shape[1]
    group_rows = item_ids.shape[0]
    offset = lax.axis_index("shard") * local_rows
    qkv_full, out_full, up_full, down_full, norm_full = (
        lax.all_gather(qkv_weight, "shard", axis=0, tiled=True),
        lax.all_gather(out_weight, "shard", axis=0, tiled=True),
        lax.all_gather(up_weight, "shard", axis=0, tiled=True),
        lax.all_gather(down_weight, "shard", axis=0, tiled=True),
        lax.all_gather(norm_weight, "shard", axis=1, tiled=True),
    )
    hidden = up_full.shape[1]
    norm_values = norm_full.astype(jnp.float32)
    live_rows = lax.dynamic_slice_in_dim(live_mask, offset, local_rows)
    query_items = lax.dynamic_slice_in_dim(item_ids, offset, local_rows)
    group_count = jnp.sum(live_mask).astype(jnp.float32)
    total_count = lax.psum(group_count, "grp")
    inputs = tokens.astype(jnp.float32)
    first_norm, normed_one, inverse_one = norm_forward(inputs, norm_values[0], norm_values[1])
    first_low = first_norm.astype(jnp.bfloat16)
    projected = jnp.dot(first_low, qkv_full, preferred_element_type=jnp.float32).astype(
        jnp.bfloat16
    )
    query_flat = projected[:, :model_width]
    queries = query_flat.reshape(local_rows, HEADS, HEAD_DIM)
    key_values = projected[:, model_width:]
    start_state = (
        jnp.full((local_rows, HEADS), -1e30, jnp.float32),
        jnp.zeros((local_rows, HEADS), jnp.float32),
        jnp.zeros((local_rows, HEADS, HEAD_DIM), jnp.float32),
    )
    running_max, running_sum, weighted_sum = attend_fold(
        queries,
        query_items,
        item_ids,
        live_mask,
        start_state,
        lax.all_gather(key_values, "shard", axis=0, tiled=True),
    )
    attended = weighted_sum / running_sum[..., None]
    log_total = running_max + jnp.log(running_sum)
    attended_low = attended.reshape(local_rows, model_width).astype(jnp.bfloat16)
    mixed = inputs + jnp.dot(attended_low, out_full, preferred_element_type=jnp.float32)
    second_norm, normed_two, inverse_two = norm_forward(mixed, norm_values[2], norm_values[3])
    second_low = second_norm.astype(jnp.bfloat16)
    expanded = jnp.dot(second_low, up_full, preferred_element_type=jnp.float32)
    activated, gelu_pull = jax.vjp(exact_gelu, expanded)
    activated_low = activated.astype(jnp.bfloat16)
    block_out = mixed + jnp.dot(activated_low, down_full, preferred_element_type=jnp.float32)
    upstream = cotangent.astype(jnp.float32) * live_rows.astype(jnp.float32)[:, None]
    upstream_low = upstream.astype(jnp.bfloat16)
    down_term = outer_sum(activated_low, upstream_low)
    (grad_expanded,) = gelu_pull(back_dot(upstream_low, down_full))
    expanded_low = grad_expanded.astype(jnp.bfloat16)
    up_term = outer_sum(second_low, expanded_low)
    grad_mixed, gain_two, shift_two = norm_backward(
        back_dot(expanded_low, up_full), normed_two, inverse_two, norm_values[2]
    )
    grad_mixed = grad_mixed + upstream
    mixed_low = grad_mixed.astype(jnp.bfloat16)
    out_term = outer_sum(attended_low, mixed_low)
    grad_flat = back_dot(mixed_low, out_full).astype(jnp.bfloat16)
    grad_attended = grad_flat.reshape(local_rows, HEADS, HEAD_DIM)
    grad_dot = jnp.sum(grad_attended.astype(jnp.float32) * attended, -1)
    zero_query = jnp.zeros((local_rows, HEADS, HEAD_DIM), jnp.float32)
    fold_back = summed_fold(
        queries, query_items, grad_attended, log_total, grad_dot, item_ids, live_mask
    )
    start_back = (zero_query, jnp.zeros((group_rows, 2 * model_width), jnp.float32))
    folded = fold_back(
        start_back, lax.all_gather(key_values, "shard", axis=0, tiled=True), jnp.int32(0)
    )
    grad_query, grad_pairs = folded
    grad_kv = lax.psum_scatter(
        grad_pairs.astype(jnp.bfloat16), "shard", scatter_dimension=0, tiled=True
    ).astype(jnp.float32)
    grad_projected = jnp.concatenate(
        [grad_query.reshape(local_rows, model_width), grad_kv], 1
    ).astype(jnp.bfloat16)
    qkv_term = outer_sum(first_low, grad_projected)
    grad_first, gain_one, shift_one = norm_backward(
        back_dot(grad_projected, qkv_full), normed_one, inverse_one, norm_values[0]
    )
    input_grad = grad_first + grad_mixed
    norm_term = jnp.stack([gain_one, shift_one, gain_two, shift_two])
    qkv_sum, out_sum, up_sum, down_sum, norm_sum = (
        lax.psum_scatter(qkv_term, ("grp", "shard"), scatter_dimension=0, tiled=True),
        lax.psum_scatter(out_term, ("grp", "shard"), scatter_dimension=0, tiled=True),
        lax.psum_scatter(up_term, ("grp", "shard"), scatter_dimension=0, tiled=True),
        lax.psum_scatter(down_term, ("grp", "shard"), scatter_dimension=0, tiled=True),
        lax.psum_scatter(norm_term, ("grp", "shard"), scatter_dimension=1, tiled=True),
    )
    qkv_grad, qkv_moment, qkv_square, qkv_fresh, qkv_copy = adamw(
        qkv_sum, total_count, qkv_master, qkv_first, qkv_second, model_width ** (-0.5), 0.1
    )
    out_grad, out_moment, out_square, out_fresh, out_copy = adamw(
        out_sum, total_count, out_master, out_first, out_second, math.sqrt(group_rows) / 64, 0.1
    )
    up_grad, up_moment, up_square, up_fresh, up_copy = adamw(
        up_sum, total_count, up_master, up_first, up_second, model_width ** (-0.5), 0.1
    )
    down_grad, down_moment, down_square, down_fresh, down_copy = adamw(
        down_sum, total_count, down_master, down_first, down_second, hidden ** (-0.5), 0.1
    )
    norm_grad, norm_moment, norm_square, norm_fresh, norm_copy = adamw(
        norm_sum, total_count, norm_master, norm_first, norm_second, 0.4, 0.0
    )
    return (
        block_out,
        input_grad,
        qkv_grad,
        qkv_moment,
        qkv_square,
        qkv_fresh,
        qkv_copy,
        out_grad,
        out_moment,
        out_square,
        out_fresh,
        out_copy,
        up_grad,
        up_moment,
        up_square,
        up_fresh,
        up_copy,
        down_grad,
        down_moment,
        down_square,
        down_fresh,
        down_copy,
        norm_grad,
        norm_moment,
        norm_square,
        norm_fresh,
        norm_copy,
    )


MESH = pl.DeviceIdType.MESH
F32, LOW = jnp.float32, jnp.bfloat16
VMEM = pl.BlockSpec(memory_space=pltpu.VMEM)
ANY = pl.BlockSpec(memory_space=pl.ANY)
SHARDS, GROUPS = 8, 4
WIDTH, ROWS, LANES = 1024, 128, 128
HIDDEN = 512
DMA = pltpu.SemaphoreType.DMA


class Place:
    def __init__(self):
        self.g, self.s = lax.axis_index("grp"), lax.axis_index("shard")
        self.z, self.y = self.s // 2, self.s % 2
        self.x, self.c = self.g // 2, self.g % 2
        self.half, self.near = self.z // 2, self.z % 2
        self.corner = self.near * 2 + self.y
        g, s = self.g, self.s
        over = 1 - 2 * self.y
        along = 2 - 4 * self.near
        self.across = (g, s + over)
        self.up = (g, s + 2)
        self.down = (g, s - 2)
        self.far = (g, (s + 4) % SHARDS)
        self.sibling = (g + 1 - 2 * self.c, s)
        self.beside = ((g + 2) % GROUPS, s)
        self.square = [(g, s), self.across, (g, s + along), (g, s + along + over)]
        self.corners = [
            self.corner,
            self.corner + over,
            (self.corner + 2) % 4,
            (self.corner + over + 2) % 4,
        ]

    def at_shard(self, k):
        return (self.g, (self.s + k) % SHARDS)

    def from_shard(self, k):
        return (self.s + SHARDS - k) % SHARDS


def remote(src, dst, send, recv, device):
    return pltpu.make_async_remote_copy(
        src_ref=src, dst_ref=dst, send_sem=send, recv_sem=recv, device_id=device, device_id_type=MESH
    )


def greet_all(here):
    barrier = pltpu.get_barrier_semaphore()
    me, everyone = here.g * SHARDS + here.s, GROUPS * SHARDS

    def greet(k, carry):
        other = (me + k) % everyone
        pl.semaphore_signal(
            barrier, inc=1, device_id=(other // SHARDS, other % SHARDS), device_id_type=MESH
        )
        return carry

    lax.fori_loop(1, everyone, greet, 0)
    pl.semaphore_wait(barrier, everyone - 1)


def flat(value):
    return value.reshape(-1, value.shape[-1])


def dot(left, right):
    return lax.dot_general(left, right, (((1,), (0,)), ((), ())), preferred_element_type=F32)


def dot_nt(left, right):
    return lax.dot_general(left, right, (((1,), (1,)), ((), ())), preferred_element_type=F32)


def dot_tn(left, right):
    return lax.dot_general(left, right, (((0,), (0,)), ((), ())), preferred_element_type=F32)


def run(*steps):
    for step in steps:
        for _ in step:
            pass


def buffer(kind, *shape):
    return pltpu.VMEM(shape, kind)


def gather_sems():
    return [DMA((3, 4)), DMA((SHARDS,))]


def plane_gather(here, block, sems, ends):
    send, recv = sems
    z, y = here.z, here.y

    def copy(lane, zz, yy):
        device = (here.across, here.up, here.down)[lane]
        i = zz * 2 + yy
        return remote(block(i), block(i), send.at[lane, zz], recv.at[i], device)

    def arrived(zz, yy):
        copy(0, zz, yy).wait_recv()

    def finish():
        for zz in range(4):
            copy(0, zz, y).wait_send()

            @pl.when((zz <= z) & (z < 3))
            def _():
                copy(1, zz, y).wait_send()

            @pl.when((zz >= z) & (z > 0))
            def _():
                copy(2, zz, y).wait_send()

    ends.append(finish)

    @pl.when(z < 3)
    def _():
        copy(1, z, y).start()

    @pl.when(z > 0)
    def _():
        copy(2, z, y).start()

    copy(0, z, y).start()
    yield
    for step in range(1, 4):

        @pl.when(z >= step)
        def _():
            zz = z - step
            arrived(zz, y)

            @pl.when(z < 3)
            def _():
                copy(1, zz, y).start()

            copy(0, zz, y).start()

        @pl.when(z + step <= 3)
        def _():
            zz = z + step
            arrived(zz, y)

            @pl.when(z > 0)
            def _():
                copy(2, zz, y).start()

            copy(0, zz, y).start()

        yield
    for zz in range(4):
        arrived(zz, 1 - y)
    yield


def sum_scratch(rows):
    shape = (4, rows, WIDTH)
    return [buffer(LOW, *shape), buffer(LOW, *shape), buffer(LOW, 2, *shape)] + [DMA((4,))] * 3 + [DMA((2, 4))]


def plane_sum(here, part, total, scratch, ends, prepare=None):
    landed, ready, relayed, y_send, y_recv, z_send, z_recv = scratch
    z, y = here.z, here.y
    order = [
        jnp.where(z < 2, 3, 0),
        jnp.where(z == 0, 2, jnp.where(z == 1, 0, jnp.where(z == 2, 3, 1))),
        1 + z % 2,
        z,
    ]
    first = [
        remote(part.at[zz * 2 + 1 - y], landed.at[i], y_send.at[i], y_recv.at[i], here.across)
        for i, zz in enumerate(order)
    ]

    def relay(lane, zz):
        device = (here.up, here.down)[lane]
        return remote(ready.at[zz], relayed.at[lane, zz], z_send.at[zz], z_recv.at[lane, zz], device)

    for i, zz in enumerate(order):
        if prepare is not None:
            prepare(zz)
        first[i].start()
    yield
    for i, zz in enumerate(order):
        first[i].wait_recv()
        if i < 3:
            ready[zz] = (part[zz * 2 + y].astype(F32) + landed[i].astype(F32)).astype(LOW)

            @pl.when(zz > z)
            def _():
                @pl.when(z > 0)
                def _():
                    relay(0, zz).wait_recv()
                    ready[zz] = (ready[zz].astype(F32) + relayed[0, zz].astype(F32)).astype(LOW)

                relay(0, zz).start()

            @pl.when(zz < z)
            def _():
                @pl.when(z < 3)
                def _():
                    relay(1, zz).wait_recv()
                    ready[zz] = (ready[zz].astype(F32) + relayed[1, zz].astype(F32)).astype(LOW)

                relay(1, zz).start()

        else:
            total[...] = part[zz * 2 + y].astype(F32) + landed[i].astype(F32)
        yield

    @pl.when(z > 0)
    def _():
        relay(0, z).wait_recv()
        total[...] += relayed[0, z].astype(F32)

    @pl.when(z < 3)
    def _():
        relay(1, z).wait_recv()
        total[...] += relayed[1, z].astype(F32)

    def finish():
        for copy in first:
            copy.wait_send()
        for zz in order[:3]:
            relay(0, zz).wait_send()

    ends.append(finish)
    yield


def square_gather(here, held, sems, ends):
    send, recv, sib_send, sib_recv = sems
    c = here.c

    def copy(i):
        block = held.at[c, here.corner]
        return remote(block, block, send.at[i], recv.at[i], here.square[i])

    def came(i):
        block = held.at[c, here.corners[i]]
        return remote(block, block, send.at[i], recv.at[i], here.square[i])

    def pass_on(i):
        block = held.at[c, here.corners[i]]
        return remote(block, block, sib_send.at[i], sib_recv.at[i], here.sibling)

    def passed(i):
        block = held.at[1 - c, here.corners[i]]
        return remote(block, block, sib_send.at[i], sib_recv.at[i], here.sibling)

    def finish():
        for i in range(1, 4):
            copy(i).wait_send()
        for i in range(4):
            pass_on(i).wait_send()

    ends.append(finish)
    for i in (3, 1, 2):
        copy(i).start()
    pass_on(0).start()
    yield
    passed(0).wait_recv()
    yield
    for i in (1, 2, 3):
        came(i).wait_recv()
        pass_on(i).start()
        passed(i).wait_recv()
        yield


def square_sems():
    return [DMA((4,))] * 4


def square_scratch():
    shape = (4, ROWS, WIDTH)
    return [buffer(LOW, *shape)] * 3 + [DMA((4,))] * 4


def square_sum(here, part, total, scratch, ends):
    landed, ready, final, sib_send, sib_recv, send, recv = scratch
    c = here.c

    def swap(i):
        return remote(
            part.at[1 - c, here.corners[i]], landed.at[i], sib_send.at[i], sib_recv.at[i], here.sibling
        )

    def ship(i):
        return remote(ready.at[i], final.at[i], send.at[i], recv.at[i], here.square[i])

    def start(i):
        swap(i).start()

    def go(i):
        swap(i).wait_recv()
        value = part[c, here.corners[i]].astype(F32) + landed[i].astype(F32)
        if i:
            ready[i] = value.astype(LOW)
            ship(i).start()
        else:
            total[...] = value

    def end():
        for i in range(1, 4):
            ship(i).wait_recv()
        total[...] += final[1].astype(F32) + final[2].astype(F32) + final[3].astype(F32)

    def finish():
        for i in range(4):
            swap(i).wait_send()
        for i in range(1, 4):
            ship(i).wait_send()

    ends.append(finish)
    return start, go, end


def cross_scratch(rows, cols):
    return [buffer(LOW, 2, rows, cols)] + [buffer(LOW, rows, cols)] * 2 + [DMA((2,))] * 2 + [DMA((1,))] * 2


def cross_sum(here, part, total, scratch, ends):
    landed, ready, final, c_send, c_recv, x_send, x_recv = scratch
    g, x, c = here.g, here.x, here.c
    first = [
        remote(part.at[xx * 2 + 1 - c], landed.at[xx], c_send.at[xx], c_recv.at[xx], here.sibling)
        for xx in range(2)
    ]
    second = remote(ready, final, x_send.at[0], x_recv.at[0], here.beside)
    for copy in first:
        copy.start()
    yield
    for copy in first:
        copy.wait_recv()
    ready[...] = (part[(1 - x) * 2 + c].astype(F32) + landed[1 - x].astype(F32)).astype(LOW)
    second.start()
    yield
    second.wait_recv()
    value = part[g].astype(F32) + landed[x].astype(F32) + final[...].astype(F32)
    total[...] = value.astype(total.dtype).reshape(total.shape)

    def finish():
        for copy in first + [second]:
            copy.wait_send()

    ends.append(finish)
    yield


def pair_scratch(rows, cols):
    return [buffer(LOW, 2, rows, cols)] + [buffer(LOW, rows, cols)] * 2 + [DMA((1,))] * 4


def pair_sum(here, outgoing, mine, total, scratch, ends):
    landed, ready, final, x_send, x_recv, z_send, z_recv = scratch
    half = here.half
    first = remote(outgoing, landed, x_send.at[0], x_recv.at[0], here.beside)
    second = remote(ready, final, z_send.at[0], z_recv.at[0], here.far)
    first.start()
    yield
    first.wait_recv()
    ready[...] = (mine(1 - half)[...].astype(F32) + landed[1 - half].astype(F32)).astype(LOW)
    second.start()
    yield
    second.wait_recv()
    value = mine(half)[...].astype(F32) + landed[half].astype(F32) + final[...].astype(F32)
    total[...] = value.astype(LOW).reshape(total.shape)

    def finish():
        first.wait_send()
        second.wait_send()

    ends.append(finish)
    yield


def trade_sems():
    return [DMA((SHARDS,))] * 2


def plane_trade(here, mine, theirs, sems, ends):
    send, recv = sems

    def copy(k):
        device = here.at_shard(k)
        return remote(mine.at[device[1]], theirs.at[here.s], send.at[k], recv.at[k], device)

    for k in range(1, SHARDS):
        copy(k).start()
    theirs[here.s] = mine[here.s]
    yield
    for k in range(1, SHARDS):
        copy(k).wait_recv()

    def finish():
        for k in range(1, SHARDS):
            copy(k).wait_send()

    ends.append(finish)
    yield


def centre(values):
    mean = jnp.mean(values, -1, keepdims=True)
    centred = values - mean
    variance = jnp.mean(centred * centred, -1, keepdims=True)
    inverse = lax.rsqrt(variance + eps_norm)
    return centred * inverse, inverse


def centre_back(e, normed, inverse, gain):
    scaled = e * gain
    mean_one = jnp.mean(scaled, -1, keepdims=True)
    mean_two = jnp.mean(scaled * normed, -1, keepdims=True)
    return inverse * (scaled - mean_one - normed * mean_two)


def wide(norm, row):
    return jnp.concatenate([norm[j, row : row + 1, :] for j in range(SHARDS)], 1)


def column(row):
    return jnp.broadcast_to(row, (LANES, LANES)).T


def scratch_plan():
    plan = dict(
        own_norm=buffer(F32, 8, LANES),
        norm=buffer(F32, SHARDS, 8, LANES),
        norm_sems=trade_sems(),
        wq=buffer(LOW, SHARDS, 2, 64, 3 * LANES),
        wq_sems=trade_sems() + [DMA((1,))] * 2,
        wo=buffer(LOW, SHARDS, GROUPS, 32, WIDTH),
        wo_sems=gather_sems(),
        wo_more=[DMA((3,))] * 2,
        wu=buffer(LOW, SHARDS, 2, 64, HIDDEN),
        wu_sems=trade_sems() + [DMA((1,))] * 2,
        wd=buffer(LOW, 2, 2, ROWS, WIDTH),
        wd_sems=[DMA((2,))] * 2,
        a1=buffer(LOW, SHARDS, ROWS, WIDTH),
        a1_sems=gather_sems(),
        a2=buffer(LOW, 2, 4, ROWS, WIDTH),
        a2_sems=square_sems(),
        dz=buffer(LOW, 2, 4, ROWS, WIDTH),
        dz_sems=square_sems(),
        qkv=buffer(LOW, SHARDS, ROWS, 3 * LANES),
        probs=buffer(LOW, 2, SHARDS, ROWS, WIDTH),
        o_mine=buffer(LOW, SHARDS, ROWS, LANES),
        o_all=buffer(LOW, SHARDS, ROWS, LANES),
        o_sems=trade_sems(),
        n1=buffer(F32, ROWS, WIDTH),
        r1=buffer(F32, ROWS, LANES),
        h1=buffer(F32, ROWS, WIDTH),
        n2=buffer(F32, ROWS, WIDTH),
        r2=buffer(F32, ROWS, LANES),
        act=buffer(LOW, 2, 4, ROWS, HIDDEN),
        du=buffer(LOW, 2, 4, ROWS, HIDDEN),
        da2=buffer(LOW, 2, 4, ROWS, WIDTH),
        da2_sum=square_scratch(),
        e2=buffer(F32, ROWS, WIDTH),
        ffn=buffer(LOW, 2, 4, ROWS, WIDTH),
        ffn_sum=square_scratch(),
        block=buffer(F32, ROWS, WIDTH),
        dh1=buffer(F32, ROWS, WIDTH),
        do_mine=buffer(LOW, SHARDS, ROWS, LANES),
        do_all=buffer(LOW, SHARDS, ROWS, LANES),
        do_sems=trade_sems(),
        gk=buffer(F32, LANES, WIDTH),
        gv=buffer(F32, LANES, WIDTH),
        dqkv=buffer(LOW, SHARDS, ROWS, 3 * LANES),
        da1=buffer(LOW, SHARDS, ROWS, WIDTH),
        da1_sum=sum_scratch(ROWS),
        e1=buffer(F32, ROWS, WIDTH),
        gd=buffer(LOW, 2, 2, ROWS, WIDTH),
        gd_sum=pair_scratch(ROWS, WIDTH),
        gd_total=buffer(LOW, ROWS, WIDTH),
        gd_land=buffer(LOW, ROWS, WIDTH),
        gd_sems=[DMA((1,))] * 2,
        gu=buffer(LOW, 2, 2, 256, HIDDEN),
        gu_sum=pair_scratch(256, HIDDEN),
        gu_total=buffer(LOW, SHARDS, 32, HIDDEN),
        gu_land=buffer(LOW, 2, 4, 32, HIDDEN),
        gu_sems=[DMA((SHARDS,)), DMA((2, 4))],
        go=buffer(LOW, GROUPS, 256, WIDTH),
        go_sum=cross_scratch(256, WIDTH),
        go_total=buffer(LOW, SHARDS, 32, WIDTH),
        go_plane=sum_scratch(32),
        gq=buffer(LOW, GROUPS, 256, 3 * LANES),
        gq_sum=cross_scratch(256, 3 * LANES),
        gq_total=buffer(LOW, SHARDS, 32, 3 * LANES),
        gq_land=buffer(LOW, SHARDS, 32, 3 * LANES),
        gq_sems=trade_sems(),
        np_mine=buffer(F32, GROUPS, 8, 2 * LANES),
        np_land=buffer(F32, GROUPS, 8, 2 * LANES),
        np_all=buffer(F32, SHARDS, 8, 2 * LANES),
        np_sems=[DMA((GROUPS,))] * 2 + trade_sems(),
    )
    return plan


def step_kernel(*refs):
    plan = scratch_plan()
    inputs, refs = refs[:9], refs[9:]
    outputs, refs = refs[:7], list(refs[7:])
    tok, cot, item_rows, live_rows, norm_weight, wqkv, wout, wup, wdown = inputs
    block_out, input_grad, qkv_sum, up_sum, out_sum, down_sum, norm_sum = outputs
    b = {}
    for name, kind in plan.items():
        many = isinstance(kind, list)
        got = [refs.pop(0) for _ in range(len(kind) if many else 1)]
        b[name] = got if many else got[0]

    here = Place()
    g, s, x, c, z, y, half, corner = (
        here.g, here.s, here.x, here.c, here.z, here.y, here.half, here.corner
    )
    ends = []
    greet_all(here)

    norm, own_norm, wq = b["norm"], b["own_norm"], b["wq"]
    own_norm[...] = jnp.zeros_like(own_norm)
    own_norm[0:4, :] = norm_weight[...].astype(F32)
    norm[s] = own_norm[...]

    def norm_copy(k):
        send, recv = b["norm_sems"]
        return remote(own_norm, norm.at[s], send.at[k], recv.at[k], here.at_shard(k))

    def wq_copies(k):
        device = here.at_shard(k)
        send, recv = b["wq_sems"][:2]
        half_rows = pl.ds(pl.multiple_of(c * 64, 64), 64)
        return [
            remote(
                wqkv.at[half_rows, pl.ds(pl.multiple_of(j * WIDTH + device[1] * LANES, LANES), LANES)],
                wq.at[s, c, :, pl.ds(j * LANES, LANES)],
                send.at[k],
                recv.at[k],
                device,
            )
            for j in range(3)
        ]

    def wq_whole(k):
        send, recv = b["wq_sems"][:2]
        block = wq.at[here.from_shard(k), c]
        return remote(block, block, send.at[k], recv.at[k], here.at_shard(k))

    for k in range(1, SHARDS):
        norm_copy(k).start()
    for k in range(1, SHARDS):
        for copy in wq_copies(k):
            copy.start()
    n1, inverse = centre(tok[...].astype(F32))
    b["n1"][...] = n1
    b["r1"][...] = jnp.broadcast_to(inverse, (ROWS, LANES))
    for k in range(1, SHARDS):
        norm_copy(k).wait_recv()
    a1 = b["a1"]
    a1[s] = (n1 * wide(norm, 0) + wide(norm, 1)).astype(LOW)
    a1_step = plane_gather(here, lambda i: a1.at[i], b["a1_sems"], ends)
    next(a1_step)

    wd = b["wd"]
    wd_send, wd_recv = b["wd_sems"]
    wd_rows = pl.ds(pl.multiple_of(c * 256 + x * ROWS, ROWS), ROWS)
    wd_far = remote(wdown.at[wd_rows, :], wd.at[half, x], wd_send.at[0], wd_recv.at[0], here.far)
    wd_far.start()
    for j in range(2):
        wd[half, j] = wdown[pl.ds(pl.multiple_of(c * 256 + j * ROWS, ROWS), ROWS), :]
    wd_beside = remote(
        wd.at[1 - half, x], wd.at[1 - half, x], wd_send.at[1], wd_recv.at[1], here.beside
    )
    for j in range(3):
        wq[s, c, :, j * LANES : (j + 1) * LANES] = wqkv[
            pl.ds(pl.multiple_of(c * 64, 64), 64),
            pl.ds(pl.multiple_of(j * WIDTH + s * LANES, LANES), LANES),
        ]
    dz = b["dz"]
    own_live = column(live_rows[pl.ds(s, 1), :].astype(F32))
    dz[c, corner] = (cot[...].astype(F32) * jnp.concatenate([own_live] * SHARDS, 1)).astype(LOW)
    for k in range(1, SHARDS):
        wq_whole(k).wait_recv()
    wq_core = remote(
        wq.at[:, c], wq.at[:, c], b["wq_sems"][2].at[0], b["wq_sems"][3].at[0], here.sibling
    )
    wq_core.start()
    run(a1_step)

    wo = b["wo"]
    wo[s, g] = wout[pl.ds(pl.multiple_of(g * 32, 32), 32), :]
    wo_step = plane_gather(here, lambda i: wo.at[i, g], b["wo_sems"], ends)
    next(wo_step)
    wo_send, wo_recv = b["wo_more"]
    beside_g = here.beside[0]
    wo_beside = remote(wo.at[:, g], wo.at[:, g], wo_send.at[0], wo_recv.at[0], here.beside)
    wo_core = [
        remote(wo.at[:, k], wo.at[:, k], wo_send.at[1 + i], wo_recv.at[1 + i], here.sibling)
        for i, k in enumerate((g, beside_g))
    ]

    wu = b["wu"]
    wu_send, wu_recv, wu_xsend, wu_xrecv = b["wu_sems"]
    wu_rows = pl.ds(pl.multiple_of(x * 64, 64), 64)

    def wu_columns(shard, j):
        return pl.ds(pl.multiple_of((shard % 4 + j * 4) * HIDDEN + c * 256, 256), 256)

    def wu_copies(k):
        device = here.at_shard(k)
        return [
            remote(
                wup.at[wu_rows, wu_columns(device[1], j)],
                wu.at[s, x, :, pl.ds(j * 256, 256)],
                wu_send.at[k],
                wu_recv.at[k],
                device,
            )
            for j in range(2)
        ]

    def wu_whole(k):
        block = wu.at[here.from_shard(k), x]
        return remote(block, block, wu_send.at[k], wu_recv.at[k], here.at_shard(k))

    for k in range(1, SHARDS):
        for copy in wu_copies(k):
            copy.start()
    for j in range(2):
        wu[s, x, :, j * 256 : (j + 1) * 256] = wup[wu_rows, wu_columns(s, j)]
    wu_beside = remote(wu.at[:, x], wu.at[:, x], wu_xsend.at[0], wu_xrecv.at[0], here.beside)

    wq_core.wait_recv()
    qkv, probs = b["qkv"], b["probs"]
    qkv[...] = dot(flat(a1[...]), flat(wq[...])).astype(LOW).reshape(qkv.shape)
    keys = flat(qkv[:, :, LANES : 2 * LANES])
    values = flat(qkv[:, :, 2 * LANES :])
    key_items = jnp.concatenate(
        [jnp.where(live_rows[j : j + 1, :] > 0, item_rows[j : j + 1, :], -1) for j in range(SHARDS)], 1
    )
    lane = lax.broadcasted_iota(jnp.int32, (2 * ROWS, LANES), 1)
    mine = [lane < HEAD_DIM, lane >= HEAD_DIM]
    o_mine, o_all = b["o_mine"], b["o_all"]

    def o_copy(to, k):
        send, recv = b["o_sems"]
        return remote(o_mine.at[to], o_all.at[s], send.at[k], recv.at[k], (g, to))

    def attend(zz):
        pair = pl.ds(zz * 2, 2)
        queries = flat(qkv[pair, :, :LANES])
        items = jnp.concatenate([column(item_rows[pl.ds(zz * 2 + j, 1), :]) for j in range(2)], 0)
        allowed = jnp.concatenate([items] * SHARDS, 1) == key_items
        outs = []
        for h in range(2):
            scores = dot_nt(jnp.where(mine[h], queries, jnp.zeros_like(queries)), keys) * score_scale
            scores = jnp.where(allowed, scores, -1e30)
            peak = jnp.max(scores, -1, keepdims=True)
            expo = jnp.exp(scores - peak)
            chance = (expo * (1.0 / jnp.sum(expo, -1, keepdims=True))).astype(LOW)
            probs[h, pair] = chance.reshape(2, ROWS, WIDTH)
            outs.append(dot(chance, values))
        o_mine[pair] = jnp.where(mine[0], outs[0], outs[1]).astype(LOW).reshape(2, ROWS, LANES)

    for step in range(1, 4):
        zz = (z + step) % 4
        attend(zz)
        for j in range(2):
            to = zz * 2 + j
            o_copy(to, (to + SHARDS - s) % SHARDS).start()
        next(wo_step)
    attend(z)
    o_all[s] = o_mine[s]
    o_copy(here.across[1], (here.across[1] + SHARDS - s) % SHARDS).start()
    dz_step = square_gather(here, dz, b["dz_sems"], ends)
    next(dz_step)
    run(wo_step)
    wo_beside.start()
    wo_core[0].start()
    wd_far.wait_recv()
    wd_beside.start()
    for k in range(1, SHARDS):
        wu_whole(k).wait_recv()
    wu_beside.start()
    wo_beside.wait_recv()
    wo_core[1].start()
    for k in range(1, SHARDS):
        o_copy(here.from_shard(k), k).wait_recv()
    for copy in wo_core:
        copy.wait_recv()

    attended = jnp.concatenate([o_all[j] for j in range(SHARDS)], 1)
    h1 = tok[...].astype(F32) + dot(attended, wo[...].reshape(WIDTH, WIDTH))
    b["h1"][...] = h1
    n2, inverse = centre(h1)
    b["n2"][...] = n2
    b["r2"][...] = jnp.broadcast_to(inverse, (ROWS, LANES))
    a2 = b["a2"]
    a2[c, corner] = (n2 * wide(norm, 2) + wide(norm, 3)).astype(LOW)
    a2_step = square_gather(here, a2, b["a2_sems"], ends)
    next(a2_step)
    wu_beside.wait_recv()
    wd_beside.wait_recv()

    act, du, da2 = b["act"], b["du"], b["da2"]
    up = wu[...].reshape(WIDTH, HIDDEN)
    down = wd[...].reshape(HIDDEN, WIDTH)
    start, go, end = square_sum(here, da2, b["e2"], b["da2_sum"], ends)
    shape = (2, ROWS, HIDDEN)

    def feed(i):
        at = here.corners[i]
        u = dot(flat(a2[:, at]), up)
        half_erf = 0.5 + 0.5 * lax.erf(u * (0.5**0.5))
        act[:, at] = (u * half_erf).astype(LOW).reshape(shape)
        slope = half_erf + u * jnp.exp(-0.5 * u * u) * (1.0 / math.sqrt(2.0 * math.pi))
        grad = (dot_nt(flat(dz[:, at]), down) * slope).astype(LOW)
        du[:, at] = grad.reshape(shape)
        da2[:, at] = dot_nt(grad, up).astype(LOW).reshape(2, ROWS, WIDTH)

    for i in range(4):
        next(dz_step)
        next(a2_step)
        feed(i)
        start(i)
        if i > 1:
            go(i - 1)
    go(3)
    gd = b["gd"]
    gd[...] = dot_tn(flat(act[...]), flat(dz[...])).astype(LOW).reshape(gd.shape)
    gd_step = pair_sum(here, gd.at[:, 1 - x], lambda i: gd.at[i, x], b["gd_total"], b["gd_sum"], ends)
    next(gd_step)
    go(0)
    end()

    e2, n2 = b["e2"][...], b["n2"][...]
    dh1 = centre_back(e2, n2, b["r2"][:, :1], wide(norm, 2)) + dz[c, corner].astype(F32)
    b["dh1"][...] = dh1
    low = dh1.astype(LOW)
    do_mine, do_all = b["do_mine"], b["do_all"]
    for k in range(SHARDS):
        do_mine[k] = dot_nt(low, wo[k].reshape(ROWS, WIDTH)).astype(LOW)
    do_step = plane_trade(here, do_mine, do_all, b["do_sems"], ends)
    next(do_step)
    gu = b["gu"]
    gu[...] = dot_tn(flat(a2[...]), flat(du[...])).astype(LOW).reshape(gu.shape)
    gu_step = pair_sum(here, gu.at[1 - x], lambda i: gu.at[x, i], b["gu_total"], b["gu_sum"], ends)
    next(gu_step)
    go_part = b["go"]
    go_part[...] = dot_tn(attended, low).astype(LOW).reshape(go_part.shape)
    go_step = cross_sum(here, go_part, b["go_total"], b["go_sum"], ends)
    next(go_step)
    run(do_step)

    ffn = b["ffn"]
    f_start, f_go, f_end = square_sum(here, ffn, b["block"], b["ffn_sum"], ends)
    ffn[...] = dot(flat(act[...]), down).astype(LOW).reshape(ffn.shape)
    for i in range(4):
        f_start(i)
    gk, gv, dqkv = b["gk"], b["gv"], b["dqkv"]

    def back(zz, first):
        pair = pl.ds(zz * 2, 2)
        queries, outs = flat(qkv[pair, :, :LANES]), flat(do_all[pair])
        queries_t, outs_t = queries.T, outs.T
        grad_query, grad_key, grad_value = [], [], []
        for h in range(2):
            chance_low = flat(probs[h, pair])
            chance = chance_low.astype(F32)
            grad_chance = dot_nt(jnp.where(mine[h], outs, jnp.zeros_like(outs)), values)
            inner = jnp.sum(chance * grad_chance, -1, keepdims=True)
            grad_scores = (chance * (grad_chance - inner)).astype(LOW)
            lanes = slice(h * HEAD_DIM, (h + 1) * HEAD_DIM)
            grad_query.append(dot(grad_scores, keys))
            grad_key.append(dot(queries_t[lanes], grad_scores))
            grad_value.append(dot(outs_t[lanes], chance_low))
        grad_query = jnp.where(mine[0], grad_query[0], grad_query[1]) * score_scale
        dqkv[pair, :, :LANES] = grad_query.astype(LOW).reshape(2, ROWS, LANES)
        grad_key, grad_value = jnp.concatenate(grad_key, 0), jnp.concatenate(grad_value, 0)
        if first:
            gk[...], gv[...] = grad_key, grad_value
        else:
            gk[...] += grad_key
            gv[...] += grad_value

    back(0, True)
    for i in range(1, 4):
        f_go(i)
    f_go(0)
    next(go_step)
    back(1, False)
    next(gd_step)
    back(2, False)
    back(3, False)
    next(gu_step)
    thirds = (SHARDS, ROWS, LANES)
    dqkv[:, :, LANES : 2 * LANES] = (gk[...].T * score_scale).astype(LOW).reshape(thirds)
    dqkv[:, :, 2 * LANES :] = gv[...].T.astype(LOW).reshape(thirds)

    da1, weight = b["da1"], flat(wq[...])

    def spread(zz):
        pair = pl.ds(zz * 2, 2)
        da1[pair] = dot_nt(flat(dqkv[pair]), weight).astype(LOW).reshape(2, ROWS, WIDTH)

    da1_step = plane_sum(here, da1, b["e1"], b["da1_sum"], ends, spread)
    next(da1_step)
    gq = b["gq"]
    gq[...] = dot_tn(flat(a1[...]), flat(dqkv[...])).astype(LOW).reshape(gq.shape)
    gq_step = cross_sum(here, gq, b["gq_total"], b["gq_sum"], ends)
    next(gq_step)
    run(go_step)
    go_out = plane_sum(here, b["go_total"], out_sum, b["go_plane"], ends)
    next(go_out)
    next(da1_step)
    run(gd_step)
    owner = here.y * 4 + c * 2 + x
    stays = (z == g) & (owner == s)
    gd_away = remote(
        b["gd_total"], b["gd_land"], b["gd_sems"][0].at[0], b["gd_sems"][1].at[0], (z, owner)
    )

    @pl.when(jnp.logical_not(stays))
    def _():
        gd_away.start()

    next(da1_step)
    next(gq_step)
    next(go_out)
    run(gu_step)
    gu_total, gu_land = b["gu_total"], b["gu_land"]
    gu_send, gu_recv = b["gu_sems"]

    def gu_copy(k):
        to = (s + k) % SHARDS
        return remote(
            gu_total.at[to], gu_land.at[c, corner], gu_send.at[k], gu_recv.at[c, corner], (x * 2 + half, to)
        )

    def gu_came(cc, at):
        return remote(
            gu_total.at[0], gu_land.at[cc, at], gu_send.at[0], gu_recv.at[cc, at], here.sibling
        )

    @pl.when(c == half)
    def _():
        gu_land[c, corner] = gu_total[s]

    @pl.when(c != half)
    def _():
        gu_copy(0).start()

    for k in range(1, SHARDS):
        gu_copy(k).start()
    next(da1_step)
    next(go_out)
    run(gq_step)
    gq_out = plane_trade(here, b["gq_total"], b["gq_land"], b["gq_sems"], ends)
    next(gq_out)
    run(da1_step)

    e1, n1 = b["e1"][...], b["n1"][...]
    count = jnp.sum(live_rows[pl.ds(s, 1), :].astype(F32), 1, keepdims=True)
    part = jnp.concatenate(
        [
            jnp.sum(e1 * n1, 0, keepdims=True),
            jnp.sum(e1, 0, keepdims=True),
            jnp.sum(e2 * n2, 0, keepdims=True),
            jnp.sum(e2, 0, keepdims=True),
            jnp.broadcast_to(count, (4, WIDTH)),
        ],
        0,
    )
    np_mine, np_land, np_all = b["np_mine"], b["np_land"], b["np_all"]
    n_send, n_recv, m_send, m_recv = b["np_sems"]
    for k in range(GROUPS):
        np_mine[k] = part[:, k * 2 * LANES : (k + 1) * 2 * LANES]

    def grp_copy(k):
        to = (g + k) % GROUPS
        return remote(np_mine.at[to], np_land.at[k], n_send.at[k], n_recv.at[k], (to, s))

    for k in range(1, GROUPS):
        grp_copy(k).start()
    input_grad[...] = centre_back(e1, n1, b["r1"][:, :1], wide(norm, 0)) + b["dh1"][...]
    for k in range(1, GROUPS):
        grp_copy(k).wait_recv()
    np_all[s] = np_mine[g] + np_land[1] + np_land[2] + np_land[3]

    def all_copy(k):
        return remote(np_all.at[s], np_all.at[s], m_send.at[k], m_recv.at[k], here.at_shard(k))

    for k in range(1, SHARDS):
        all_copy(k).start()

    f_end()
    block_out[...] = b["h1"][...] + b["block"][...]
    run(go_out)
    for cc in range(2):
        for at in range(4):

            @pl.when(jnp.logical_not((cc == c) & (at == corner) & (c == half)))
            def _():
                gu_came(cc, at).wait_recv()

            for j in range(2):
                first = (j * 4 + at) * HIDDEN + cc * 256
                up_sum[:, first : first + 256] = gu_land[cc, at, :, j * 256 : (j + 1) * 256].astype(F32)
    run(gq_out)
    for j in range(SHARDS):
        for i in range(3):
            qkv_sum[:, i * WIDTH + j * LANES : i * WIDTH + (j + 1) * LANES] = b["gq_land"][
                j, :, i * LANES : (i + 1) * LANES
            ].astype(F32)

    @pl.when(stays)
    def _():
        down_sum[...] = b["gd_total"][...].astype(F32)

    @pl.when(jnp.logical_not(stays))
    def _():
        gd_away.wait_recv()
        down_sum[...] = b["gd_land"][...].astype(F32)
        gd_away.wait_send()

    for k in range(1, SHARDS):
        all_copy(k).wait_recv()
    total = np_all[0]
    for j in range(1, SHARDS):
        total += np_all[j]
    norm_sum[...] = pltpu.roll(total, 2 * LANES - s * 32, 1)[:, :LANES]

    for k in range(1, GROUPS):
        grp_copy(k).wait_send()
    for k in range(1, SHARDS):
        all_copy(k).wait_send()
        norm_copy(k).wait_send()
        wq_whole(k).wait_send()
        wu_whole(k).wait_send()
        o_copy(here.at_shard(k)[1], k).wait_send()
        gu_copy(k).wait_send()

    @pl.when(c != half)
    def _():
        gu_copy(0).wait_send()

    for copy in (wq_core, wd_far, wd_beside, wo_beside, wu_beside, *wo_core):
        copy.wait_send()
    for finish in ends:
        finish()


def shaped(kind, *shape):
    return jax.ShapeDtypeStruct(shape, kind)


def fast_body(
    tokens, cotangent, item_ids, live_mask, qkv_weight, out_weight, up_weight, down_weight, norm_weight,
    qkv_master, qkv_first, qkv_second, out_master, out_first, out_second, up_master, up_first, up_second,
    down_master, down_first, down_second, norm_master, norm_first, norm_second,
):
    rows = item_ids.shape[0]
    args = (
        tokens,
        cotangent,
        item_ids.reshape(SHARDS, ROWS),
        live_mask.reshape(SHARDS, ROWS),
        norm_weight,
        qkv_weight,
        out_weight,
        up_weight,
        down_weight,
    )
    scratch = []
    for kind in scratch_plan().values():
        scratch += kind if isinstance(kind, list) else [kind]
    block_out, input_grad, qkv_sum, up_sum, out_sum, down_sum, norm_sum = pl.pallas_call(
        step_kernel,
        out_shape=[
            shaped(F32, ROWS, WIDTH),
            shaped(F32, ROWS, WIDTH),
            shaped(F32, 32, 3 * WIDTH),
            shaped(F32, 32, 4 * WIDTH),
            shaped(F32, 32, WIDTH),
            shaped(F32, ROWS, WIDTH),
            shaped(F32, 8, LANES),
        ],
        in_specs=[VMEM] * len(args),
        out_specs=[VMEM] * 7,
        scratch_shapes=scratch,
        compiler_params=pltpu.CompilerParams(
            collective_id=0, has_side_effects=True, vmem_limit_bytes=62 * 2**20
        ),
    )(*args)
    norm_own = norm_sum[:, :32]
    total_count = norm_own[4, 0]
    model_width, hidden = tokens.shape[1], up_weight.shape[1]
    return (
        block_out,
        input_grad,
        *adamw(qkv_sum, total_count, qkv_master, qkv_first, qkv_second, model_width ** (-0.5), 0.1),
        *adamw(out_sum, total_count, out_master, out_first, out_second, math.sqrt(rows) / 64, 0.1),
        *adamw(up_sum, total_count, up_master, up_first, up_second, model_width ** (-0.5), 0.1),
        *adamw(down_sum, total_count, down_master, down_first, down_second, hidden ** (-0.5), 0.1),
        *adamw(norm_own[:4], total_count, norm_master, norm_first, norm_second, 0.4, 0.0),
    )


def suits(mesh):
    return mesh.shape["grp"] == GROUPS and mesh.shape["shard"] == SHARDS


def solution(mesh):
    placed = (
        P(("grp", "shard"), None),
        P(("grp", "shard"), None),
        P("grp"),
        P("grp"),
        P("shard", None),
        P("shard", None),
        P("shard", None),
        P("shard", None),
        P(None, "shard"),
        P(("grp", "shard"), None),
        P(("grp", "shard"), None),
        P(("grp", "shard"), None),
        P(("grp", "shard"), None),
        P(("grp", "shard"), None),
        P(("grp", "shard"), None),
        P(("grp", "shard"), None),
        P(("grp", "shard"), None),
        P(("grp", "shard"), None),
        P(("grp", "shard"), None),
        P(("grp", "shard"), None),
        P(("grp", "shard"), None),
        P(None, ("grp", "shard")),
        P(None, ("grp", "shard")),
        P(None, ("grp", "shard")),
    )
    return jax.shard_map(
        fast_body if suits(mesh) else body,
        mesh=mesh,
        in_specs=placed,
        out_specs=(
            P(("grp", "shard"), None),
            P(("grp", "shard"), None),
            P(("grp", "shard"), None),
            P(("grp", "shard"), None),
            P(("grp", "shard"), None),
            P(("grp", "shard"), None),
            P(("grp", "shard"), None),
            P(("grp", "shard"), None),
            P(("grp", "shard"), None),
            P(("grp", "shard"), None),
            P(("grp", "shard"), None),
            P(("grp", "shard"), None),
            P(("grp", "shard"), None),
            P(("grp", "shard"), None),
            P(("grp", "shard"), None),
            P(("grp", "shard"), None),
            P(("grp", "shard"), None),
            P(("grp", "shard"), None),
            P(("grp", "shard"), None),
            P(("grp", "shard"), None),
            P(("grp", "shard"), None),
            P(("grp", "shard"), None),
            P(None, ("grp", "shard")),
            P(None, ("grp", "shard")),
            P(None, ("grp", "shard")),
            P(None, ("grp", "shard")),
            P(None, ("grp", "shard")),
        ),
        check_vma=False,
    )
```

```python
import functools
import math

import jax
import jax.numpy as jnp
from jax import lax
from jax.experimental import pallas as pl
from jax.experimental.pallas import tpu as pltpu
from jax.sharding import PartitionSpec as P

HEADS = 16
HEAD_DIM = 64
STEP = 5


eps_norm = 1e-06
score_scale = 0.125


def exact_gelu(inputs):
    return jax.nn.gelu(inputs, approximate=False)


def outer_sum(left, right):
    return lax.dot_general(
        left, right, (((0,), (0,)), ((), ())), preferred_element_type=jnp.float32
    )


def back_dot(gradient, weight):
    return lax.dot_general(
        gradient, weight, (((1,), (1,)), ((), ())), preferred_element_type=jnp.float32
    )


def norm_forward(values, gain, shift):
    mean = jnp.mean(values, -1, keepdims=True)
    centred = values - mean
    variance = jnp.mean(centred * centred, -1, keepdims=True)
    inverse = lax.rsqrt(variance + eps_norm)
    normed = centred * inverse
    return (normed * gain + shift, normed, inverse)


def norm_backward(upstream, normed, inverse, gain):
    scaled = upstream * gain
    mean_one = jnp.mean(scaled, -1, keepdims=True)
    mean_two = jnp.mean(scaled * normed, -1, keepdims=True)
    return (
        inverse * (scaled - mean_one - normed * mean_two),
        jnp.sum(upstream * normed, 0),
        jnp.sum(upstream, 0),
    )


def block_scores(queries, query_items, key_heads, key_items, key_live):
    scores = (
        jnp.einsum("qhd,khd->qhk", queries, key_heads, preferred_element_type=jnp.float32)
        * score_scale
    )
    allowed = (query_items[:, None] == key_items[None, :]) & (key_live[None, :] > 0)
    return (scores, allowed[:, None, :])


def score_grads(
    queries, query_items, grad_out, log_total, grad_dot, key_heads, value_heads, key_items, key_live
):
    scores, allowed = block_scores(queries, query_items, key_heads, key_items, key_live)
    attention = jnp.where(allowed, jnp.exp(scores - log_total[..., None]), 0.0)
    grad_attention = jnp.einsum(
        "qhd,khd->qhk", grad_out, value_heads, preferred_element_type=jnp.float32
    )
    grad_scores = (attention * (grad_attention - grad_dot[..., None])).astype(jnp.bfloat16)
    return (grad_scores, attention.astype(jnp.bfloat16))


def key_terms(grad_scores, attention_low, queries, grad_out):
    grad_key = (
        jnp.einsum("qhk,qhd->khd", grad_scores, queries, preferred_element_type=jnp.float32)
        * score_scale
    )
    grad_value = jnp.einsum(
        "qhk,qhd->khd", attention_low, grad_out, preferred_element_type=jnp.float32
    )
    return (grad_key, grad_value)


def query_term(grad_scores, key_heads):
    return (
        jnp.einsum("qhk,khd->qhd", grad_scores, key_heads, preferred_element_type=jnp.float32)
        * score_scale
    )


def key_blocks(shard_piece, item_ids, live_mask):
    piece_rows = shard_piece.shape[0]
    block_rows = math.gcd(piece_rows, 512)
    block_count = piece_rows // block_rows
    heads = shard_piece.reshape(block_count, block_rows, 2, HEADS, HEAD_DIM)
    key_items = item_ids.reshape(block_count, block_rows)
    key_live = live_mask.reshape(block_count, block_rows)
    return (heads[:, :, 0], heads[:, :, 1], key_items, key_live, block_rows)


def attend_fold(queries, query_items, item_ids, live_mask, carried, shard_piece):
    key_heads, value_heads, key_items, key_live, block_rows = key_blocks(
        shard_piece, item_ids, live_mask
    )

    def attend_advance(running, current):
        running_max, running_sum, weighted_sum = running
        key_block, value_block, item_block, live_block = current
        scores, allowed = block_scores(queries, query_items, key_block, item_block, live_block)
        new_max = jnp.maximum(running_max, jnp.max(jnp.where(allowed, scores, -1e30), -1))
        attention = jnp.where(allowed, jnp.exp(scores - new_max[..., None]), 0.0)
        factor = jnp.exp(running_max - new_max)
        running_sum = running_sum * factor + jnp.sum(attention, -1)
        weighted_sum = weighted_sum * factor[..., None] + jnp.einsum(
            "qhk,khd->qhd",
            attention.astype(jnp.bfloat16),
            value_block,
            preferred_element_type=jnp.float32,
        )
        return ((new_max, running_sum, weighted_sum), None)

    carried, _ = lax.scan(attend_advance, carried, (key_heads, value_heads, key_items, key_live))
    return carried


def summed_fold(queries, query_items, grad_out, log_total, grad_dot, item_ids, live_mask):

    def fold_keys(carried, shard_piece, first_row):
        grad_query, grad_pairs = carried
        key_heads, value_heads, key_items, key_live, block_rows = key_blocks(
            shard_piece, item_ids, live_mask
        )

        def fold_advance(running, current):
            key_block, value_block, item_block, live_block = current
            grad_scores, attention_low = score_grads(
                queries,
                query_items,
                grad_out,
                log_total,
                grad_dot,
                key_block,
                value_block,
                item_block,
                live_block,
            )
            grad_key, grad_value = key_terms(grad_scores, attention_low, queries, grad_out)
            paired = jnp.concatenate(
                [grad_key.reshape(block_rows, -1), grad_value.reshape(block_rows, -1)], 1
            )
            return (running + query_term(grad_scores, key_block), paired)

        grad_query, pieces = lax.scan(
            fold_advance, grad_query, (key_heads, value_heads, key_items, key_live)
        )
        grad_pairs = pieces.reshape(shard_piece.shape[0], -1)
        return (grad_query, grad_pairs)

    return fold_keys


def adamw(summed, live_total, master, old_first, old_second, step_rate, shrink):
    gradient = summed / live_total
    moment = 0.5 * old_first + 0.5 * gradient
    square = 0.5 * old_second + 0.5 * gradient * gradient
    correction = 1.0 - 0.5**STEP
    updated = master - step_rate * (
        moment / correction / (jnp.sqrt(square / correction) + 1e-08) + shrink * master
    )
    return (gradient, moment, square, updated, updated.astype(jnp.bfloat16))


def body(
    tokens,
    cotangent,
    item_ids,
    live_mask,
    qkv_weight,
    out_weight,
    up_weight,
    down_weight,
    norm_weight,
    qkv_master,
    qkv_first,
    qkv_second,
    out_master,
    out_first,
    out_second,
    up_master,
    up_first,
    up_second,
    down_master,
    down_first,
    down_second,
    norm_master,
    norm_first,
    norm_second,
):
    local_rows = tokens.shape[0]
    model_width = tokens.shape[1]
    group_rows = item_ids.shape[0]
    offset = lax.axis_index("shard") * local_rows
    qkv_full, out_full, up_full, down_full, norm_full = (
        lax.all_gather(qkv_weight, "shard", axis=0, tiled=True),
        lax.all_gather(out_weight, "shard", axis=0, tiled=True),
        lax.all_gather(up_weight, "shard", axis=0, tiled=True),
        lax.all_gather(down_weight, "shard", axis=0, tiled=True),
        lax.all_gather(norm_weight, "shard", axis=1, tiled=True),
    )
    hidden = up_full.shape[1]
    norm_values = norm_full.astype(jnp.float32)
    live_rows = lax.dynamic_slice_in_dim(live_mask, offset, local_rows)
    query_items = lax.dynamic_slice_in_dim(item_ids, offset, local_rows)
    group_count = jnp.sum(live_mask).astype(jnp.float32)
    total_count = lax.psum(group_count, "grp")
    inputs = tokens.astype(jnp.float32)
    first_norm, normed_one, inverse_one = norm_forward(inputs, norm_values[0], norm_values[1])
    first_low = first_norm.astype(jnp.bfloat16)
    projected = jnp.dot(first_low, qkv_full, preferred_element_type=jnp.float32).astype(
        jnp.bfloat16
    )
    query_flat = projected[:, :model_width]
    queries = query_flat.reshape(local_rows, HEADS, HEAD_DIM)
    key_values = projected[:, model_width:]
    start_state = (
        jnp.full((local_rows, HEADS), -1e30, jnp.float32),
        jnp.zeros((local_rows, HEADS), jnp.float32),
        jnp.zeros((local_rows, HEADS, HEAD_DIM), jnp.float32),
    )
    running_max, running_sum, weighted_sum = attend_fold(
        queries,
        query_items,
        item_ids,
        live_mask,
        start_state,
        lax.all_gather(key_values, "shard", axis=0, tiled=True),
    )
    attended = weighted_sum / running_sum[..., None]
    log_total = running_max + jnp.log(running_sum)
    attended_low = attended.reshape(local_rows, model_width).astype(jnp.bfloat16)
    mixed = inputs + jnp.dot(attended_low, out_full, preferred_element_type=jnp.float32)
    second_norm, normed_two, inverse_two = norm_forward(mixed, norm_values[2], norm_values[3])
    second_low = second_norm.astype(jnp.bfloat16)
    expanded = jnp.dot(second_low, up_full, preferred_element_type=jnp.float32)
    activated, gelu_pull = jax.vjp(exact_gelu, expanded)
    activated_low = activated.astype(jnp.bfloat16)
    block_out = mixed + jnp.dot(activated_low, down_full, preferred_element_type=jnp.float32)
    upstream = cotangent.astype(jnp.float32) * live_rows.astype(jnp.float32)[:, None]
    upstream_low = upstream.astype(jnp.bfloat16)
    down_term = outer_sum(activated_low, upstream_low)
    (grad_expanded,) = gelu_pull(back_dot(upstream_low, down_full))
    expanded_low = grad_expanded.astype(jnp.bfloat16)
    up_term = outer_sum(second_low, expanded_low)
    grad_mixed, gain_two, shift_two = norm_backward(
        back_dot(expanded_low, up_full), normed_two, inverse_two, norm_values[2]
    )
    grad_mixed = grad_mixed + upstream
    mixed_low = grad_mixed.astype(jnp.bfloat16)
    out_term = outer_sum(attended_low, mixed_low)
    grad_flat = back_dot(mixed_low, out_full).astype(jnp.bfloat16)
    grad_attended = grad_flat.reshape(local_rows, HEADS, HEAD_DIM)
    grad_dot = jnp.sum(grad_attended.astype(jnp.float32) * attended, -1)
    zero_query = jnp.zeros((local_rows, HEADS, HEAD_DIM), jnp.float32)
    fold_back = summed_fold(
        queries, query_items, grad_attended, log_total, grad_dot, item_ids, live_mask
    )
    start_back = (zero_query, jnp.zeros((group_rows, 2 * model_width), jnp.float32))
    folded = fold_back(
        start_back, lax.all_gather(key_values, "shard", axis=0, tiled=True), jnp.int32(0)
    )
    grad_query, grad_pairs = folded
    grad_kv = lax.psum_scatter(
        grad_pairs.astype(jnp.bfloat16), "shard", scatter_dimension=0, tiled=True
    ).astype(jnp.float32)
    grad_projected = jnp.concatenate(
        [grad_query.reshape(local_rows, model_width), grad_kv], 1
    ).astype(jnp.bfloat16)
    qkv_term = outer_sum(first_low, grad_projected)
    grad_first, gain_one, shift_one = norm_backward(
        back_dot(grad_projected, qkv_full), normed_one, inverse_one, norm_values[0]
    )
    input_grad = grad_first + grad_mixed
    norm_term = jnp.stack([gain_one, shift_one, gain_two, shift_two])
    qkv_sum, out_sum, up_sum, down_sum, norm_sum = (
        lax.psum_scatter(qkv_term, ("grp", "shard"), scatter_dimension=0, tiled=True),
        lax.psum_scatter(out_term, ("grp", "shard"), scatter_dimension=0, tiled=True),
        lax.psum_scatter(up_term, ("grp", "shard"), scatter_dimension=0, tiled=True),
        lax.psum_scatter(down_term, ("grp", "shard"), scatter_dimension=0, tiled=True),
        lax.psum_scatter(norm_term, ("grp", "shard"), scatter_dimension=1, tiled=True),
    )
    qkv_grad, qkv_moment, qkv_square, qkv_fresh, qkv_copy = adamw(
        qkv_sum, total_count, qkv_master, qkv_first, qkv_second, model_width ** (-0.5), 0.1
    )
    out_grad, out_moment, out_square, out_fresh, out_copy = adamw(
        out_sum, total_count, out_master, out_first, out_second, math.sqrt(group_rows) / 64, 0.1
    )
    up_grad, up_moment, up_square, up_fresh, up_copy = adamw(
        up_sum, total_count, up_master, up_first, up_second, model_width ** (-0.5), 0.1
    )
    down_grad, down_moment, down_square, down_fresh, down_copy = adamw(
        down_sum, total_count, down_master, down_first, down_second, hidden ** (-0.5), 0.1
    )
    norm_grad, norm_moment, norm_square, norm_fresh, norm_copy = adamw(
        norm_sum, total_count, norm_master, norm_first, norm_second, 0.4, 0.0
    )
    return (
        block_out,
        input_grad,
        qkv_grad,
        qkv_moment,
        qkv_square,
        qkv_fresh,
        qkv_copy,
        out_grad,
        out_moment,
        out_square,
        out_fresh,
        out_copy,
        up_grad,
        up_moment,
        up_square,
        up_fresh,
        up_copy,
        down_grad,
        down_moment,
        down_square,
        down_fresh,
        down_copy,
        norm_grad,
        norm_moment,
        norm_square,
        norm_fresh,
        norm_copy,
    )


MESH = pl.DeviceIdType.MESH
F32, LOW = jnp.float32, jnp.bfloat16
VMEM = pl.BlockSpec(memory_space=pltpu.VMEM)
ANY = pl.BlockSpec(memory_space=pltpu.HBM)
SHARDS, GROUPS = 8, 4
WIDTH, ROWS, LANES = 1024, 128, 128
HIDDEN = 512
DMA = pltpu.SemaphoreType.DMA


class Place:
    def __init__(self):
        self.g, self.s = lax.axis_index("grp"), lax.axis_index("shard")
        self.z, self.y = self.s // 2, self.s % 2
        self.x, self.c = self.g // 2, self.g % 2
        self.half, self.near = self.z // 2, self.z % 2
        self.corner = self.near * 2 + self.y
        g, s = self.g, self.s
        over = 1 - 2 * self.y
        along = 2 - 4 * self.near
        self.across = (g, s + over)
        self.up = (g, s + 2)
        self.down = (g, s - 2)
        self.far = (g, (s + 4) % SHARDS)
        self.sibling = (g + 1 - 2 * self.c, s)
        self.beside = ((g + 2) % GROUPS, s)
        self.square = [(g, s), self.across, (g, s + along), (g, s + along + over)]
        self.corners = [
            self.corner,
            self.corner + over,
            (self.corner + 2) % 4,
            (self.corner + over + 2) % 4,
        ]

    def at_shard(self, k):
        return (self.g, (self.s + k) % SHARDS)

    def from_shard(self, k):
        return (self.s + SHARDS - k) % SHARDS


def remote(src, dst, send, recv, device):
    return pltpu.make_async_remote_copy(
        src_ref=src, dst_ref=dst, send_sem=send, recv_sem=recv, device_id=device, device_id_type=MESH
    )


def greet_all(here):
    barrier = pltpu.get_barrier_semaphore()
    me, everyone = here.g * SHARDS + here.s, GROUPS * SHARDS

    def greet(k, carry):
        other = (me + k) % everyone
        pl.semaphore_signal(
            barrier, inc=1, device_id=(other // SHARDS, other % SHARDS), device_id_type=MESH
        )
        return carry

    lax.fori_loop(1, everyone, greet, 0)
    pl.semaphore_wait(barrier, everyone - 1)


def flat(value):
    return value.reshape(-1, value.shape[-1])


def dot(left, right):
    return lax.dot_general(left, right, (((1,), (0,)), ((), ())), preferred_element_type=F32)


def dot_nt(left, right):
    return lax.dot_general(left, right, (((1,), (1,)), ((), ())), preferred_element_type=F32)


def dot_tn(left, right):
    return lax.dot_general(left, right, (((0,), (0,)), ((), ())), preferred_element_type=F32)


def run(*steps):
    for step in steps:
        for _ in step:
            pass


def buffer(kind, *shape):
    return pltpu.VMEM(shape, kind)


def gather_sems():
    return [DMA((3, 4)), DMA((SHARDS,))]


def plane_gather(here, block, sems, ends, came=None):
    send, recv = sems
    z, y = here.z, here.y

    def copy(lane, zz, yy):
        device = (here.across, here.up, here.down)[lane]
        i = zz * 2 + yy
        return remote(block(i), block(i), send.at[lane, zz], recv.at[i], device)

    def arrived(zz, yy):
        copy(0, zz, yy).wait_recv()
        if came is not None:
            came(zz * 2 + yy)

    def finish():
        for zz in range(4):
            copy(0, zz, y).wait_send()

            @pl.when((zz <= z) & (z < 3))
            def _():
                copy(1, zz, y).wait_send()

            @pl.when((zz >= z) & (z > 0))
            def _():
                copy(2, zz, y).wait_send()

    ends.append(finish)

    @pl.when(z < 3)
    def _():
        copy(1, z, y).start()

    @pl.when(z > 0)
    def _():
        copy(2, z, y).start()

    copy(0, z, y).start()
    if came is not None:
        came(z * 2 + y)
    yield
    for step in range(1, 4):

        @pl.when(z >= step)
        def _():
            zz = z - step
            arrived(zz, y)

            @pl.when(z < 3)
            def _():
                copy(1, zz, y).start()

            copy(0, zz, y).start()

        @pl.when(z + step <= 3)
        def _():
            zz = z + step
            arrived(zz, y)

            @pl.when(z > 0)
            def _():
                copy(2, zz, y).start()

            copy(0, zz, y).start()

        yield
    for zz in range(4):
        arrived(zz, 1 - y)
    yield


def sum_scratch(rows):
    shape = (4, rows, WIDTH)
    return [buffer(LOW, *shape), buffer(LOW, *shape), buffer(LOW, 2, *shape)] + [DMA((4,))] * 3 + [DMA((2, 4))]


def plane_sum(here, part, total, scratch, ends, prepare=None):
    landed, ready, relayed, y_send, y_recv, z_send, z_recv = scratch
    z, y = here.z, here.y
    order = [
        jnp.where(z < 2, 3, 0),
        jnp.where(z == 0, 2, jnp.where(z == 1, 0, jnp.where(z == 2, 3, 1))),
        1 + z % 2,
        z,
    ]
    first = [
        remote(part.at[zz * 2 + 1 - y], landed.at[i], y_send.at[i], y_recv.at[i], here.across)
        for i, zz in enumerate(order)
    ]

    def relay(lane, zz):
        device = (here.up, here.down)[lane]
        return remote(ready.at[zz], relayed.at[lane, zz], z_send.at[zz], z_recv.at[lane, zz], device)

    for i, zz in enumerate(order):
        if prepare is not None:
            prepare(zz)
        first[i].start()
    yield
    for i, zz in enumerate(order):
        first[i].wait_recv()
        if i < 3:
            ready[zz] = (part[zz * 2 + y].astype(F32) + landed[i].astype(F32)).astype(LOW)

            @pl.when(zz > z)
            def _():
                @pl.when(z > 0)
                def _():
                    relay(0, zz).wait_recv()
                    ready[zz] = (ready[zz].astype(F32) + relayed[0, zz].astype(F32)).astype(LOW)

                relay(0, zz).start()

            @pl.when(zz < z)
            def _():
                @pl.when(z < 3)
                def _():
                    relay(1, zz).wait_recv()
                    ready[zz] = (ready[zz].astype(F32) + relayed[1, zz].astype(F32)).astype(LOW)

                relay(1, zz).start()

        else:
            total[...] = part[zz * 2 + y].astype(F32) + landed[i].astype(F32)
        yield

    @pl.when(z > 0)
    def _():
        relay(0, z).wait_recv()
        total[...] += relayed[0, z].astype(F32)

    @pl.when(z < 3)
    def _():
        relay(1, z).wait_recv()
        total[...] += relayed[1, z].astype(F32)

    def finish():
        for copy in first:
            copy.wait_send()
        for zz in order[:3]:
            relay(0, zz).wait_send()

    ends.append(finish)
    yield


def square_gather(here, held, sems, ends):
    send, recv, half_send, half_recv, sib_send, sib_recv = sems
    c = here.c
    cut = held.shape[2] // 2

    def copy(i, at):
        block = held.at[c, here.corners[at]]
        return remote(block, block, send.at[i], recv.at[i], here.square[i])

    def onward(i, at):
        block = held.at[c, here.corners[at], pl.ds((i - 1) * cut, cut)]
        return remote(block, block, half_send.at[i - 1], half_recv.at[i - 1], here.square[3 - i])

    def pass_on(i):
        block = held.at[c, here.corners[i]]
        return remote(block, block, sib_send.at[i], sib_recv.at[i], here.sibling)

    def passed(i):
        block = held.at[1 - c, here.corners[i]]
        return remote(block, block, sib_send.at[i], sib_recv.at[i], here.sibling)

    def finish():
        for i in (1, 2):
            copy(i, 0).wait_send()
            onward(i, i).wait_send()
        for i in range(4):
            pass_on(i).wait_send()

    ends.append(finish)
    for i in (1, 2):
        copy(i, 0).start()
    pass_on(0).start()
    yield
    passed(0).wait_recv()
    yield
    for i in (1, 2):
        copy(i, i).wait_recv()
        onward(i, i).start()
        pass_on(i).start()
    yield
    passed(1).wait_recv()
    yield
    passed(2).wait_recv()
    for i in (1, 2):
        onward(i, 3).wait_recv()
    pass_on(3).start()
    yield
    passed(3).wait_recv()
    yield


def square_sems():
    return [DMA((4,))] * 2 + [DMA((2,))] * 2 + [DMA((4,))] * 2


def square_scratch():
    shape = (4, ROWS, WIDTH)
    return [buffer(LOW, *shape)] * 3 + [DMA((4,))] * 4


def square_sum(here, part, total, scratch):
    landed, ready, final, sib_send, sib_recv, send, recv = scratch
    c = here.c

    def swap(i):
        return remote(
            part(1 - c, here.corners[i]), landed.at[i], sib_send.at[i], sib_recv.at[i], here.sibling
        )

    def ship(i):
        return remote(ready.at[i], final.at[i], send.at[i], recv.at[i], here.square[i])

    def start(i):
        swap(i).start()

    def go(i):
        swap(i).wait_recv()
        value = part(c, here.corners[i])[...].astype(F32) + landed[i].astype(F32)
        if i:
            ready[i] = value.astype(LOW)
            ship(i).start()
        else:
            total[...] = value

    def end():
        for i in range(1, 4):
            ship(i).wait_recv()
        total[...] += final[1].astype(F32) + final[2].astype(F32) + final[3].astype(F32)
        for i in range(4):
            swap(i).wait_send()
        for i in range(1, 4):
            ship(i).wait_send()

    return start, go, end


def cross_scratch(rows, cols):
    return [buffer(LOW, 2, rows, cols)] + [buffer(LOW, rows, cols)] * 2 + [DMA((2,))] * 2 + [DMA((1,))] * 2


def cross_sum(here, part, total, scratch, ends):
    landed, ready, final, c_send, c_recv, x_send, x_recv = scratch
    g, x, c = here.g, here.x, here.c
    first = [
        remote(part.at[xx * 2 + 1 - c], landed.at[xx], c_send.at[xx], c_recv.at[xx], here.sibling)
        for xx in range(2)
    ]
    second = remote(ready, final, x_send.at[0], x_recv.at[0], here.beside)
    for copy in first:
        copy.start()
    yield
    for copy in first:
        copy.wait_recv()
    ready[...] = (part[(1 - x) * 2 + c].astype(F32) + landed[1 - x].astype(F32)).astype(LOW)
    second.start()
    yield
    second.wait_recv()
    value = part[g].astype(F32) + landed[x].astype(F32) + final[...].astype(F32)
    total[...] = value.astype(total.dtype).reshape(total.shape)

    def finish():
        for copy in first + [second]:
            copy.wait_send()

    ends.append(finish)
    yield


def pair_scratch(rows, cols):
    return [buffer(LOW, 2, rows, cols)] + [buffer(LOW, rows, cols)] * 2 + [DMA((1,))] * 4


def pair_sum(here, outgoing, mine, total, scratch, ends):
    landed, ready, final, x_send, x_recv, z_send, z_recv = scratch
    half = here.half
    first = remote(outgoing, landed, x_send.at[0], x_recv.at[0], here.beside)
    second = remote(ready, final, z_send.at[0], z_recv.at[0], here.far)
    first.start()
    yield
    first.wait_recv()
    ready[...] = (mine(1 - half)[...].astype(F32) + landed[1 - half].astype(F32)).astype(LOW)
    second.start()
    yield
    second.wait_recv()
    value = mine(half)[...].astype(F32) + landed[half].astype(F32) + final[...].astype(F32)
    total[...] = value.astype(LOW).reshape(total.shape)

    def finish():
        first.wait_send()
        second.wait_send()

    ends.append(finish)
    yield


def spread_scratch(rows):
    return [buffer(LOW, 4, rows, WIDTH)] * 3 + [DMA((1,))] * 2 + [DMA((4,))] * 2


def spread_sum(here, part, total, scratch, ends):
    landed, ready, final, y_send, y_recv, z_send, z_recv = scratch
    z, y = here.z, here.y
    first = remote(part.at[:, 1 - y], landed, y_send.at[0], y_recv.at[0], here.across)

    def second(k):
        to = (z + k) % 4
        return remote(ready.at[to], final.at[k], z_send.at[k], z_recv.at[k], (here.g, to * 2 + y))

    first.start()
    yield
    first.wait_recv()
    ready[...] = (part[:, y].astype(F32) + landed[...].astype(F32)).astype(LOW)
    for k in (2, 1, 3):
        second(k).start()
    yield
    value = ready[z].astype(F32)
    for k in range(1, 4):
        second(k).wait_recv()
        value += final[k].astype(F32)
    total[...] = value

    def finish():
        first.wait_send()
        for k in range(1, 4):
            second(k).wait_send()

    ends.append(finish)
    yield


def trade_sems():
    return [DMA((SHARDS,))] * 2


def plane_trade(here, mine, theirs, sems, ends):
    send, recv = sems

    def copy(k):
        device = here.at_shard(k)
        return remote(mine.at[device[1]], theirs.at[here.s], send.at[k], recv.at[k], device)

    for k in range(1, SHARDS):
        copy(k).start()
    theirs[here.s] = mine[here.s]
    yield
    for k in range(1, SHARDS):
        copy(k).wait_recv()

    def finish():
        for k in range(1, SHARDS):
            copy(k).wait_send()

    ends.append(finish)
    yield


def centre(values):
    mean = jnp.mean(values, -1, keepdims=True)
    centred = values - mean
    variance = jnp.mean(centred * centred, -1, keepdims=True)
    inverse = lax.rsqrt(variance + eps_norm)
    return centred * inverse, inverse


def centre_back(e, normed, inverse, gain):
    scaled = e * gain
    mean_one = jnp.mean(scaled, -1, keepdims=True)
    mean_two = jnp.mean(scaled * normed, -1, keepdims=True)
    return inverse * (scaled - mean_one - normed * mean_two)


def wide(norm, row):
    return jnp.concatenate([norm[j, row : row + 1, :] for j in range(SHARDS)], 1)


def column(row):
    return jnp.broadcast_to(row, (LANES, LANES)).T


def scratch_plan():
    plan = dict(
        own_norm=buffer(F32, 8, LANES),
        own_sems=DMA((SHARDS,)),
        norm=buffer(F32, SHARDS, 8, LANES),
        norm_sems=trade_sems(),
        wq=buffer(LOW, SHARDS, GROUPS, 32, 3 * LANES),
        wq_sems=trade_sems() + [DMA((3,))] * 2,
        wo=buffer(LOW, SHARDS, GROUPS, 32, WIDTH),
        wo_sems=gather_sems(),
        wo_more=[DMA((SHARDS + 2,))] * 2,
        wu=buffer(LOW, SHARDS, 2, 64, HIDDEN),
        wu_sems=trade_sems() + [DMA((1,))] * 2,
        wd=buffer(LOW, 2, 2, ROWS, WIDTH),
        wd_sems=[DMA((2,))] * 2,
        a1=buffer(LOW, SHARDS, ROWS, WIDTH),
        a1_sems=gather_sems(),
        a2=buffer(LOW, 2, 4, ROWS, WIDTH),
        a2_sems=square_sems(),
        dz=buffer(LOW, 2, 4, ROWS, WIDTH),
        dz_sems=square_sems(),
        qkv=buffer(LOW, SHARDS, ROWS, 3 * LANES),
        probs=buffer(LOW, 2, SHARDS, ROWS, WIDTH),
        o_mine=buffer(LOW, SHARDS, ROWS, LANES),
        o_all=buffer(LOW, SHARDS, ROWS, LANES),
        o_sems=trade_sems(),
        n1=buffer(F32, ROWS, WIDTH),
        r1=buffer(F32, ROWS, LANES),
        h1=buffer(F32, ROWS, WIDTH),
        n2=buffer(F32, ROWS, WIDTH),
        r2=buffer(F32, ROWS, LANES),
        act=buffer(LOW, 2, 4, ROWS, HIDDEN),
        du=buffer(LOW, 2, 4, ROWS, HIDDEN),
        dact=buffer(F32, 2, 4, ROWS, HIDDEN),
        da2=buffer(LOW, SHARDS, ROWS, WIDTH),
        da2_sum=square_scratch(),
        e2=buffer(F32, ROWS, WIDTH),
        ffn=buffer(LOW, 2, 4, ROWS, WIDTH),
        ffn_sum=square_scratch(),
        block=buffer(F32, ROWS, WIDTH),
        dh1=buffer(F32, ROWS, WIDTH),
        do_mine=buffer(LOW, SHARDS, ROWS, LANES),
        do_all=buffer(LOW, SHARDS, ROWS, LANES),
        do_sems=trade_sems(),
        gk=buffer(F32, LANES, WIDTH),
        gv=buffer(F32, LANES, WIDTH),
        dqkv=buffer(LOW, SHARDS, ROWS, 3 * LANES),
        da1_sum=sum_scratch(ROWS),
        e1=buffer(F32, ROWS, WIDTH),
        gd=buffer(LOW, 2, 2, ROWS, WIDTH),
        gd_sum=pair_scratch(ROWS, WIDTH),
        gd_total=buffer(LOW, ROWS, WIDTH),
        gd_land=buffer(LOW, ROWS, WIDTH),
        gd_sems=[DMA((1,))] * 2,
        gu=buffer(LOW, 2, 2, 256, HIDDEN),
        gu_sum=pair_scratch(256, HIDDEN),
        gu_total=buffer(LOW, SHARDS, 32, HIDDEN),
        gu_land=buffer(LOW, 2, 4, 32, HIDDEN),
        gu_sems=[DMA((SHARDS,)), DMA((2, 4))],
        go=buffer(LOW, GROUPS, 256, WIDTH),
        go_sum=cross_scratch(256, WIDTH),
        go_total=buffer(LOW, 4, 2, 32, WIDTH),
        go_plane=spread_scratch(32),
        gq=buffer(LOW, GROUPS, 256, 3 * LANES),
        gq_sum=cross_scratch(256, 3 * LANES),
        gq_total=buffer(LOW, SHARDS, 32, 3 * LANES),
        gq_land=buffer(LOW, SHARDS, 32, 3 * LANES),
        gq_sems=trade_sems(),
        np_mine=buffer(F32, GROUPS, 8, 2 * LANES),
        np_land=buffer(F32, GROUPS, 8, 2 * LANES),
        np_all=buffer(F32, SHARDS, 8, 2 * LANES),
        np_sems=[DMA((GROUPS,))] * 2 + trade_sems(),
    )
    return plan


def step_kernel(*refs):
    plan = scratch_plan()
    inputs, refs = refs[:9], refs[9:]
    outputs, refs = refs[:7], list(refs[7:])
    tok, cot, item_rows, live_rows, norm_weight, wqkv, wout, wup, wdown = inputs
    block_out, input_grad, qkv_sum, up_sum, out_sum, down_sum, norm_sum = outputs
    b = {}
    for name, kind in plan.items():
        many = isinstance(kind, list)
        got = [refs.pop(0) for _ in range(len(kind) if many else 1)]
        b[name] = got if many else got[0]

    here = Place()
    g, s, x, c, z, y, half, corner = (
        here.g, here.s, here.x, here.c, here.z, here.y, here.half, here.corner
    )
    ends = []
    quarter = pl.ds(pl.multiple_of(g * 32, 32), 32)
    beside_g = here.beside[0]
    wq, wo, wu, wd = b["wq"], b["wo"], b["wu"], b["wd"]
    wu_rows = pl.ds(pl.multiple_of(x * 64, 64), 64)

    def wu_columns(shard, j):
        return pl.ds(pl.multiple_of((shard % 4 + j * 4) * HIDDEN + c * 256, 256), 256)

    own_pairs = [
        (
            wqkv.at[quarter, pl.ds(pl.multiple_of(j * WIDTH + s * LANES, LANES), LANES)],
            wq.at[s, g, :, pl.ds(j * LANES, LANES)],
        )
        for j in range(3)
    ]
    own_pairs.append((wout.at[quarter, :], wo.at[s, g]))
    own_pairs += [(wup.at[wu_rows, wu_columns(s, j)], wu.at[s, x, :, pl.ds(j * 256, 256)]) for j in range(2)]
    own_pairs += [
        (wdown.at[pl.ds(pl.multiple_of(c * 256 + j * ROWS, ROWS), ROWS), :], wd.at[half, j]) for j in range(2)
    ]
    own_copies = [pltpu.make_async_copy(*pair, b["own_sems"].at[i]) for i, pair in enumerate(own_pairs)]
    for copy in own_copies:
        copy.start()
    greet_all(here)

    norm, own_norm = b["norm"], b["own_norm"]
    own_norm[...] = jnp.zeros_like(own_norm)
    own_norm[0:4, :] = norm_weight[...].astype(F32)
    norm[s] = own_norm[...]

    def norm_copy(k):
        send, recv = b["norm_sems"]
        return remote(own_norm, norm.at[s], send.at[k], recv.at[k], here.at_shard(k))

    def wq_copies(k):
        device = here.at_shard(k)
        send, recv = b["wq_sems"][:2]
        return [
            remote(
                wqkv.at[quarter, pl.ds(pl.multiple_of(j * WIDTH + device[1] * LANES, LANES), LANES)],
                wq.at[s, g, :, pl.ds(j * LANES, LANES)],
                send.at[k],
                recv.at[k],
                device,
            )
            for j in range(3)
        ]

    def wq_whole(k):
        send, recv = b["wq_sems"][:2]
        block = wq.at[here.from_shard(k), g]
        return remote(block, block, send.at[k], recv.at[k], here.at_shard(k))

    for k in range(1, SHARDS):
        norm_copy(k).start()
    for k in range(1, SHARDS):
        for copy in wq_copies(k):
            copy.start()
    n1, inverse = centre(tok[...].astype(F32))
    b["n1"][...] = n1
    b["r1"][...] = jnp.broadcast_to(inverse, (ROWS, LANES))
    for k in range(1, SHARDS):
        norm_copy(k).wait_recv()
    a1 = b["a1"]
    a1[s] = (n1 * wide(norm, 0) + wide(norm, 1)).astype(LOW)
    a1_step = plane_gather(here, lambda i: a1.at[i], b["a1_sems"], ends)
    next(a1_step)

    own_copies[3].wait()
    wo_send, wo_recv = b["wo_more"]

    def wo_beside(i, k):
        block = wo.at[i, k]
        return remote(block, block, wo_send.at[i], wo_recv.at[i], here.beside)

    def wo_came(i):
        wo_beside(i, g).start()

    wo_step = plane_gather(here, lambda i: wo.at[i, g], b["wo_sems"], ends, wo_came)
    next(wo_step)
    wo_core = [
        remote(wo.at[:, k], wo.at[:, k], wo_send.at[SHARDS + i], wo_recv.at[SHARDS + i], here.sibling)
        for i, k in enumerate((g, beside_g))
    ]

    wd_send, wd_recv = b["wd_sems"]
    wd_rows = pl.ds(pl.multiple_of(c * 256 + x * ROWS, ROWS), ROWS)
    wd_far = remote(wdown.at[wd_rows, :], wd.at[half, x], wd_send.at[0], wd_recv.at[0], here.far)
    wd_beside = remote(
        wd.at[1 - half, x], wd.at[1 - half, x], wd_send.at[1], wd_recv.at[1], here.beside
    )

    wu_send, wu_recv, wu_xsend, wu_xrecv = b["wu_sems"]

    def wu_copies(k):
        device = here.at_shard(k)
        return [
            remote(
                wup.at[wu_rows, wu_columns(device[1], j)],
                wu.at[s, x, :, pl.ds(j * 256, 256)],
                wu_send.at[k],
                wu_recv.at[k],
                device,
            )
            for j in range(2)
        ]

    def wu_whole(k):
        block = wu.at[here.from_shard(k), x]
        return remote(block, block, wu_send.at[k], wu_recv.at[k], here.at_shard(k))

    wu_beside = remote(wu.at[:, x], wu.at[:, x], wu_xsend.at[0], wu_xrecv.at[0], here.beside)

    dz = b["dz"]
    own_live = column(live_rows[pl.ds(s, 1), :].astype(F32))
    dz[c, corner] = (cot[...].astype(F32) * jnp.concatenate([own_live] * SHARDS, 1)).astype(LOW)
    for k in range(1, SHARDS):
        wq_whole(k).wait_recv()
    wq_send, wq_recv = b["wq_sems"][2:]
    wq_beside = remote(wq.at[:, g], wq.at[:, g], wq_send.at[0], wq_recv.at[0], here.beside)
    wq_core = [
        remote(wq.at[:, k], wq.at[:, k], wq_send.at[1 + i], wq_recv.at[1 + i], here.sibling)
        for i, k in enumerate((g, beside_g))
    ]
    for copy in own_copies[:3]:
        copy.wait()
    wq_beside.start()
    wq_core[0].start()
    next(a1_step)
    next(wo_step)
    next(a1_step)
    next(wo_step)
    wq_beside.wait_recv()
    wq_core[1].start()
    wd_far.start()
    next(a1_step)
    next(wo_step)
    for k in range(1, SHARDS):
        for copy in wu_copies(k):
            copy.start()
    for copy in own_copies[4:]:
        copy.wait()
    run(a1_step)
    dz_step = square_gather(here, dz, b["dz_sems"], ends)
    next(dz_step)

    for copy in wq_core:
        copy.wait_recv()
    qkv, probs = b["qkv"], b["probs"]
    qkv[...] = dot(flat(a1[...]), flat(wq[...])).astype(LOW).reshape(qkv.shape)
    keys = flat(qkv[:, :, LANES : 2 * LANES])
    values = flat(qkv[:, :, 2 * LANES :])
    key_items = jnp.concatenate(
        [jnp.where(live_rows[j : j + 1, :] > 0, item_rows[j : j + 1, :], -1) for j in range(SHARDS)], 1
    )
    lane = lax.broadcasted_iota(jnp.int32, (2 * ROWS, LANES), 1)
    mine = [lane < HEAD_DIM, lane >= HEAD_DIM]
    o_mine, o_all = b["o_mine"], b["o_all"]

    def o_copy(to, k):
        send, recv = b["o_sems"]
        return remote(o_mine.at[to], o_all.at[s], send.at[k], recv.at[k], (g, to))

    def attend(zz):
        pair = pl.ds(zz * 2, 2)
        queries = flat(qkv[pair, :, :LANES])
        items = jnp.concatenate([column(item_rows[pl.ds(zz * 2 + j, 1), :]) for j in range(2)], 0)
        allowed = jnp.concatenate([items] * SHARDS, 1) == key_items
        outs = []
        for h in range(2):
            scores = dot_nt(jnp.where(mine[h], queries, jnp.zeros_like(queries)), keys) * score_scale
            scores = jnp.where(allowed, scores, -1e30)
            peak = jnp.max(scores, -1, keepdims=True)
            expo = jnp.exp(scores - peak)
            chance = (expo * (1.0 / jnp.sum(expo, -1, keepdims=True))).astype(LOW)
            probs[h, pair] = chance.reshape(2, ROWS, WIDTH)
            outs.append(dot(chance, values))
        o_mine[pair] = jnp.where(mine[0], outs[0], outs[1]).astype(LOW).reshape(2, ROWS, LANES)

    for step in range(1, 4):
        zz = (z + step) % 4
        attend(zz)
        for j in range(2):
            to = zz * 2 + j
            o_copy(to, (to + SHARDS - s) % SHARDS).start()
        if step == 1:
            run(wo_step)
            wo_core[0].start()
    for i in range(SHARDS):
        wo_beside(i, beside_g).wait_recv()
    wo_core[1].start()
    attend(z)
    o_all[s] = o_mine[s]
    o_copy(here.across[1], (here.across[1] + SHARDS - s) % SHARDS).start()
    wd_far.wait_recv()
    wd_beside.start()
    for k in range(1, SHARDS):
        wu_whole(k).wait_recv()
    wu_beside.start()
    next(dz_step)
    next(dz_step)
    for k in range(1, SHARDS):
        o_copy(here.from_shard(k), k).wait_recv()
    for copy in wo_core:
        copy.wait_recv()

    attended = jnp.concatenate([o_all[j] for j in range(SHARDS)], 1)
    h1 = tok[...].astype(F32) + dot(attended, wo[...].reshape(WIDTH, WIDTH))
    b["h1"][...] = h1
    n2, inverse = centre(h1)
    b["n2"][...] = n2
    b["r2"][...] = jnp.broadcast_to(inverse, (ROWS, LANES))
    a2 = b["a2"]
    a2[c, corner] = (n2 * wide(norm, 2) + wide(norm, 3)).astype(LOW)
    a2_step = square_gather(here, a2, b["a2_sems"], ends)
    next(a2_step)
    wu_beside.wait_recv()
    wd_beside.wait_recv()

    act, du, da2, dact = b["act"], b["du"], b["da2"], b["dact"]
    up = wu[...].reshape(WIDTH, HIDDEN)
    down = wd[...].reshape(HIDDEN, WIDTH)
    start, go, end = square_sum(here, lambda cc, at: da2.at[cc * 4 + at], b["e2"], b["da2_sum"])
    shape = (2, ROWS, HIDDEN)

    def feed(i):
        at = here.corners[i]
        u = dot(flat(a2[:, at]), up)
        half_erf = 0.5 + 0.5 * lax.erf(u * (0.5**0.5))
        act[:, at] = (u * half_erf).astype(LOW).reshape(shape)
        slope = half_erf + u * jnp.exp(-0.5 * u * u) * (1.0 / math.sqrt(2.0 * math.pi))
        grad = (flat(dact[:, at]) * slope).astype(LOW)
        du[:, at] = grad.reshape(shape)
        grad = dot_nt(grad, up).astype(LOW)
        for cc in range(2):
            da2[cc * 4 + at] = grad[cc * ROWS : (cc + 1) * ROWS]

    next(a2_step)
    run(dz_step)
    dact[...] = dot_nt(flat(dz[...]), down).reshape(dact.shape)
    feed(0)
    start(0)
    next(a2_step)
    next(a2_step)
    feed(1)
    start(1)
    next(a2_step)
    feed(2)
    start(2)
    go(1)
    next(a2_step)
    feed(3)
    start(3)
    go(2)
    go(3)
    ffn = b["ffn"]
    f_start, f_go, f_end = square_sum(here, lambda cc, at: ffn.at[cc, at], b["block"], b["ffn_sum"])
    ffn[...] = dot(flat(act[...]), down).astype(LOW).reshape(ffn.shape)
    for i in range(4):
        f_start(i)
    gd = b["gd"]
    gd[...] = dot_tn(flat(act[...]), flat(dz[...])).astype(LOW).reshape(gd.shape)
    gd_step = pair_sum(here, gd.at[:, 1 - x], lambda i: gd.at[i, x], b["gd_total"], b["gd_sum"], ends)
    next(gd_step)
    gu = b["gu"]
    gu[...] = dot_tn(flat(a2[...]), flat(du[...])).astype(LOW).reshape(gu.shape)
    gu_step = pair_sum(here, gu.at[1 - x], lambda i: gu.at[x, i], b["gu_total"], b["gu_sum"], ends)
    next(gu_step)
    go(0)
    end()

    e2, n2 = b["e2"][...], b["n2"][...]
    dh1 = centre_back(e2, n2, b["r2"][:, :1], wide(norm, 2)) + dz[c, corner].astype(F32)
    b["dh1"][...] = dh1
    low = dh1.astype(LOW)
    do_mine, do_all = b["do_mine"], b["do_all"]
    for k in range(SHARDS):
        do_mine[k] = dot_nt(low, wo[k].reshape(ROWS, WIDTH)).astype(LOW)
    do_step = plane_trade(here, do_mine, do_all, b["do_sems"], ends)
    next(do_step)
    go_part = b["go"]
    go_part[...] = dot_tn(attended, low).astype(LOW).reshape(go_part.shape)
    go_step = cross_sum(here, go_part, b["go_total"], b["go_sum"], ends)
    next(go_step)
    next(go_step)
    run(do_step)
    next(gd_step)
    for i in range(1, 4):
        f_go(i)
    f_go(0)

    gk, gv, dqkv = b["gk"], b["gv"], b["dqkv"]

    def back(zz, first):
        pair = pl.ds(zz * 2, 2)
        queries, outs = flat(qkv[pair, :, :LANES]), flat(do_all[pair])
        queries_t, outs_t = queries.T, outs.T
        grad_query, grad_key, grad_value = [], [], []
        for h in range(2):
            chance_low = flat(probs[h, pair])
            chance = chance_low.astype(F32)
            grad_chance = dot_nt(jnp.where(mine[h], outs, jnp.zeros_like(outs)), values)
            inner = jnp.sum(chance * grad_chance, -1, keepdims=True)
            grad_scores = (chance * (grad_chance - inner)).astype(LOW)
            lanes = slice(h * HEAD_DIM, (h + 1) * HEAD_DIM)
            grad_query.append(dot(grad_scores, keys))
            grad_key.append(dot(queries_t[lanes], grad_scores))
            grad_value.append(dot(outs_t[lanes], chance_low))
        grad_query = jnp.where(mine[0], grad_query[0], grad_query[1]) * score_scale
        dqkv[pair, :, :LANES] = grad_query.astype(LOW).reshape(2, ROWS, LANES)
        grad_key, grad_value = jnp.concatenate(grad_key, 0), jnp.concatenate(grad_value, 0)
        if first:
            gk[...], gv[...] = grad_key, grad_value
        else:
            gk[...] += grad_key
            gv[...] += grad_value

    back(0, True)
    back(1, False)
    next(gu_step)
    back(2, False)
    back(3, False)
    thirds = (SHARDS, ROWS, LANES)
    dqkv[:, :, LANES : 2 * LANES] = (gk[...].T * score_scale).astype(LOW).reshape(thirds)
    dqkv[:, :, 2 * LANES :] = gv[...].T.astype(LOW).reshape(thirds)

    da1, weight = da2, flat(wq[...])

    def spread(zz):
        pair = pl.ds(zz * 2, 2)
        da1[pair] = dot_nt(flat(dqkv[pair]), weight).astype(LOW).reshape(2, ROWS, WIDTH)

    da1_step = plane_sum(here, da1, b["e1"], b["da1_sum"], ends, spread)
    next(da1_step)
    gq = b["gq"]
    gq[...] = dot_tn(flat(a1[...]), flat(dqkv[...])).astype(LOW).reshape(gq.shape)
    gq_step = cross_sum(here, gq, b["gq_total"], b["gq_sum"], ends)
    next(gq_step)
    run(gd_step)
    owner = here.y * 4 + c * 2 + x
    stays = (z == g) & (owner == s)
    gd_away = remote(
        b["gd_total"], b["gd_land"], b["gd_sems"][0].at[0], b["gd_sems"][1].at[0], (z, owner)
    )

    @pl.when(jnp.logical_not(stays))
    def _():
        gd_away.start()

    next(gq_step)
    next(da1_step)
    run(gu_step)
    gu_total, gu_land = b["gu_total"], b["gu_land"]
    gu_send, gu_recv = b["gu_sems"]

    def gu_copy(k):
        to = (s + k) % SHARDS
        return remote(
            gu_total.at[to], gu_land.at[c, corner], gu_send.at[k], gu_recv.at[c, corner], (x * 2 + half, to)
        )

    def gu_came(cc, at):
        return remote(
            gu_total.at[0], gu_land.at[cc, at], gu_send.at[0], gu_recv.at[cc, at], here.sibling
        )

    @pl.when(c == half)
    def _():
        gu_land[c, corner] = gu_total[s]

    @pl.when(c != half)
    def _():
        gu_copy(0).start()

    for k in range(1, SHARDS):
        gu_copy(k).start()
    run(go_step)
    go_out = spread_sum(here, b["go_total"], out_sum, b["go_plane"], ends)
    next(go_out)
    next(da1_step)
    run(gq_step)
    gq_out = plane_trade(here, b["gq_total"], b["gq_land"], b["gq_sems"], ends)
    next(gq_out)
    next(da1_step)
    next(go_out)
    next(da1_step)
    run(da1_step)

    e1, n1 = b["e1"][...], b["n1"][...]
    count = jnp.sum(live_rows[pl.ds(s, 1), :].astype(F32), 1, keepdims=True)
    part = jnp.concatenate(
        [
            jnp.sum(e1 * n1, 0, keepdims=True),
            jnp.sum(e1, 0, keepdims=True),
            jnp.sum(e2 * n2, 0, keepdims=True),
            jnp.sum(e2, 0, keepdims=True),
            jnp.broadcast_to(count, (4, WIDTH)),
        ],
        0,
    )
    np_mine, np_land, np_all = b["np_mine"], b["np_land"], b["np_all"]
    n_send, n_recv, m_send, m_recv = b["np_sems"]
    for k in range(GROUPS):
        np_mine[k] = part[:, k * 2 * LANES : (k + 1) * 2 * LANES]

    def grp_copy(k):
        to = (g + k) % GROUPS
        return remote(np_mine.at[to], np_land.at[k], n_send.at[k], n_recv.at[k], (to, s))

    for k in range(1, GROUPS):
        grp_copy(k).start()
    input_grad[...] = centre_back(e1, n1, b["r1"][:, :1], wide(norm, 0)) + b["dh1"][...]
    for k in range(1, GROUPS):
        grp_copy(k).wait_recv()
    np_all[s] = np_mine[g] + np_land[1] + np_land[2] + np_land[3]

    def all_copy(k):
        return remote(np_all.at[s], np_all.at[s], m_send.at[k], m_recv.at[k], here.at_shard(k))

    for k in range(1, SHARDS):
        all_copy(k).start()

    f_end()
    block_out[...] = b["h1"][...] + b["block"][...]
    run(go_out)
    for cc in range(2):
        for at in range(4):

            @pl.when(jnp.logical_not((cc == c) & (at == corner) & (c == half)))
            def _():
                gu_came(cc, at).wait_recv()

            for j in range(2):
                first = (j * 4 + at) * HIDDEN + cc * 256
                up_sum[:, first : first + 256] = gu_land[cc, at, :, j * 256 : (j + 1) * 256].astype(F32)
    run(gq_out)
    for j in range(SHARDS):
        for i in range(3):
            qkv_sum[:, i * WIDTH + j * LANES : i * WIDTH + (j + 1) * LANES] = b["gq_land"][
                j, :, i * LANES : (i + 1) * LANES
            ].astype(F32)

    @pl.when(stays)
    def _():
        down_sum[...] = b["gd_total"][...].astype(F32)

    @pl.when(jnp.logical_not(stays))
    def _():
        gd_away.wait_recv()
        down_sum[...] = b["gd_land"][...].astype(F32)
        gd_away.wait_send()

    for k in range(1, SHARDS):
        all_copy(k).wait_recv()
    total = np_all[0]
    for j in range(1, SHARDS):
        total += np_all[j]
    norm_sum[...] = pltpu.roll(total, 2 * LANES - s * 32, 1)[:, :LANES]

    for k in range(1, GROUPS):
        grp_copy(k).wait_send()
    for k in range(1, SHARDS):
        all_copy(k).wait_send()
        norm_copy(k).wait_send()
        wq_whole(k).wait_send()
        wu_whole(k).wait_send()
        o_copy(here.at_shard(k)[1], k).wait_send()
        gu_copy(k).wait_send()

    @pl.when(c != half)
    def _():
        gu_copy(0).wait_send()

    for copy in (wq_beside, wd_far, wd_beside, wu_beside, *wq_core, *wo_core):
        copy.wait_send()
    for i in range(SHARDS):
        wo_beside(i, g).wait_send()
    for finish in ends:
        finish()


SIZES = ((32, 3 * WIDTH), (32, WIDTH), (32, 4 * WIDTH), (ROWS, WIDTH))
KINDS = (F32, F32, F32, F32, LOW)


def adamw_kernel(rates, *refs):
    refs = list(refs)

    def take(n):
        got = refs[:n]
        del refs[:n]
        return got

    norm_sum, *norm_old = take(4)
    sums, olds, passed = take(4), [take(3) for _ in SIZES], take(2)
    norm_new = take(5)
    news, handed = [take(5) for _ in SIZES], take(2)
    held_in, held_out = [take(4) for _ in SIZES], [take(5) for _ in SIZES]
    held_pass = take(2)
    in_sem, out_sem, pass_sem = take(3)
    loads = [
        [
            pltpu.make_async_copy(src, dst, in_sem.at[i, j])
            for j, (src, dst) in enumerate(zip([sums[i], *olds[i]], held_in[i]))
        ]
        for i in range(4)
    ]
    stores = [
        [pltpu.make_async_copy(src, dst, out_sem.at[i, j]) for j, (src, dst) in enumerate(zip(held_out[i], news[i]))]
        for i in range(4)
    ]
    passes = [pltpu.make_async_copy(passed[i], held_pass[i], pass_sem.at[i]) for i in range(2)]
    hands = [pltpu.make_async_copy(held_pass[i], handed[i], pass_sem.at[2 + i]) for i in range(2)]
    order = (2, 0, 3, 1)
    for i in order:
        for copy in loads[i]:
            copy.start()
    for copy in passes:
        copy.start()
    count = norm_sum[4:5, 0:1]
    results = adamw(norm_sum[0:4, 0:32], count, *[ref[...] for ref in norm_old], rates[4], 0.0)
    for ref, value in zip(norm_new, results):
        ref[...] = value
    for i in order:
        for copy in loads[i]:
            copy.wait()
        rows, cols = SIZES[i]
        step = 16

        def some(k, carry):
            at = pl.ds(pl.multiple_of(k * step, step), step)
            for first in range(0, cols, WIDTH):
                lanes = slice(first, first + WIDTH)
                summed, *old = [ref[at, lanes] for ref in held_in[i]]
                results = adamw(summed, count, *old, rates[i], 0.1)
                for ref, value in zip(held_out[i], results):
                    ref[at, lanes] = value
            return carry

        lax.fori_loop(0, rows // step, some, 0)
        for copy in stores[i]:
            copy.start()
    for i in range(2):
        passes[i].wait()
        hands[i].start()
    for i in order:
        for copy in stores[i]:
            copy.wait()
    for copy in hands:
        copy.wait()


def shaped(kind, *shape):
    return jax.ShapeDtypeStruct(shape, kind)


def call_adamw(rates, norms, sums, olds, passed):
    return pl.pallas_call(
        functools.partial(adamw_kernel, rates),
        out_shape=[shaped(kind, *norms[1].shape) for kind in KINDS]
        + [shaped(kind, *size) for size in SIZES for kind in KINDS]
        + [shaped(F32, ROWS, WIDTH)] * 2,
        in_specs=[VMEM] * 4 + [ANY] * 18,
        out_specs=[VMEM] * 5 + [ANY] * 22,
        scratch_shapes=[buffer(F32, *size) for size in SIZES for _ in range(4)]
        + [buffer(kind, *size) for size in SIZES for kind in KINDS]
        + [buffer(F32, ROWS, WIDTH)] * 2
        + [DMA((4, 4)), DMA((4, 5)), DMA((4,))],
        compiler_params=pltpu.CompilerParams(vmem_limit_bytes=32 * 2**20),
    )(*norms, *sums, *olds, *passed)


def fast_body(
    tokens, cotangent, item_ids, live_mask, qkv_weight, out_weight, up_weight, down_weight, norm_weight,
    qkv_master, qkv_first, qkv_second, out_master, out_first, out_second, up_master, up_first, up_second,
    down_master, down_first, down_second, norm_master, norm_first, norm_second,
):
    rows = item_ids.shape[0]
    args = (
        tokens,
        cotangent,
        item_ids.reshape(SHARDS, ROWS),
        live_mask.reshape(SHARDS, ROWS),
        norm_weight,
        qkv_weight,
        out_weight,
        up_weight,
        down_weight,
    )
    scratch = []
    for kind in scratch_plan().values():
        scratch += kind if isinstance(kind, list) else [kind]
    block_out, input_grad, qkv_sum, up_sum, out_sum, down_sum, norm_sum = pl.pallas_call(
        step_kernel,
        out_shape=[
            shaped(F32, ROWS, WIDTH),
            shaped(F32, ROWS, WIDTH),
            shaped(F32, 32, 3 * WIDTH),
            shaped(F32, 32, 4 * WIDTH),
            shaped(F32, 32, WIDTH),
            shaped(F32, ROWS, WIDTH),
            shaped(F32, 8, LANES),
        ],
        in_specs=[VMEM] * 5 + [ANY] * 4,
        out_specs=[VMEM] * 7,
        scratch_shapes=scratch,
        compiler_params=pltpu.CompilerParams(
            collective_id=0, has_side_effects=True, vmem_limit_bytes=60 * 2**20
        ),
    )(*args)
    model_width, hidden = tokens.shape[1], up_weight.shape[1]
    rates = (
        model_width ** (-0.5),
        math.sqrt(rows) / 64,
        model_width ** (-0.5),
        hidden ** (-0.5),
        0.4,
    )
    news = call_adamw(
        rates,
        (norm_sum, norm_master, norm_first, norm_second),
        (qkv_sum, out_sum, up_sum, down_sum),
        (
            qkv_master, qkv_first, qkv_second, out_master, out_first, out_second,
            up_master, up_first, up_second, down_master, down_first, down_second,
        ),
        (block_out, input_grad),
    )
    return (*news[25:], *news[5:25], *news[:5])


def suits(mesh):
    return mesh.shape["grp"] == GROUPS and mesh.shape["shard"] == SHARDS


def solution(mesh):
    placed = (
        P(("grp", "shard"), None),
        P(("grp", "shard"), None),
        P("grp"),
        P("grp"),
        P("shard", None),
        P("shard", None),
        P("shard", None),
        P("shard", None),
        P(None, "shard"),
        P(("grp", "shard"), None),
        P(("grp", "shard"), None),
        P(("grp", "shard"), None),
        P(("grp", "shard"), None),
        P(("grp", "shard"), None),
        P(("grp", "shard"), None),
        P(("grp", "shard"), None),
        P(("grp", "shard"), None),
        P(("grp", "shard"), None),
        P(("grp", "shard"), None),
        P(("grp", "shard"), None),
        P(("grp", "shard"), None),
        P(None, ("grp", "shard")),
        P(None, ("grp", "shard")),
        P(None, ("grp", "shard")),
    )
    return jax.shard_map(
        fast_body if suits(mesh) else body,
        mesh=mesh,
        in_specs=placed,
        out_specs=(
            P(("grp", "shard"), None),
            P(("grp", "shard"), None),
            P(("grp", "shard"), None),
            P(("grp", "shard"), None),
            P(("grp", "shard"), None),
            P(("grp", "shard"), None),
            P(("grp", "shard"), None),
            P(("grp", "shard"), None),
            P(("grp", "shard"), None),
            P(("grp", "shard"), None),
            P(("grp", "shard"), None),
            P(("grp", "shard"), None),
            P(("grp", "shard"), None),
            P(("grp", "shard"), None),
            P(("grp", "shard"), None),
            P(("grp", "shard"), None),
            P(("grp", "shard"), None),
            P(("grp", "shard"), None),
            P(("grp", "shard"), None),
            P(("grp", "shard"), None),
            P(("grp", "shard"), None),
            P(("grp", "shard"), None),
            P(None, ("grp", "shard")),
            P(None, ("grp", "shard")),
            P(None, ("grp", "shard")),
            P(None, ("grp", "shard")),
            P(None, ("grp", "shard")),
        ),
        check_vma=False,
    )
```

```python
import functools
import math

import jax
import jax.numpy as jnp
from jax import lax
from jax.experimental import pallas as pl
from jax.experimental.pallas import tpu as pltpu
from jax.sharding import PartitionSpec as P

HEADS = 16
HEAD_DIM = 64
STEP = 5


eps_norm = 1e-06
score_scale = 0.125


def exact_gelu(inputs):
    return jax.nn.gelu(inputs, approximate=False)


def outer_sum(left, right):
    return lax.dot_general(
        left, right, (((0,), (0,)), ((), ())), preferred_element_type=jnp.float32
    )


def back_dot(gradient, weight):
    return lax.dot_general(
        gradient, weight, (((1,), (1,)), ((), ())), preferred_element_type=jnp.float32
    )


def norm_forward(values, gain, shift):
    mean = jnp.mean(values, -1, keepdims=True)
    centred = values - mean
    variance = jnp.mean(centred * centred, -1, keepdims=True)
    inverse = lax.rsqrt(variance + eps_norm)
    normed = centred * inverse
    return (normed * gain + shift, normed, inverse)


def norm_backward(upstream, normed, inverse, gain):
    scaled = upstream * gain
    mean_one = jnp.mean(scaled, -1, keepdims=True)
    mean_two = jnp.mean(scaled * normed, -1, keepdims=True)
    return (
        inverse * (scaled - mean_one - normed * mean_two),
        jnp.sum(upstream * normed, 0),
        jnp.sum(upstream, 0),
    )


def block_scores(queries, query_items, key_heads, key_items, key_live):
    scores = (
        jnp.einsum("qhd,khd->qhk", queries, key_heads, preferred_element_type=jnp.float32)
        * score_scale
    )
    allowed = (query_items[:, None] == key_items[None, :]) & (key_live[None, :] > 0)
    return (scores, allowed[:, None, :])


def score_grads(
    queries, query_items, grad_out, log_total, grad_dot, key_heads, value_heads, key_items, key_live
):
    scores, allowed = block_scores(queries, query_items, key_heads, key_items, key_live)
    attention = jnp.where(allowed, jnp.exp(scores - log_total[..., None]), 0.0)
    grad_attention = jnp.einsum(
        "qhd,khd->qhk", grad_out, value_heads, preferred_element_type=jnp.float32
    )
    grad_scores = (attention * (grad_attention - grad_dot[..., None])).astype(jnp.bfloat16)
    return (grad_scores, attention.astype(jnp.bfloat16))


def key_terms(grad_scores, attention_low, queries, grad_out):
    grad_key = (
        jnp.einsum("qhk,qhd->khd", grad_scores, queries, preferred_element_type=jnp.float32)
        * score_scale
    )
    grad_value = jnp.einsum(
        "qhk,qhd->khd", attention_low, grad_out, preferred_element_type=jnp.float32
    )
    return (grad_key, grad_value)


def query_term(grad_scores, key_heads):
    return (
        jnp.einsum("qhk,khd->qhd", grad_scores, key_heads, preferred_element_type=jnp.float32)
        * score_scale
    )


def key_blocks(shard_piece, item_ids, live_mask):
    piece_rows = shard_piece.shape[0]
    block_rows = math.gcd(piece_rows, 512)
    block_count = piece_rows // block_rows
    heads = shard_piece.reshape(block_count, block_rows, 2, HEADS, HEAD_DIM)
    key_items = item_ids.reshape(block_count, block_rows)
    key_live = live_mask.reshape(block_count, block_rows)
    return (heads[:, :, 0], heads[:, :, 1], key_items, key_live, block_rows)


def attend_fold(queries, query_items, item_ids, live_mask, carried, shard_piece):
    key_heads, value_heads, key_items, key_live, block_rows = key_blocks(
        shard_piece, item_ids, live_mask
    )

    def attend_advance(running, current):
        running_max, running_sum, weighted_sum = running
        key_block, value_block, item_block, live_block = current
        scores, allowed = block_scores(queries, query_items, key_block, item_block, live_block)
        new_max = jnp.maximum(running_max, jnp.max(jnp.where(allowed, scores, -1e30), -1))
        attention = jnp.where(allowed, jnp.exp(scores - new_max[..., None]), 0.0)
        factor = jnp.exp(running_max - new_max)
        running_sum = running_sum * factor + jnp.sum(attention, -1)
        weighted_sum = weighted_sum * factor[..., None] + jnp.einsum(
            "qhk,khd->qhd",
            attention.astype(jnp.bfloat16),
            value_block,
            preferred_element_type=jnp.float32,
        )
        return ((new_max, running_sum, weighted_sum), None)

    carried, _ = lax.scan(attend_advance, carried, (key_heads, value_heads, key_items, key_live))
    return carried


def summed_fold(queries, query_items, grad_out, log_total, grad_dot, item_ids, live_mask):

    def fold_keys(carried, shard_piece, first_row):
        grad_query, grad_pairs = carried
        key_heads, value_heads, key_items, key_live, block_rows = key_blocks(
            shard_piece, item_ids, live_mask
        )

        def fold_advance(running, current):
            key_block, value_block, item_block, live_block = current
            grad_scores, attention_low = score_grads(
                queries,
                query_items,
                grad_out,
                log_total,
                grad_dot,
                key_block,
                value_block,
                item_block,
                live_block,
            )
            grad_key, grad_value = key_terms(grad_scores, attention_low, queries, grad_out)
            paired = jnp.concatenate(
                [grad_key.reshape(block_rows, -1), grad_value.reshape(block_rows, -1)], 1
            )
            return (running + query_term(grad_scores, key_block), paired)

        grad_query, pieces = lax.scan(
            fold_advance, grad_query, (key_heads, value_heads, key_items, key_live)
        )
        grad_pairs = pieces.reshape(shard_piece.shape[0], -1)
        return (grad_query, grad_pairs)

    return fold_keys


def adamw(summed, live_total, master, old_first, old_second, step_rate, shrink):
    gradient = summed / live_total
    moment = 0.5 * old_first + 0.5 * gradient
    square = 0.5 * old_second + 0.5 * gradient * gradient
    correction = 1.0 - 0.5**STEP
    updated = master - step_rate * (
        moment / correction / (jnp.sqrt(square / correction) + 1e-08) + shrink * master
    )
    return (gradient, moment, square, updated, updated.astype(jnp.bfloat16))


def body(
    tokens,
    cotangent,
    item_ids,
    live_mask,
    qkv_weight,
    out_weight,
    up_weight,
    down_weight,
    norm_weight,
    qkv_master,
    qkv_first,
    qkv_second,
    out_master,
    out_first,
    out_second,
    up_master,
    up_first,
    up_second,
    down_master,
    down_first,
    down_second,
    norm_master,
    norm_first,
    norm_second,
):
    local_rows = tokens.shape[0]
    model_width = tokens.shape[1]
    group_rows = item_ids.shape[0]
    offset = lax.axis_index("shard") * local_rows
    qkv_full, out_full, up_full, down_full, norm_full = (
        lax.all_gather(qkv_weight, "shard", axis=0, tiled=True),
        lax.all_gather(out_weight, "shard", axis=0, tiled=True),
        lax.all_gather(up_weight, "shard", axis=0, tiled=True),
        lax.all_gather(down_weight, "shard", axis=0, tiled=True),
        lax.all_gather(norm_weight, "shard", axis=1, tiled=True),
    )
    hidden = up_full.shape[1]
    norm_values = norm_full.astype(jnp.float32)
    live_rows = lax.dynamic_slice_in_dim(live_mask, offset, local_rows)
    query_items = lax.dynamic_slice_in_dim(item_ids, offset, local_rows)
    group_count = jnp.sum(live_mask).astype(jnp.float32)
    total_count = lax.psum(group_count, "grp")
    inputs = tokens.astype(jnp.float32)
    first_norm, normed_one, inverse_one = norm_forward(inputs, norm_values[0], norm_values[1])
    first_low = first_norm.astype(jnp.bfloat16)
    projected = jnp.dot(first_low, qkv_full, preferred_element_type=jnp.float32).astype(
        jnp.bfloat16
    )
    query_flat = projected[:, :model_width]
    queries = query_flat.reshape(local_rows, HEADS, HEAD_DIM)
    key_values = projected[:, model_width:]
    start_state = (
        jnp.full((local_rows, HEADS), -1e30, jnp.float32),
        jnp.zeros((local_rows, HEADS), jnp.float32),
        jnp.zeros((local_rows, HEADS, HEAD_DIM), jnp.float32),
    )
    running_max, running_sum, weighted_sum = attend_fold(
        queries,
        query_items,
        item_ids,
        live_mask,
        start_state,
        lax.all_gather(key_values, "shard", axis=0, tiled=True),
    )
    attended = weighted_sum / running_sum[..., None]
    log_total = running_max + jnp.log(running_sum)
    attended_low = attended.reshape(local_rows, model_width).astype(jnp.bfloat16)
    mixed = inputs + jnp.dot(attended_low, out_full, preferred_element_type=jnp.float32)
    second_norm, normed_two, inverse_two = norm_forward(mixed, norm_values[2], norm_values[3])
    second_low = second_norm.astype(jnp.bfloat16)
    expanded = jnp.dot(second_low, up_full, preferred_element_type=jnp.float32)
    activated, gelu_pull = jax.vjp(exact_gelu, expanded)
    activated_low = activated.astype(jnp.bfloat16)
    block_out = mixed + jnp.dot(activated_low, down_full, preferred_element_type=jnp.float32)
    upstream = cotangent.astype(jnp.float32) * live_rows.astype(jnp.float32)[:, None]
    upstream_low = upstream.astype(jnp.bfloat16)
    down_term = outer_sum(activated_low, upstream_low)
    (grad_expanded,) = gelu_pull(back_dot(upstream_low, down_full))
    expanded_low = grad_expanded.astype(jnp.bfloat16)
    up_term = outer_sum(second_low, expanded_low)
    grad_mixed, gain_two, shift_two = norm_backward(
        back_dot(expanded_low, up_full), normed_two, inverse_two, norm_values[2]
    )
    grad_mixed = grad_mixed + upstream
    mixed_low = grad_mixed.astype(jnp.bfloat16)
    out_term = outer_sum(attended_low, mixed_low)
    grad_flat = back_dot(mixed_low, out_full).astype(jnp.bfloat16)
    grad_attended = grad_flat.reshape(local_rows, HEADS, HEAD_DIM)
    grad_dot = jnp.sum(grad_attended.astype(jnp.float32) * attended, -1)
    zero_query = jnp.zeros((local_rows, HEADS, HEAD_DIM), jnp.float32)
    fold_back = summed_fold(
        queries, query_items, grad_attended, log_total, grad_dot, item_ids, live_mask
    )
    start_back = (zero_query, jnp.zeros((group_rows, 2 * model_width), jnp.float32))
    folded = fold_back(
        start_back, lax.all_gather(key_values, "shard", axis=0, tiled=True), jnp.int32(0)
    )
    grad_query, grad_pairs = folded
    grad_kv = lax.psum_scatter(
        grad_pairs.astype(jnp.bfloat16), "shard", scatter_dimension=0, tiled=True
    ).astype(jnp.float32)
    grad_projected = jnp.concatenate(
        [grad_query.reshape(local_rows, model_width), grad_kv], 1
    ).astype(jnp.bfloat16)
    qkv_term = outer_sum(first_low, grad_projected)
    grad_first, gain_one, shift_one = norm_backward(
        back_dot(grad_projected, qkv_full), normed_one, inverse_one, norm_values[0]
    )
    input_grad = grad_first + grad_mixed
    norm_term = jnp.stack([gain_one, shift_one, gain_two, shift_two])
    qkv_sum, out_sum, up_sum, down_sum, norm_sum = (
        lax.psum_scatter(qkv_term, ("grp", "shard"), scatter_dimension=0, tiled=True),
        lax.psum_scatter(out_term, ("grp", "shard"), scatter_dimension=0, tiled=True),
        lax.psum_scatter(up_term, ("grp", "shard"), scatter_dimension=0, tiled=True),
        lax.psum_scatter(down_term, ("grp", "shard"), scatter_dimension=0, tiled=True),
        lax.psum_scatter(norm_term, ("grp", "shard"), scatter_dimension=1, tiled=True),
    )
    qkv_grad, qkv_moment, qkv_square, qkv_fresh, qkv_copy = adamw(
        qkv_sum, total_count, qkv_master, qkv_first, qkv_second, model_width ** (-0.5), 0.1
    )
    out_grad, out_moment, out_square, out_fresh, out_copy = adamw(
        out_sum, total_count, out_master, out_first, out_second, math.sqrt(group_rows) / 64, 0.1
    )
    up_grad, up_moment, up_square, up_fresh, up_copy = adamw(
        up_sum, total_count, up_master, up_first, up_second, model_width ** (-0.5), 0.1
    )
    down_grad, down_moment, down_square, down_fresh, down_copy = adamw(
        down_sum, total_count, down_master, down_first, down_second, hidden ** (-0.5), 0.1
    )
    norm_grad, norm_moment, norm_square, norm_fresh, norm_copy = adamw(
        norm_sum, total_count, norm_master, norm_first, norm_second, 0.4, 0.0
    )
    return (
        block_out,
        input_grad,
        qkv_grad,
        qkv_moment,
        qkv_square,
        qkv_fresh,
        qkv_copy,
        out_grad,
        out_moment,
        out_square,
        out_fresh,
        out_copy,
        up_grad,
        up_moment,
        up_square,
        up_fresh,
        up_copy,
        down_grad,
        down_moment,
        down_square,
        down_fresh,
        down_copy,
        norm_grad,
        norm_moment,
        norm_square,
        norm_fresh,
        norm_copy,
    )


MESH = pl.DeviceIdType.MESH
F32, LOW = jnp.float32, jnp.bfloat16
VMEM = pl.BlockSpec(memory_space=pltpu.VMEM)
ANY = pl.BlockSpec(memory_space=pltpu.HBM)
SHARDS, GROUPS = 8, 4
WIDTH, ROWS, LANES = 1024, 128, 128
HIDDEN = 512
DMA = pltpu.SemaphoreType.DMA


class Place:
    def __init__(self):
        self.g, self.s = lax.axis_index("grp"), lax.axis_index("shard")
        self.z, self.y = self.s // 2, self.s % 2
        self.x, self.c = self.g // 2, self.g % 2
        self.half, self.near = self.z // 2, self.z % 2
        self.corner = self.near * 2 + self.y
        g, s = self.g, self.s
        over = 1 - 2 * self.y
        along = 2 - 4 * self.near
        self.across = (g, s + over)
        self.up = (g, s + 2)
        self.down = (g, s - 2)
        self.far = (g, (s + 4) % SHARDS)
        self.sibling = (g + 1 - 2 * self.c, s)
        self.beside = ((g + 2) % GROUPS, s)
        self.square = [(g, s), self.across, (g, s + along), (g, s + along + over)]
        self.corners = [
            self.corner,
            self.corner + over,
            (self.corner + 2) % 4,
            (self.corner + over + 2) % 4,
        ]

    def at_shard(self, k):
        return (self.g, (self.s + k) % SHARDS)

    def from_shard(self, k):
        return (self.s + SHARDS - k) % SHARDS


def remote(src, dst, send, recv, device):
    return pltpu.make_async_remote_copy(
        src_ref=src, dst_ref=dst, send_sem=send, recv_sem=recv, device_id=device, device_id_type=MESH
    )


def greet_all(here):
    barrier = pltpu.get_barrier_semaphore()
    me, everyone = here.g * SHARDS + here.s, GROUPS * SHARDS

    def greet(k, carry):
        other = (me + k) % everyone
        pl.semaphore_signal(
            barrier, inc=1, device_id=(other // SHARDS, other % SHARDS), device_id_type=MESH
        )
        return carry

    lax.fori_loop(1, everyone, greet, 0)
    pl.semaphore_wait(barrier, everyone - 1)


def flat(value):
    return value.reshape(-1, value.shape[-1])


def dot(left, right):
    return lax.dot_general(left, right, (((1,), (0,)), ((), ())), preferred_element_type=F32)


def dot_nt(left, right):
    return lax.dot_general(left, right, (((1,), (1,)), ((), ())), preferred_element_type=F32)


def dot_tn(left, right):
    return lax.dot_general(left, right, (((0,), (0,)), ((), ())), preferred_element_type=F32)


def run(*steps):
    for step in steps:
        for _ in step:
            pass


def buffer(kind, *shape):
    return pltpu.VMEM(shape, kind)


def gather_sems():
    return [DMA((3, 4)), DMA((SHARDS,))]


def plane_gather(here, block, sems, ends, came=None):
    send, recv = sems
    z, y = here.z, here.y

    def copy(lane, zz, yy):
        device = (here.across, here.up, here.down)[lane]
        i = zz * 2 + yy
        return remote(block(i), block(i), send.at[lane, zz], recv.at[i], device)

    def arrived(zz, yy):
        copy(0, zz, yy).wait_recv()
        if came is not None:
            came(zz * 2 + yy)

    def finish():
        for zz in range(4):
            copy(0, zz, y).wait_send()

            @pl.when((zz <= z) & (z < 3))
            def _():
                copy(1, zz, y).wait_send()

            @pl.when((zz >= z) & (z > 0))
            def _():
                copy(2, zz, y).wait_send()

    ends.append(finish)

    @pl.when(z < 3)
    def _():
        copy(1, z, y).start()

    @pl.when(z > 0)
    def _():
        copy(2, z, y).start()

    copy(0, z, y).start()
    if came is not None:
        came(z * 2 + y)
    yield
    for step in range(1, 4):

        @pl.when(z >= step)
        def _():
            zz = z - step
            arrived(zz, y)

            @pl.when(z < 3)
            def _():
                copy(1, zz, y).start()

            copy(0, zz, y).start()

        @pl.when(z + step <= 3)
        def _():
            zz = z + step
            arrived(zz, y)

            @pl.when(z > 0)
            def _():
                copy(2, zz, y).start()

            copy(0, zz, y).start()

        yield
    for zz in range(4):
        arrived(zz, 1 - y)
    yield


def sum_scratch(rows):
    shape = (4, rows, WIDTH)
    return [buffer(LOW, *shape), buffer(LOW, *shape), buffer(LOW, 2, *shape)] + [DMA((4,))] * 3 + [DMA((2, 4))]


def plane_sum(here, part, total, scratch, ends, prepare=None):
    landed, ready, relayed, y_send, y_recv, z_send, z_recv = scratch
    z, y = here.z, here.y
    order = [
        jnp.where(z < 2, 3, 0),
        jnp.where(z == 0, 2, jnp.where(z == 1, 0, jnp.where(z == 2, 3, 1))),
        1 + z % 2,
        z,
    ]
    first = [
        remote(part.at[zz * 2 + 1 - y], landed.at[i], y_send.at[i], y_recv.at[i], here.across)
        for i, zz in enumerate(order)
    ]

    def relay(lane, zz):
        device = (here.up, here.down)[lane]
        return remote(ready.at[zz], relayed.at[lane, zz], z_send.at[zz], z_recv.at[lane, zz], device)

    for i, zz in enumerate(order):
        if prepare is not None:
            prepare(zz)
        first[i].start()
    yield
    for i, zz in enumerate(order):
        first[i].wait_recv()
        if i < 3:
            ready[zz] = (part[zz * 2 + y].astype(F32) + landed[i].astype(F32)).astype(LOW)

            @pl.when(zz > z)
            def _():
                @pl.when(z > 0)
                def _():
                    relay(0, zz).wait_recv()
                    ready[zz] = (ready[zz].astype(F32) + relayed[0, zz].astype(F32)).astype(LOW)

                relay(0, zz).start()

            @pl.when(zz < z)
            def _():
                @pl.when(z < 3)
                def _():
                    relay(1, zz).wait_recv()
                    ready[zz] = (ready[zz].astype(F32) + relayed[1, zz].astype(F32)).astype(LOW)

                relay(1, zz).start()

        else:
            total[...] = part[zz * 2 + y].astype(F32) + landed[i].astype(F32)
        yield

    @pl.when(z > 0)
    def _():
        relay(0, z).wait_recv()
        total[...] += relayed[0, z].astype(F32)

    @pl.when(z < 3)
    def _():
        relay(1, z).wait_recv()
        total[...] += relayed[1, z].astype(F32)

    def finish():
        for copy in first:
            copy.wait_send()
        for zz in order[:3]:
            relay(0, zz).wait_send()

    ends.append(finish)
    yield


def square_gather(here, held, sems, ends):
    send, recv, half_send, half_recv, sib_send, sib_recv = sems
    c = here.c
    cut = held.shape[2] // 2

    def copy(i, at):
        block = held.at[c, here.corners[at]]
        return remote(block, block, send.at[i], recv.at[i], here.square[i])

    def onward(i, at):
        block = held.at[c, here.corners[at], pl.ds((i - 1) * cut, cut)]
        return remote(block, block, half_send.at[i - 1], half_recv.at[i - 1], here.square[3 - i])

    def pass_on(i):
        block = held.at[c, here.corners[i]]
        return remote(block, block, sib_send.at[i], sib_recv.at[i], here.sibling)

    def passed(i):
        block = held.at[1 - c, here.corners[i]]
        return remote(block, block, sib_send.at[i], sib_recv.at[i], here.sibling)

    def finish():
        for i in (1, 2):
            copy(i, 0).wait_send()
            onward(i, i).wait_send()
        for i in range(4):
            pass_on(i).wait_send()

    ends.append(finish)

    def start():
        for i in (1, 2):
            copy(i, 0).start()
        pass_on(0).start()

    def relay():
        for i in (1, 2):
            copy(i, i).wait_recv()
            onward(i, i).start()
            pass_on(i).start()

    def last():
        for i in (1, 2):
            onward(i, 3).wait_recv()
        pass_on(3).start()

    def got(i):
        passed(i).wait_recv()

    return start, relay, last, got


def square_sems():
    return [DMA((4,))] * 2 + [DMA((2,))] * 2 + [DMA((4,))] * 2


def square_scratch():
    shape = (4, ROWS, WIDTH)
    return [buffer(LOW, *shape)] * 3 + [DMA((4,))] * 4


def square_sum(here, part, total, scratch):
    landed, ready, final, sib_send, sib_recv, send, recv = scratch
    c = here.c

    def swap(i):
        return remote(
            part(1 - c, here.corners[i]), landed.at[i], sib_send.at[i], sib_recv.at[i], here.sibling
        )

    def ship(i):
        return remote(ready.at[i], final.at[i], send.at[i], recv.at[i], here.square[i])

    def start(i):
        swap(i).start()

    def go(i):
        swap(i).wait_recv()
        value = part(c, here.corners[i])[...].astype(F32) + landed[i].astype(F32)
        if i:
            ready[i] = value.astype(LOW)
            ship(i).start()
        else:
            total[...] = value

    def end():
        for i in range(1, 4):
            ship(i).wait_recv()
        total[...] += final[1].astype(F32) + final[2].astype(F32) + final[3].astype(F32)
        for i in range(4):
            swap(i).wait_send()
        for i in range(1, 4):
            ship(i).wait_send()

    return start, go, end


def cross_scratch(rows, cols):
    return [buffer(LOW, 2, rows, cols)] + [buffer(LOW, rows, cols)] * 2 + [DMA((2,))] * 2 + [DMA((1,))] * 2


def cross_sum(here, part, total, scratch, ends):
    landed, ready, final, c_send, c_recv, x_send, x_recv = scratch
    g, x, c = here.g, here.x, here.c
    first = [
        remote(part.at[xx * 2 + 1 - c], landed.at[xx], c_send.at[xx], c_recv.at[xx], here.sibling)
        for xx in range(2)
    ]
    second = remote(ready, final, x_send.at[0], x_recv.at[0], here.beside)
    for copy in first:
        copy.start()
    yield
    for copy in first:
        copy.wait_recv()
    ready[...] = (part[(1 - x) * 2 + c].astype(F32) + landed[1 - x].astype(F32)).astype(LOW)
    second.start()
    yield
    second.wait_recv()
    value = part[g].astype(F32) + landed[x].astype(F32) + final[...].astype(F32)
    total[...] = value.astype(total.dtype).reshape(total.shape)

    def finish():
        for copy in first + [second]:
            copy.wait_send()

    ends.append(finish)
    yield


def pair_scratch(rows, cols, parts=1):
    return [buffer(LOW, parts, 2, rows, cols)] + [buffer(LOW, parts, rows, cols)] * 2 + [DMA((1,))] * 4


def pair_sum(here, part, total, scratch, ends):
    landed, ready, final, x_send, x_recv, z_send, z_recv = scratch
    x, half = here.x, here.half
    first = remote(part.at[1 - x], landed, x_send.at[0], x_recv.at[0], here.beside)
    second = remote(ready, final, z_send.at[0], z_recv.at[0], here.far)
    first.start()
    yield
    first.wait_recv()
    ready[...] = (part[x, :, 1 - half].astype(F32) + landed[:, 1 - half].astype(F32)).astype(LOW)
    second.start()
    yield
    second.wait_recv()
    value = part[x, :, half].astype(F32) + landed[:, half].astype(F32) + final[...].astype(F32)
    total[...] = value.astype(LOW).reshape(total.shape)

    def finish():
        first.wait_send()
        second.wait_send()

    ends.append(finish)
    yield


def spread_scratch(rows):
    return [buffer(LOW, 4, rows, WIDTH)] * 3 + [DMA((1,))] * 2 + [DMA((4,))] * 2


def spread_sum(here, part, total, scratch, ends):
    landed, ready, final, y_send, y_recv, z_send, z_recv = scratch
    z, y = here.z, here.y
    first = remote(part.at[:, 1 - y], landed, y_send.at[0], y_recv.at[0], here.across)

    def second(k):
        to = (z + k) % 4
        return remote(ready.at[to], final.at[k], z_send.at[k], z_recv.at[k], (here.g, to * 2 + y))

    first.start()
    yield
    first.wait_recv()
    ready[...] = (part[:, y].astype(F32) + landed[...].astype(F32)).astype(LOW)
    for k in (2, 1, 3):
        second(k).start()
    yield
    value = ready[z].astype(F32)
    for k in range(1, 4):
        second(k).wait_recv()
        value += final[k].astype(F32)
    total[...] = value

    def finish():
        first.wait_send()
        for k in range(1, 4):
            second(k).wait_send()

    ends.append(finish)
    yield


def trade_sems():
    return [DMA((SHARDS,))] * 2


def plane_trade(here, mine, theirs, sems, ends):
    send, recv = sems

    def copy(k):
        device = here.at_shard(k)
        return remote(mine.at[device[1]], theirs.at[here.s], send.at[k], recv.at[k], device)

    for k in range(1, SHARDS):
        copy(k).start()
    theirs[here.s] = mine[here.s]
    yield
    for k in range(1, SHARDS):
        copy(k).wait_recv()

    def finish():
        for k in range(1, SHARDS):
            copy(k).wait_send()

    ends.append(finish)
    yield


def centre(values):
    mean = jnp.mean(values, -1, keepdims=True)
    centred = values - mean
    variance = jnp.mean(centred * centred, -1, keepdims=True)
    inverse = lax.rsqrt(variance + eps_norm)
    return centred * inverse, inverse


def centre_back(e, normed, inverse, gain):
    scaled = e * gain
    mean_one = jnp.mean(scaled, -1, keepdims=True)
    mean_two = jnp.mean(scaled * normed, -1, keepdims=True)
    return inverse * (scaled - mean_one - normed * mean_two)


def wide(norm, row):
    return jnp.concatenate([norm[j, row : row + 1, :] for j in range(SHARDS)], 1)


def column(row):
    return jnp.broadcast_to(row, (LANES, LANES)).T


def scratch_plan():
    plan = dict(
        own_norm=buffer(F32, 8, LANES),
        own_sems=DMA((SHARDS,)),
        norm=buffer(F32, SHARDS, 8, LANES),
        norm_sems=trade_sems(),
        wq=buffer(LOW, SHARDS, GROUPS, 32, 3 * LANES),
        wq_sems=trade_sems() + [DMA((3,))] * 2,
        wo=buffer(LOW, SHARDS, GROUPS, 32, WIDTH),
        wo_sems=gather_sems(),
        wo_more=[DMA((SHARDS + 2,))] * 2,
        wu=buffer(LOW, SHARDS, 2, 64, HIDDEN),
        wu_sems=trade_sems() + [DMA((1,))] * 2,
        wd=buffer(LOW, 2, 2, ROWS, WIDTH),
        wd_sems=[DMA((2,))] * 2,
        a1=buffer(LOW, SHARDS, ROWS, WIDTH),
        a1_sems=gather_sems(),
        a2=buffer(LOW, 2, 4, ROWS, WIDTH),
        a2_sems=square_sems(),
        dz=buffer(LOW, 2, 4, ROWS, WIDTH),
        dz_sems=square_sems(),
        qkv=buffer(LOW, SHARDS, ROWS, 3 * LANES),
        probs=buffer(LOW, 2, SHARDS, ROWS, WIDTH),
        o_mine=buffer(LOW, SHARDS, ROWS, LANES),
        o_all=buffer(LOW, SHARDS, ROWS, LANES),
        o_sems=trade_sems(),
        n1=buffer(F32, ROWS, WIDTH),
        r1=buffer(F32, ROWS, LANES),
        h1=buffer(F32, ROWS, WIDTH),
        n2=buffer(F32, ROWS, WIDTH),
        r2=buffer(F32, ROWS, LANES),
        act=buffer(LOW, 2, 4, ROWS, HIDDEN),
        du=buffer(LOW, 2, 4, ROWS, HIDDEN),
        dact=buffer(F32, 2, 4, ROWS, HIDDEN),
        da2=buffer(LOW, SHARDS, ROWS, WIDTH),
        da2_sum=square_scratch(),
        e2=buffer(F32, ROWS, WIDTH),
        ffn=buffer(LOW, 2, 4, ROWS, WIDTH),
        ffn_sum=square_scratch(),
        block=buffer(F32, ROWS, WIDTH),
        dh1=buffer(F32, ROWS, WIDTH),
        do_mine=buffer(LOW, SHARDS, ROWS, LANES),
        do_all=buffer(LOW, SHARDS, ROWS, LANES),
        do_sems=trade_sems(),
        gk=buffer(F32, LANES, WIDTH),
        gv=buffer(F32, LANES, WIDTH),
        dqkv=buffer(LOW, SHARDS, ROWS, 3 * LANES),
        da1_sum=sum_scratch(ROWS),
        e1=buffer(F32, ROWS, WIDTH),
        gd=buffer(LOW, 2, 1, 2, ROWS, WIDTH),
        gd_sum=pair_scratch(ROWS, WIDTH),
        gd_total=buffer(LOW, ROWS, WIDTH),
        gd_land=buffer(LOW, ROWS, WIDTH),
        gd_sems=[DMA((1,))] * 2,
        gu=buffer(LOW, 2, 2, 2, ROWS, HIDDEN),
        gu_sum=pair_scratch(ROWS, HIDDEN, 2),
        gu_total=buffer(LOW, 2, 4, 32, HIDDEN),
        gu_land=buffer(LOW, 2, 4, 32, HIDDEN),
        gu_sems=[DMA((2, 4)), DMA((2, 4))],
        go=buffer(LOW, GROUPS, 256, WIDTH),
        go_sum=cross_scratch(256, WIDTH),
        go_total=buffer(LOW, 4, 2, 32, WIDTH),
        go_plane=spread_scratch(32),
        gq=buffer(LOW, GROUPS, 256, 3 * LANES),
        gq_sum=cross_scratch(256, 3 * LANES),
        gq_total=buffer(LOW, SHARDS, 32, 3 * LANES),
        gq_land=buffer(LOW, SHARDS, 32, 3 * LANES),
        gq_sems=trade_sems(),
        np_mine=buffer(F32, GROUPS, 8, 2 * LANES),
        np_land=buffer(F32, GROUPS, 8, 2 * LANES),
        np_all=buffer(F32, SHARDS, 8, 2 * LANES),
        np_sems=[DMA((GROUPS,))] * 2 + trade_sems(),
    )
    return plan


def step_kernel(*refs):
    plan = scratch_plan()
    inputs, refs = refs[:9], refs[9:]
    outputs, refs = refs[:7], list(refs[7:])
    tok, cot, item_rows, live_rows, norm_weight, wqkv, wout, wup, wdown = inputs
    block_out, input_grad, qkv_sum, up_sum, out_sum, down_sum, norm_sum = outputs
    b = {}
    for name, kind in plan.items():
        many = isinstance(kind, list)
        got = [refs.pop(0) for _ in range(len(kind) if many else 1)]
        b[name] = got if many else got[0]

    here = Place()
    g, s, x, c, z, y, half, corner = (
        here.g, here.s, here.x, here.c, here.z, here.y, here.half, here.corner
    )
    ends = []
    quarter = pl.ds(pl.multiple_of(g * 32, 32), 32)
    beside_g = here.beside[0]
    wq, wo, wu, wd = b["wq"], b["wo"], b["wu"], b["wd"]
    wu_rows = pl.ds(pl.multiple_of(x * 64, 64), 64)

    def wu_columns(shard, j):
        return pl.ds(pl.multiple_of((shard % 4 + j * 4) * HIDDEN + c * 256, 256), 256)

    own_pairs = [
        (
            wqkv.at[quarter, pl.ds(pl.multiple_of(j * WIDTH + s * LANES, LANES), LANES)],
            wq.at[s, g, :, pl.ds(j * LANES, LANES)],
        )
        for j in range(3)
    ]
    own_pairs.append((wout.at[quarter, :], wo.at[s, g]))
    own_pairs += [(wup.at[wu_rows, wu_columns(s, j)], wu.at[s, x, :, pl.ds(j * 256, 256)]) for j in range(2)]
    own_pairs += [
        (wdown.at[pl.ds(pl.multiple_of(c * 256 + j * ROWS, ROWS), ROWS), :], wd.at[half, j]) for j in range(2)
    ]
    own_copies = [pltpu.make_async_copy(*pair, b["own_sems"].at[i]) for i, pair in enumerate(own_pairs)]
    for copy in own_copies:
        copy.start()
    greet_all(here)

    norm, own_norm = b["norm"], b["own_norm"]
    own_norm[...] = jnp.zeros_like(own_norm)
    own_norm[0:4, :] = norm_weight[...].astype(F32)
    norm[s] = own_norm[...]

    def norm_copy(k):
        send, recv = b["norm_sems"]
        return remote(own_norm, norm.at[s], send.at[k], recv.at[k], here.at_shard(k))

    def wq_copies(k):
        device = here.at_shard(k)
        send, recv = b["wq_sems"][:2]
        return [
            remote(
                wqkv.at[quarter, pl.ds(pl.multiple_of(j * WIDTH + device[1] * LANES, LANES), LANES)],
                wq.at[s, g, :, pl.ds(j * LANES, LANES)],
                send.at[k],
                recv.at[k],
                device,
            )
            for j in range(3)
        ]

    def wq_whole(k):
        send, recv = b["wq_sems"][:2]
        block = wq.at[here.from_shard(k), g]
        return remote(block, block, send.at[k], recv.at[k], here.at_shard(k))

    for k in range(1, SHARDS):
        norm_copy(k).start()
    for k in range(1, SHARDS):
        for copy in wq_copies(k):
            copy.start()
    n1, inverse = centre(tok[...].astype(F32))
    b["n1"][...] = n1
    b["r1"][...] = jnp.broadcast_to(inverse, (ROWS, LANES))
    for k in range(1, SHARDS):
        norm_copy(k).wait_recv()
    a1 = b["a1"]
    a1[s] = (n1 * wide(norm, 0) + wide(norm, 1)).astype(LOW)
    a1_step = plane_gather(here, lambda i: a1.at[i], b["a1_sems"], ends)
    next(a1_step)

    own_copies[3].wait()
    wo_send, wo_recv = b["wo_more"]

    def wo_beside(i, k):
        block = wo.at[i, k]
        return remote(block, block, wo_send.at[i], wo_recv.at[i], here.beside)

    def wo_came(i):
        wo_beside(i, g).start()

    wo_step = plane_gather(here, lambda i: wo.at[i, g], b["wo_sems"], ends, wo_came)
    next(wo_step)
    wo_core = [
        remote(wo.at[:, k], wo.at[:, k], wo_send.at[SHARDS + i], wo_recv.at[SHARDS + i], here.sibling)
        for i, k in enumerate((g, beside_g))
    ]

    wd_send, wd_recv = b["wd_sems"]
    wd_rows = pl.ds(pl.multiple_of(c * 256 + x * ROWS, ROWS), ROWS)
    wd_far = remote(wdown.at[wd_rows, :], wd.at[half, x], wd_send.at[0], wd_recv.at[0], here.far)
    wd_beside = remote(
        wd.at[1 - half, x], wd.at[1 - half, x], wd_send.at[1], wd_recv.at[1], here.beside
    )

    wu_send, wu_recv, wu_xsend, wu_xrecv = b["wu_sems"]

    def wu_copies(k):
        device = here.at_shard(k)
        return [
            remote(
                wup.at[wu_rows, wu_columns(device[1], j)],
                wu.at[s, x, :, pl.ds(j * 256, 256)],
                wu_send.at[k],
                wu_recv.at[k],
                device,
            )
            for j in range(2)
        ]

    def wu_whole(k):
        block = wu.at[here.from_shard(k), x]
        return remote(block, block, wu_send.at[k], wu_recv.at[k], here.at_shard(k))

    wu_beside = remote(wu.at[:, x], wu.at[:, x], wu_xsend.at[0], wu_xrecv.at[0], here.beside)

    dz = b["dz"]
    own_live = column(live_rows[pl.ds(s, 1), :].astype(F32))
    dz[c, corner] = (cot[...].astype(F32) * jnp.concatenate([own_live] * SHARDS, 1)).astype(LOW)
    for k in range(1, SHARDS):
        wq_whole(k).wait_recv()
    wq_send, wq_recv = b["wq_sems"][2:]
    wq_beside = remote(wq.at[:, g], wq.at[:, g], wq_send.at[0], wq_recv.at[0], here.beside)
    wq_core = [
        remote(wq.at[:, k], wq.at[:, k], wq_send.at[1 + i], wq_recv.at[1 + i], here.sibling)
        for i, k in enumerate((g, beside_g))
    ]
    for copy in own_copies[:3]:
        copy.wait()
    wq_beside.start()
    wq_core[0].start()
    next(a1_step)
    next(wo_step)
    next(a1_step)
    next(wo_step)
    wq_beside.wait_recv()
    wq_core[1].start()
    wd_far.start()
    next(a1_step)
    next(wo_step)
    for k in range(1, SHARDS):
        for copy in wu_copies(k):
            copy.start()
    for copy in own_copies[4:]:
        copy.wait()
    run(a1_step)
    dz_start, dz_relay, dz_last, dz_got = square_gather(here, dz, b["dz_sems"], ends)
    dz_start()

    for copy in wq_core:
        copy.wait_recv()
    qkv, probs = b["qkv"], b["probs"]
    qkv[...] = dot(flat(a1[...]), flat(wq[...])).astype(LOW).reshape(qkv.shape)
    keys = flat(qkv[:, :, LANES : 2 * LANES])
    values = flat(qkv[:, :, 2 * LANES :])
    key_items = jnp.concatenate(
        [jnp.where(live_rows[j : j + 1, :] > 0, item_rows[j : j + 1, :], -1) for j in range(SHARDS)], 1
    )
    lane = lax.broadcasted_iota(jnp.int32, (2 * ROWS, LANES), 1)
    mine = [lane < HEAD_DIM, lane >= HEAD_DIM]
    o_mine, o_all = b["o_mine"], b["o_all"]

    def o_copy(to, k):
        send, recv = b["o_sems"]
        return remote(o_mine.at[to], o_all.at[s], send.at[k], recv.at[k], (g, to))

    def attend(zz):
        pair = pl.ds(zz * 2, 2)
        queries = flat(qkv[pair, :, :LANES])
        items = jnp.concatenate([column(item_rows[pl.ds(zz * 2 + j, 1), :]) for j in range(2)], 0)
        allowed = jnp.concatenate([items] * SHARDS, 1) == key_items
        outs = []
        for h in range(2):
            scores = dot_nt(jnp.where(mine[h], queries, jnp.zeros_like(queries)), keys) * score_scale
            scores = jnp.where(allowed, scores, -1e30)
            peak = jnp.max(scores, -1, keepdims=True)
            expo = jnp.exp(scores - peak)
            chance = (expo * (1.0 / jnp.sum(expo, -1, keepdims=True))).astype(LOW)
            probs[h, pair] = chance.reshape(2, ROWS, WIDTH)
            outs.append(dot(chance, values))
        o_mine[pair] = jnp.where(mine[0], outs[0], outs[1]).astype(LOW).reshape(2, ROWS, LANES)

    for step in range(1, 4):
        zz = (z + step) % 4
        attend(zz)
        for j in range(2):
            to = zz * 2 + j
            o_copy(to, (to + SHARDS - s) % SHARDS).start()
        if step == 1:
            run(wo_step)
            wo_core[0].start()
    for i in range(SHARDS):
        wo_beside(i, beside_g).wait_recv()
    wo_core[1].start()
    attend(z)
    o_all[s] = o_mine[s]
    o_copy(here.across[1], (here.across[1] + SHARDS - s) % SHARDS).start()
    wd_far.wait_recv()
    wd_beside.start()
    for k in range(1, SHARDS):
        wu_whole(k).wait_recv()
    wu_beside.start()
    dz_relay()
    for k in range(1, SHARDS):
        o_copy(here.from_shard(k), k).wait_recv()
    for copy in wo_core:
        copy.wait_recv()

    attended = jnp.concatenate([o_all[j] for j in range(SHARDS)], 1)
    h1 = tok[...].astype(F32) + dot(attended, wo[...].reshape(WIDTH, WIDTH))
    b["h1"][...] = h1
    n2, inverse = centre(h1)
    b["n2"][...] = n2
    b["r2"][...] = jnp.broadcast_to(inverse, (ROWS, LANES))
    a2 = b["a2"]
    a2[c, corner] = (n2 * wide(norm, 2) + wide(norm, 3)).astype(LOW)
    a2_start, a2_relay, a2_last, a2_got = square_gather(here, a2, b["a2_sems"], ends)
    a2_start()
    dz_last()
    a2_relay()
    wu_beside.wait_recv()
    wd_beside.wait_recv()

    act, du, da2, dact = b["act"], b["du"], b["da2"], b["dact"]
    up = wu[...].reshape(WIDTH, HIDDEN)
    down = wd[...].reshape(HIDDEN, WIDTH)
    start, go, end = square_sum(here, lambda cc, at: da2.at[cc * 4 + at], b["e2"], b["da2_sum"])
    shape = (2, ROWS, HIDDEN)

    def feed(i):
        at = here.corners[i]
        u = dot(flat(a2[:, at]), up)
        half_erf = 0.5 + 0.5 * lax.erf(u * (0.5**0.5))
        act[:, at] = (u * half_erf).astype(LOW).reshape(shape)
        slope = half_erf + u * jnp.exp(-0.5 * u * u) * (1.0 / math.sqrt(2.0 * math.pi))
        grad = (flat(dact[:, at]) * slope).astype(LOW)
        du[:, at] = grad.reshape(shape)
        grad = dot_nt(grad, up).astype(LOW)
        for cc in range(2):
            da2[cc * 4 + at] = grad[cc * ROWS : (cc + 1) * ROWS]

    for i in range(4):
        dz_got(i)
    dact[...] = dot_nt(flat(dz[...]), down).reshape(dact.shape)
    a2_got(0)
    feed(0)
    start(0)
    a2_got(1)
    feed(1)
    start(1)
    a2_last()
    a2_got(2)
    feed(2)
    start(2)
    go(1)
    a2_got(3)
    feed(3)
    start(3)
    go(2)
    go(3)
    ffn = b["ffn"]
    f_start, f_go, f_end = square_sum(here, lambda cc, at: ffn.at[cc, at], b["block"], b["ffn_sum"])
    ffn[...] = dot(flat(act[...]), down).astype(LOW).reshape(ffn.shape)
    for i in range(4):
        f_start(i)
    gd = b["gd"]
    gd[...] = dot_tn(flat(act[...]), flat(dz[...])).astype(LOW).reshape(gd.shape)
    gd_step = pair_sum(here, gd, b["gd_total"], b["gd_sum"], ends)
    next(gd_step)
    gu = b["gu"]
    gu[...] = dot_tn(flat(a2[...]), flat(du[...])).astype(LOW).reshape(gu.shape)
    gu_step = pair_sum(here, gu, b["gu_total"], b["gu_sum"], ends)
    next(gu_step)
    go(0)
    end()

    e2, n2 = b["e2"][...], b["n2"][...]
    dh1 = centre_back(e2, n2, b["r2"][:, :1], wide(norm, 2)) + dz[c, corner].astype(F32)
    b["dh1"][...] = dh1
    low = dh1.astype(LOW)
    do_mine, do_all = b["do_mine"], b["do_all"]
    for k in range(SHARDS):
        do_mine[k] = dot_nt(low, wo[k].reshape(ROWS, WIDTH)).astype(LOW)
    do_step = plane_trade(here, do_mine, do_all, b["do_sems"], ends)
    next(do_step)
    go_part = b["go"]
    go_part[...] = dot_tn(attended, low).astype(LOW).reshape(go_part.shape)
    go_step = cross_sum(here, go_part, b["go_total"], b["go_sum"], ends)
    next(go_step)
    next(go_step)
    run(do_step)
    next(gd_step)
    for i in range(1, 4):
        f_go(i)
    f_go(0)

    gk, gv, dqkv = b["gk"], b["gv"], b["dqkv"]

    def back(zz, first):
        pair = pl.ds(zz * 2, 2)
        queries, outs = flat(qkv[pair, :, :LANES]), flat(do_all[pair])
        queries_t, outs_t = queries.T, outs.T
        grad_query, grad_key, grad_value = [], [], []
        for h in range(2):
            chance_low = flat(probs[h, pair])
            chance = chance_low.astype(F32)
            grad_chance = dot_nt(jnp.where(mine[h], outs, jnp.zeros_like(outs)), values)
            inner = jnp.sum(chance * grad_chance, -1, keepdims=True)
            grad_scores = (chance * (grad_chance - inner)).astype(LOW)
            lanes = slice(h * HEAD_DIM, (h + 1) * HEAD_DIM)
            grad_query.append(dot(grad_scores, keys))
            grad_key.append(dot(queries_t[lanes], grad_scores))
            grad_value.append(dot(outs_t[lanes], chance_low))
        grad_query = jnp.where(mine[0], grad_query[0], grad_query[1]) * score_scale
        dqkv[pair, :, :LANES] = grad_query.astype(LOW).reshape(2, ROWS, LANES)
        grad_key, grad_value = jnp.concatenate(grad_key, 0), jnp.concatenate(grad_value, 0)
        if first:
            gk[...], gv[...] = grad_key, grad_value
        else:
            gk[...] += grad_key
            gv[...] += grad_value

    back(0, True)
    back(1, False)
    next(gu_step)
    back(2, False)
    back(3, False)
    thirds = (SHARDS, ROWS, LANES)
    dqkv[:, :, LANES : 2 * LANES] = (gk[...].T * score_scale).astype(LOW).reshape(thirds)
    dqkv[:, :, 2 * LANES :] = gv[...].T.astype(LOW).reshape(thirds)

    da1, weight = da2, flat(wq[...])

    def spread(zz):
        pair = pl.ds(zz * 2, 2)
        da1[pair] = dot_nt(flat(dqkv[pair]), weight).astype(LOW).reshape(2, ROWS, WIDTH)

    da1_step = plane_sum(here, da1, b["e1"], b["da1_sum"], ends, spread)
    next(da1_step)
    gq = b["gq"]
    gq[...] = dot_tn(flat(a1[...]), flat(dqkv[...])).astype(LOW).reshape(gq.shape)
    gq_step = cross_sum(here, gq, b["gq_total"], b["gq_sum"], ends)
    next(gq_step)
    owner = here.y * 4 + c * 2 + half
    holder = x * 2 + here.near
    stays = (holder == g) & (owner == s)
    gd_away = remote(
        b["gd_total"], b["gd_land"], b["gd_sems"][0].at[0], b["gd_sems"][1].at[0], (holder, owner)
    )
    gu_total, gu_land = b["gu_total"], b["gu_land"]
    gu_send, gu_recv = b["gu_sems"]

    def gu_copy(k, i):
        core = here.g if k == 0 else here.sibling[0]
        cc = c if k == 0 else 1 - c
        return remote(
            gu_total.at[cc, here.corners[i]],
            gu_land.at[c, corner],
            gu_send.at[k, i],
            gu_recv.at[k, i],
            (core, here.square[i][1]),
        )

    def gu_came(k, i):
        cc = c if k == 0 else 1 - c
        block = gu_land.at[cc, here.corners[i]]
        return remote(block, block, gu_send.at[k, i], gu_recv.at[k, i], here.sibling)

    others = [(k, i) for k in range(2) for i in range(4) if (k, i) != (0, 0)]

    def send_gd():
        run(gd_step)

        @pl.when(jnp.logical_not(stays))
        def _():
            gd_away.start()

    def send_gu():
        run(gu_step)
        gu_land[c, corner] = gu_total[c, corner]
        for k, i in others:
            gu_copy(k, i).start()

    go_out = spread_sum(here, b["go_total"], out_sum, b["go_plane"], ends)
    gq_out = plane_trade(here, b["gq_total"], b["gq_land"], b["gq_sems"], ends)

    def send_go():
        run(go_step)
        next(go_out)

    def send_gq():
        run(gq_step)
        next(gq_out)

    send_gd()
    next(gq_step)
    next(da1_step)
    send_gu()
    send_go()
    next(da1_step)
    send_gq()
    next(da1_step)
    next(go_out)
    next(da1_step)
    run(da1_step)

    e1, n1 = b["e1"][...], b["n1"][...]
    count = jnp.sum(live_rows[pl.ds(s, 1), :].astype(F32), 1, keepdims=True)
    part = jnp.concatenate(
        [
            jnp.sum(e1 * n1, 0, keepdims=True),
            jnp.sum(e1, 0, keepdims=True),
            jnp.sum(e2 * n2, 0, keepdims=True),
            jnp.sum(e2, 0, keepdims=True),
            jnp.broadcast_to(count, (4, WIDTH)),
        ],
        0,
    )
    np_mine, np_land, np_all = b["np_mine"], b["np_land"], b["np_all"]
    n_send, n_recv, m_send, m_recv = b["np_sems"]
    for k in range(GROUPS):
        np_mine[k] = part[:, k * 2 * LANES : (k + 1) * 2 * LANES]

    def grp_copy(k):
        to = (g + k) % GROUPS
        return remote(np_mine.at[to], np_land.at[k], n_send.at[k], n_recv.at[k], (to, s))

    for k in range(1, GROUPS):
        grp_copy(k).start()
    input_grad[...] = centre_back(e1, n1, b["r1"][:, :1], wide(norm, 0)) + b["dh1"][...]
    for k in range(1, GROUPS):
        grp_copy(k).wait_recv()
    np_all[s] = np_mine[g] + np_land[1] + np_land[2] + np_land[3]

    def all_copy(k):
        return remote(np_all.at[s], np_all.at[s], m_send.at[k], m_recv.at[k], here.at_shard(k))

    for k in range(1, SHARDS):
        all_copy(k).start()

    f_end()
    block_out[...] = b["h1"][...] + b["block"][...]
    run(go_out)
    for k, i in others:
        gu_came(k, i).wait_recv()
    for cc in range(2):
        for at in range(4):
            for j in range(2):
                first = (j * 4 + at) * HIDDEN + cc * 256
                up_sum[:, first : first + 256] = gu_land[cc, at, :, j * 256 : (j + 1) * 256].astype(F32)
    run(gq_out)
    for j in range(SHARDS):
        for i in range(3):
            qkv_sum[:, i * WIDTH + j * LANES : i * WIDTH + (j + 1) * LANES] = b["gq_land"][
                j, :, i * LANES : (i + 1) * LANES
            ].astype(F32)

    @pl.when(stays)
    def _():
        down_sum[...] = b["gd_total"][...].astype(F32)

    @pl.when(jnp.logical_not(stays))
    def _():
        gd_away.wait_recv()
        down_sum[...] = b["gd_land"][...].astype(F32)
        gd_away.wait_send()

    for k in range(1, SHARDS):
        all_copy(k).wait_recv()
    total = np_all[0]
    for j in range(1, SHARDS):
        total += np_all[j]
    norm_sum[...] = pltpu.roll(total, 2 * LANES - s * 32, 1)[:, :LANES]

    for k in range(1, GROUPS):
        grp_copy(k).wait_send()
    for k in range(1, SHARDS):
        all_copy(k).wait_send()
        norm_copy(k).wait_send()
        wq_whole(k).wait_send()
        wu_whole(k).wait_send()
        o_copy(here.at_shard(k)[1], k).wait_send()
    for k, i in others:
        gu_copy(k, i).wait_send()
    for copy in (wq_beside, wd_far, wd_beside, wu_beside, *wq_core, *wo_core):
        copy.wait_send()
    for i in range(SHARDS):
        wo_beside(i, g).wait_send()
    for finish in ends:
        finish()


SIZES = ((32, 3 * WIDTH), (32, WIDTH), (32, 4 * WIDTH), (ROWS, WIDTH))
KINDS = (F32, F32, F32, F32, LOW)


def adamw_kernel(rates, *refs):
    refs = list(refs)

    def take(n):
        got = refs[:n]
        del refs[:n]
        return got

    norm_sum, *norm_old = take(4)
    sums, olds, passed = take(4), [take(3) for _ in SIZES], take(2)
    norm_new = take(5)
    news, handed = [take(5) for _ in SIZES], take(2)
    held_in, held_out = [take(4) for _ in SIZES], [take(5) for _ in SIZES]
    held_pass = take(2)
    in_sem, out_sem, pass_sem = take(3)
    loads = [
        [
            pltpu.make_async_copy(src, dst, in_sem.at[i, j])
            for j, (src, dst) in enumerate(zip([sums[i], *olds[i]], held_in[i]))
        ]
        for i in range(4)
    ]
    stores = [
        [pltpu.make_async_copy(src, dst, out_sem.at[i, j]) for j, (src, dst) in enumerate(zip(held_out[i], news[i]))]
        for i in range(4)
    ]
    passes = [pltpu.make_async_copy(passed[i], held_pass[i], pass_sem.at[i]) for i in range(2)]
    hands = [pltpu.make_async_copy(held_pass[i], handed[i], pass_sem.at[2 + i]) for i in range(2)]
    order = (2, 0, 3, 1)
    for i in order:
        for copy in loads[i]:
            copy.start()
    for copy in passes:
        copy.start()
    count = norm_sum[4:5, 0:1]
    results = adamw(norm_sum[0:4, 0:32], count, *[ref[...] for ref in norm_old], rates[4], 0.0)
    for ref, value in zip(norm_new, results):
        ref[...] = value
    for i in order:
        for copy in loads[i]:
            copy.wait()
        rows, cols = SIZES[i]
        step = 16

        def some(k, carry):
            at = pl.ds(pl.multiple_of(k * step, step), step)
            for first in range(0, cols, WIDTH):
                lanes = slice(first, first + WIDTH)
                summed, *old = [ref[at, lanes] for ref in held_in[i]]
                results = adamw(summed, count, *old, rates[i], 0.1)
                for ref, value in zip(held_out[i], results):
                    ref[at, lanes] = value
            return carry

        lax.fori_loop(0, rows // step, some, 0)
        for copy in stores[i]:
            copy.start()
    for i in range(2):
        passes[i].wait()
        hands[i].start()
    for i in order:
        for copy in stores[i]:
            copy.wait()
    for copy in hands:
        copy.wait()


def shaped(kind, *shape):
    return jax.ShapeDtypeStruct(shape, kind)


def call_adamw(rates, norms, sums, olds, passed):
    return pl.pallas_call(
        functools.partial(adamw_kernel, rates),
        out_shape=[shaped(kind, *norms[1].shape) for kind in KINDS]
        + [shaped(kind, *size) for size in SIZES for kind in KINDS]
        + [shaped(F32, ROWS, WIDTH)] * 2,
        in_specs=[VMEM] * 4 + [ANY] * 18,
        out_specs=[VMEM] * 5 + [ANY] * 22,
        scratch_shapes=[buffer(F32, *size) for size in SIZES for _ in range(4)]
        + [buffer(kind, *size) for size in SIZES for kind in KINDS]
        + [buffer(F32, ROWS, WIDTH)] * 2
        + [DMA((4, 4)), DMA((4, 5)), DMA((4,))],
        compiler_params=pltpu.CompilerParams(vmem_limit_bytes=60 * 2**20),
    )(*norms, *sums, *olds, *passed)


def fast_body(
    tokens, cotangent, item_ids, live_mask, qkv_weight, out_weight, up_weight, down_weight, norm_weight,
    qkv_master, qkv_first, qkv_second, out_master, out_first, out_second, up_master, up_first, up_second,
    down_master, down_first, down_second, norm_master, norm_first, norm_second,
):
    rows = item_ids.shape[0]
    args = (
        tokens,
        cotangent,
        item_ids.reshape(SHARDS, ROWS),
        live_mask.reshape(SHARDS, ROWS),
        norm_weight,
        qkv_weight,
        out_weight,
        up_weight,
        down_weight,
    )
    scratch = []
    for kind in scratch_plan().values():
        scratch += kind if isinstance(kind, list) else [kind]
    block_out, input_grad, qkv_sum, up_sum, out_sum, down_sum, norm_sum = pl.pallas_call(
        step_kernel,
        out_shape=[
            shaped(F32, ROWS, WIDTH),
            shaped(F32, ROWS, WIDTH),
            shaped(F32, 32, 3 * WIDTH),
            shaped(F32, 32, 4 * WIDTH),
            shaped(F32, 32, WIDTH),
            shaped(F32, ROWS, WIDTH),
            shaped(F32, 8, LANES),
        ],
        in_specs=[VMEM] * 5 + [ANY] * 4,
        out_specs=[VMEM] * 7,
        scratch_shapes=scratch,
        compiler_params=pltpu.CompilerParams(
            collective_id=0, has_side_effects=True, vmem_limit_bytes=60 * 2**20
        ),
    )(*args)
    model_width, hidden = tokens.shape[1], up_weight.shape[1]
    rates = (
        model_width ** (-0.5),
        math.sqrt(rows) / 64,
        model_width ** (-0.5),
        hidden ** (-0.5),
        0.4,
    )
    news = call_adamw(
        rates,
        (norm_sum, norm_master, norm_first, norm_second),
        (qkv_sum, out_sum, up_sum, down_sum),
        (
            qkv_master, qkv_first, qkv_second, out_master, out_first, out_second,
            up_master, up_first, up_second, down_master, down_first, down_second,
        ),
        (block_out, input_grad),
    )
    return (*news[25:], *news[5:25], *news[:5])


def suits(mesh):
    return mesh.shape["grp"] == GROUPS and mesh.shape["shard"] == SHARDS


def solution(mesh):
    placed = (
        P(("grp", "shard"), None),
        P(("grp", "shard"), None),
        P("grp"),
        P("grp"),
        P("shard", None),
        P("shard", None),
        P("shard", None),
        P("shard", None),
        P(None, "shard"),
        P(("grp", "shard"), None),
        P(("grp", "shard"), None),
        P(("grp", "shard"), None),
        P(("grp", "shard"), None),
        P(("grp", "shard"), None),
        P(("grp", "shard"), None),
        P(("grp", "shard"), None),
        P(("grp", "shard"), None),
        P(("grp", "shard"), None),
        P(("grp", "shard"), None),
        P(("grp", "shard"), None),
        P(("grp", "shard"), None),
        P(None, ("grp", "shard")),
        P(None, ("grp", "shard")),
        P(None, ("grp", "shard")),
    )
    return jax.shard_map(
        fast_body if suits(mesh) else body,
        mesh=mesh,
        in_specs=placed,
        out_specs=(
            P(("grp", "shard"), None),
            P(("grp", "shard"), None),
            P(("grp", "shard"), None),
            P(("grp", "shard"), None),
            P(("grp", "shard"), None),
            P(("grp", "shard"), None),
            P(("grp", "shard"), None),
            P(("grp", "shard"), None),
            P(("grp", "shard"), None),
            P(("grp", "shard"), None),
            P(("grp", "shard"), None),
            P(("grp", "shard"), None),
            P(("grp", "shard"), None),
            P(("grp", "shard"), None),
            P(("grp", "shard"), None),
            P(("grp", "shard"), None),
            P(("grp", "shard"), None),
            P(("grp", "shard"), None),
            P(("grp", "shard"), None),
            P(("grp", "shard"), None),
            P(("grp", "shard"), None),
            P(("grp", "shard"), None),
            P(None, ("grp", "shard")),
            P(None, ("grp", "shard")),
            P(None, ("grp", "shard")),
            P(None, ("grp", "shard")),
            P(None, ("grp", "shard")),
        ),
        check_vma=False,
    )
```

```python
import functools
import math

import jax
import jax.numpy as jnp
from jax import lax
from jax.experimental import pallas as pl
from jax.experimental.pallas import tpu as pltpu
from jax.sharding import PartitionSpec as P

HEADS = 16
HEAD_DIM = 64
STEP = 5


eps_norm = 1e-06
score_scale = 0.125


def exact_gelu(inputs):
    return jax.nn.gelu(inputs, approximate=False)


def outer_sum(left, right):
    return lax.dot_general(
        left, right, (((0,), (0,)), ((), ())), preferred_element_type=jnp.float32
    )


def back_dot(gradient, weight):
    return lax.dot_general(
        gradient, weight, (((1,), (1,)), ((), ())), preferred_element_type=jnp.float32
    )


def norm_forward(values, gain, shift):
    mean = jnp.mean(values, -1, keepdims=True)
    centred = values - mean
    variance = jnp.mean(centred * centred, -1, keepdims=True)
    inverse = lax.rsqrt(variance + eps_norm)
    normed = centred * inverse
    return (normed * gain + shift, normed, inverse)


def norm_backward(upstream, normed, inverse, gain):
    scaled = upstream * gain
    mean_one = jnp.mean(scaled, -1, keepdims=True)
    mean_two = jnp.mean(scaled * normed, -1, keepdims=True)
    return (
        inverse * (scaled - mean_one - normed * mean_two),
        jnp.sum(upstream * normed, 0),
        jnp.sum(upstream, 0),
    )


def block_scores(queries, query_items, key_heads, key_items, key_live):
    scores = (
        jnp.einsum("qhd,khd->qhk", queries, key_heads, preferred_element_type=jnp.float32)
        * score_scale
    )
    allowed = (query_items[:, None] == key_items[None, :]) & (key_live[None, :] > 0)
    return (scores, allowed[:, None, :])


def score_grads(
    queries, query_items, grad_out, log_total, grad_dot, key_heads, value_heads, key_items, key_live
):
    scores, allowed = block_scores(queries, query_items, key_heads, key_items, key_live)
    attention = jnp.where(allowed, jnp.exp(scores - log_total[..., None]), 0.0)
    grad_attention = jnp.einsum(
        "qhd,khd->qhk", grad_out, value_heads, preferred_element_type=jnp.float32
    )
    grad_scores = (attention * (grad_attention - grad_dot[..., None])).astype(jnp.bfloat16)
    return (grad_scores, attention.astype(jnp.bfloat16))


def key_terms(grad_scores, attention_low, queries, grad_out):
    grad_key = (
        jnp.einsum("qhk,qhd->khd", grad_scores, queries, preferred_element_type=jnp.float32)
        * score_scale
    )
    grad_value = jnp.einsum(
        "qhk,qhd->khd", attention_low, grad_out, preferred_element_type=jnp.float32
    )
    return (grad_key, grad_value)


def query_term(grad_scores, key_heads):
    return (
        jnp.einsum("qhk,khd->qhd", grad_scores, key_heads, preferred_element_type=jnp.float32)
        * score_scale
    )


def key_blocks(shard_piece, item_ids, live_mask):
    piece_rows = shard_piece.shape[0]
    block_rows = math.gcd(piece_rows, 512)
    block_count = piece_rows // block_rows
    heads = shard_piece.reshape(block_count, block_rows, 2, HEADS, HEAD_DIM)
    key_items = item_ids.reshape(block_count, block_rows)
    key_live = live_mask.reshape(block_count, block_rows)
    return (heads[:, :, 0], heads[:, :, 1], key_items, key_live, block_rows)


def attend_fold(queries, query_items, item_ids, live_mask, carried, shard_piece):
    key_heads, value_heads, key_items, key_live, block_rows = key_blocks(
        shard_piece, item_ids, live_mask
    )

    def attend_advance(running, current):
        running_max, running_sum, weighted_sum = running
        key_block, value_block, item_block, live_block = current
        scores, allowed = block_scores(queries, query_items, key_block, item_block, live_block)
        new_max = jnp.maximum(running_max, jnp.max(jnp.where(allowed, scores, -1e30), -1))
        attention = jnp.where(allowed, jnp.exp(scores - new_max[..., None]), 0.0)
        factor = jnp.exp(running_max - new_max)
        running_sum = running_sum * factor + jnp.sum(attention, -1)
        weighted_sum = weighted_sum * factor[..., None] + jnp.einsum(
            "qhk,khd->qhd",
            attention.astype(jnp.bfloat16),
            value_block,
            preferred_element_type=jnp.float32,
        )
        return ((new_max, running_sum, weighted_sum), None)

    carried, _ = lax.scan(attend_advance, carried, (key_heads, value_heads, key_items, key_live))
    return carried


def summed_fold(queries, query_items, grad_out, log_total, grad_dot, item_ids, live_mask):

    def fold_keys(carried, shard_piece, first_row):
        grad_query, grad_pairs = carried
        key_heads, value_heads, key_items, key_live, block_rows = key_blocks(
            shard_piece, item_ids, live_mask
        )

        def fold_advance(running, current):
            key_block, value_block, item_block, live_block = current
            grad_scores, attention_low = score_grads(
                queries,
                query_items,
                grad_out,
                log_total,
                grad_dot,
                key_block,
                value_block,
                item_block,
                live_block,
            )
            grad_key, grad_value = key_terms(grad_scores, attention_low, queries, grad_out)
            paired = jnp.concatenate(
                [grad_key.reshape(block_rows, -1), grad_value.reshape(block_rows, -1)], 1
            )
            return (running + query_term(grad_scores, key_block), paired)

        grad_query, pieces = lax.scan(
            fold_advance, grad_query, (key_heads, value_heads, key_items, key_live)
        )
        grad_pairs = pieces.reshape(shard_piece.shape[0], -1)
        return (grad_query, grad_pairs)

    return fold_keys


def adamw(summed, live_total, master, old_first, old_second, step_rate, shrink):
    gradient = summed / live_total
    moment = 0.5 * old_first + 0.5 * gradient
    square = 0.5 * old_second + 0.5 * gradient * gradient
    correction = 1.0 - 0.5**STEP
    updated = master - step_rate * (
        moment / correction / (jnp.sqrt(square / correction) + 1e-08) + shrink * master
    )
    return (gradient, moment, square, updated, updated.astype(jnp.bfloat16))


def body(
    tokens,
    cotangent,
    item_ids,
    live_mask,
    qkv_weight,
    out_weight,
    up_weight,
    down_weight,
    norm_weight,
    qkv_master,
    qkv_first,
    qkv_second,
    out_master,
    out_first,
    out_second,
    up_master,
    up_first,
    up_second,
    down_master,
    down_first,
    down_second,
    norm_master,
    norm_first,
    norm_second,
):
    local_rows = tokens.shape[0]
    model_width = tokens.shape[1]
    group_rows = item_ids.shape[0]
    offset = lax.axis_index("shard") * local_rows
    qkv_full, out_full, up_full, down_full, norm_full = (
        lax.all_gather(qkv_weight, "shard", axis=0, tiled=True),
        lax.all_gather(out_weight, "shard", axis=0, tiled=True),
        lax.all_gather(up_weight, "shard", axis=0, tiled=True),
        lax.all_gather(down_weight, "shard", axis=0, tiled=True),
        lax.all_gather(norm_weight, "shard", axis=1, tiled=True),
    )
    hidden = up_full.shape[1]
    norm_values = norm_full.astype(jnp.float32)
    live_rows = lax.dynamic_slice_in_dim(live_mask, offset, local_rows)
    query_items = lax.dynamic_slice_in_dim(item_ids, offset, local_rows)
    group_count = jnp.sum(live_mask).astype(jnp.float32)
    total_count = lax.psum(group_count, "grp")
    inputs = tokens.astype(jnp.float32)
    first_norm, normed_one, inverse_one = norm_forward(inputs, norm_values[0], norm_values[1])
    first_low = first_norm.astype(jnp.bfloat16)
    projected = jnp.dot(first_low, qkv_full, preferred_element_type=jnp.float32).astype(
        jnp.bfloat16
    )
    query_flat = projected[:, :model_width]
    queries = query_flat.reshape(local_rows, HEADS, HEAD_DIM)
    key_values = projected[:, model_width:]
    start_state = (
        jnp.full((local_rows, HEADS), -1e30, jnp.float32),
        jnp.zeros((local_rows, HEADS), jnp.float32),
        jnp.zeros((local_rows, HEADS, HEAD_DIM), jnp.float32),
    )
    running_max, running_sum, weighted_sum = attend_fold(
        queries,
        query_items,
        item_ids,
        live_mask,
        start_state,
        lax.all_gather(key_values, "shard", axis=0, tiled=True),
    )
    attended = weighted_sum / running_sum[..., None]
    log_total = running_max + jnp.log(running_sum)
    attended_low = attended.reshape(local_rows, model_width).astype(jnp.bfloat16)
    mixed = inputs + jnp.dot(attended_low, out_full, preferred_element_type=jnp.float32)
    second_norm, normed_two, inverse_two = norm_forward(mixed, norm_values[2], norm_values[3])
    second_low = second_norm.astype(jnp.bfloat16)
    expanded = jnp.dot(second_low, up_full, preferred_element_type=jnp.float32)
    activated, gelu_pull = jax.vjp(exact_gelu, expanded)
    activated_low = activated.astype(jnp.bfloat16)
    block_out = mixed + jnp.dot(activated_low, down_full, preferred_element_type=jnp.float32)
    upstream = cotangent.astype(jnp.float32) * live_rows.astype(jnp.float32)[:, None]
    upstream_low = upstream.astype(jnp.bfloat16)
    down_term = outer_sum(activated_low, upstream_low)
    (grad_expanded,) = gelu_pull(back_dot(upstream_low, down_full))
    expanded_low = grad_expanded.astype(jnp.bfloat16)
    up_term = outer_sum(second_low, expanded_low)
    grad_mixed, gain_two, shift_two = norm_backward(
        back_dot(expanded_low, up_full), normed_two, inverse_two, norm_values[2]
    )
    grad_mixed = grad_mixed + upstream
    mixed_low = grad_mixed.astype(jnp.bfloat16)
    out_term = outer_sum(attended_low, mixed_low)
    grad_flat = back_dot(mixed_low, out_full).astype(jnp.bfloat16)
    grad_attended = grad_flat.reshape(local_rows, HEADS, HEAD_DIM)
    grad_dot = jnp.sum(grad_attended.astype(jnp.float32) * attended, -1)
    zero_query = jnp.zeros((local_rows, HEADS, HEAD_DIM), jnp.float32)
    fold_back = summed_fold(
        queries, query_items, grad_attended, log_total, grad_dot, item_ids, live_mask
    )
    start_back = (zero_query, jnp.zeros((group_rows, 2 * model_width), jnp.float32))
    folded = fold_back(
        start_back, lax.all_gather(key_values, "shard", axis=0, tiled=True), jnp.int32(0)
    )
    grad_query, grad_pairs = folded
    grad_kv = lax.psum_scatter(
        grad_pairs.astype(jnp.bfloat16), "shard", scatter_dimension=0, tiled=True
    ).astype(jnp.float32)
    grad_projected = jnp.concatenate(
        [grad_query.reshape(local_rows, model_width), grad_kv], 1
    ).astype(jnp.bfloat16)
    qkv_term = outer_sum(first_low, grad_projected)
    grad_first, gain_one, shift_one = norm_backward(
        back_dot(grad_projected, qkv_full), normed_one, inverse_one, norm_values[0]
    )
    input_grad = grad_first + grad_mixed
    norm_term = jnp.stack([gain_one, shift_one, gain_two, shift_two])
    qkv_sum, out_sum, up_sum, down_sum, norm_sum = (
        lax.psum_scatter(qkv_term, ("grp", "shard"), scatter_dimension=0, tiled=True),
        lax.psum_scatter(out_term, ("grp", "shard"), scatter_dimension=0, tiled=True),
        lax.psum_scatter(up_term, ("grp", "shard"), scatter_dimension=0, tiled=True),
        lax.psum_scatter(down_term, ("grp", "shard"), scatter_dimension=0, tiled=True),
        lax.psum_scatter(norm_term, ("grp", "shard"), scatter_dimension=1, tiled=True),
    )
    qkv_grad, qkv_moment, qkv_square, qkv_fresh, qkv_copy = adamw(
        qkv_sum, total_count, qkv_master, qkv_first, qkv_second, model_width ** (-0.5), 0.1
    )
    out_grad, out_moment, out_square, out_fresh, out_copy = adamw(
        out_sum, total_count, out_master, out_first, out_second, math.sqrt(group_rows) / 64, 0.1
    )
    up_grad, up_moment, up_square, up_fresh, up_copy = adamw(
        up_sum, total_count, up_master, up_first, up_second, model_width ** (-0.5), 0.1
    )
    down_grad, down_moment, down_square, down_fresh, down_copy = adamw(
        down_sum, total_count, down_master, down_first, down_second, hidden ** (-0.5), 0.1
    )
    norm_grad, norm_moment, norm_square, norm_fresh, norm_copy = adamw(
        norm_sum, total_count, norm_master, norm_first, norm_second, 0.4, 0.0
    )
    return (
        block_out,
        input_grad,
        qkv_grad,
        qkv_moment,
        qkv_square,
        qkv_fresh,
        qkv_copy,
        out_grad,
        out_moment,
        out_square,
        out_fresh,
        out_copy,
        up_grad,
        up_moment,
        up_square,
        up_fresh,
        up_copy,
        down_grad,
        down_moment,
        down_square,
        down_fresh,
        down_copy,
        norm_grad,
        norm_moment,
        norm_square,
        norm_fresh,
        norm_copy,
    )


MESH = pl.DeviceIdType.MESH
F32, LOW = jnp.float32, jnp.bfloat16
VMEM = pl.BlockSpec(memory_space=pltpu.VMEM)
ANY = pl.BlockSpec(memory_space=pltpu.HBM)
SHARDS, GROUPS = 8, 4
WIDTH, ROWS, LANES = 1024, 128, 128
HIDDEN = 512
DMA = pltpu.SemaphoreType.DMA


class Place:
    def __init__(self):
        self.g, self.s = lax.axis_index("grp"), lax.axis_index("shard")
        self.z, self.y = self.s // 2, self.s % 2
        self.x, self.c = self.g // 2, self.g % 2
        self.half, self.near = self.z // 2, self.z % 2
        self.corner = self.near * 2 + self.y
        g, s = self.g, self.s
        over = 1 - 2 * self.y
        along = 2 - 4 * self.near
        self.across = (g, s + over)
        self.up = (g, s + 2)
        self.down = (g, s - 2)
        self.far = (g, (s + 4) % SHARDS)
        self.sibling = (g + 1 - 2 * self.c, s)
        self.beside = ((g + 2) % GROUPS, s)
        self.square = [(g, s), self.across, (g, s + along), (g, s + along + over)]
        self.corners = [
            self.corner,
            self.corner + over,
            (self.corner + 2) % 4,
            (self.corner + over + 2) % 4,
        ]

    def at_shard(self, k):
        return (self.g, (self.s + k) % SHARDS)


def remote(src, dst, send, recv, device):
    return pltpu.make_async_remote_copy(
        src_ref=src, dst_ref=dst, send_sem=send, recv_sem=recv, device_id=device, device_id_type=MESH
    )


def greet_all(here):
    barrier = pltpu.get_barrier_semaphore()
    me, everyone = here.g * SHARDS + here.s, GROUPS * SHARDS

    def greet(k, carry):
        other = (me + k) % everyone
        pl.semaphore_signal(
            barrier, inc=1, device_id=(other // SHARDS, other % SHARDS), device_id_type=MESH
        )
        return carry

    lax.fori_loop(1, everyone, greet, 0)
    pl.semaphore_wait(barrier, everyone - 1)


def flat(value):
    return value.reshape(-1, value.shape[-1])


def dot(left, right):
    return lax.dot_general(left, right, (((1,), (0,)), ((), ())), preferred_element_type=F32)


def dot_nt(left, right):
    return lax.dot_general(left, right, (((1,), (1,)), ((), ())), preferred_element_type=F32)


def dot_tn(left, right):
    return lax.dot_general(left, right, (((0,), (0,)), ((), ())), preferred_element_type=F32)


def run(*steps):
    for step in steps:
        for _ in step:
            pass


def buffer(kind, *shape):
    return pltpu.VMEM(shape, kind)


def gather_sems():
    return [DMA((3, 4)), DMA((SHARDS,))]


def plane_gather(here, block, sems, ends, came=None):
    send, recv = sems
    z, y = here.z, here.y

    def copy(lane, zz, yy):
        device = (here.across, here.up, here.down)[lane]
        i = zz * 2 + yy
        return remote(block(i), block(i), send.at[lane, zz], recv.at[i], device)

    def arrived(zz, yy):
        copy(0, zz, yy).wait_recv()
        if came is not None:
            came(zz * 2 + yy)

    def finish():
        for zz in range(4):
            copy(0, zz, y).wait_send()

            @pl.when((zz <= z) & (z < 3))
            def _():
                copy(1, zz, y).wait_send()

            @pl.when((zz >= z) & (z > 0))
            def _():
                copy(2, zz, y).wait_send()

    ends.append(finish)

    @pl.when(z < 3)
    def _():
        copy(1, z, y).start()

    @pl.when(z > 0)
    def _():
        copy(2, z, y).start()

    copy(0, z, y).start()
    if came is not None:
        came(z * 2 + y)
    yield
    for step in range(1, 4):

        @pl.when(z >= step)
        def _():
            zz = z - step
            arrived(zz, y)

            @pl.when(z < 3)
            def _():
                copy(1, zz, y).start()

            copy(0, zz, y).start()

        @pl.when(z + step <= 3)
        def _():
            zz = z + step
            arrived(zz, y)

            @pl.when(z > 0)
            def _():
                copy(2, zz, y).start()

            copy(0, zz, y).start()

        yield
    for zz in range(4):
        arrived(zz, 1 - y)
    yield


def sum_scratch(rows):
    shape = (4, rows, WIDTH)
    return [buffer(LOW, *shape), buffer(LOW, *shape), buffer(LOW, 2, *shape)] + [DMA((4,))] * 3 + [DMA((2, 4))]


def plane_sum(here, part, total, scratch, ends, prepare=None):
    landed, ready, relayed, y_send, y_recv, z_send, z_recv = scratch
    z, y = here.z, here.y
    order = [
        jnp.where(z < 2, 3, 0),
        jnp.where(z == 0, 2, jnp.where(z == 1, 0, jnp.where(z == 2, 3, 1))),
        1 + z % 2,
        z,
    ]
    first = [
        remote(part.at[zz * 2 + 1 - y], landed.at[i], y_send.at[i], y_recv.at[i], here.across)
        for i, zz in enumerate(order)
    ]

    def relay(lane, zz):
        device = (here.up, here.down)[lane]
        return remote(ready.at[zz], relayed.at[lane, zz], z_send.at[zz], z_recv.at[lane, zz], device)

    for i, zz in enumerate(order):
        if prepare is not None:
            prepare(zz)
        first[i].start()
    yield
    for i, zz in enumerate(order):
        first[i].wait_recv()
        if i < 3:
            ready[zz] = (part[zz * 2 + y].astype(F32) + landed[i].astype(F32)).astype(LOW)

            @pl.when(zz > z)
            def _():
                @pl.when(z > 0)
                def _():
                    relay(0, zz).wait_recv()
                    ready[zz] = (ready[zz].astype(F32) + relayed[0, zz].astype(F32)).astype(LOW)

                relay(0, zz).start()

            @pl.when(zz < z)
            def _():
                @pl.when(z < 3)
                def _():
                    relay(1, zz).wait_recv()
                    ready[zz] = (ready[zz].astype(F32) + relayed[1, zz].astype(F32)).astype(LOW)

                relay(1, zz).start()

        else:
            total[...] = part[zz * 2 + y].astype(F32) + landed[i].astype(F32)
        yield

    @pl.when(z > 0)
    def _():
        relay(0, z).wait_recv()
        total[...] += relayed[0, z].astype(F32)

    @pl.when(z < 3)
    def _():
        relay(1, z).wait_recv()
        total[...] += relayed[1, z].astype(F32)

    def finish():
        for copy in first:
            copy.wait_send()
        for zz in order[:3]:
            relay(0, zz).wait_send()

    ends.append(finish)
    yield


def square_gather(here, held, sems, ends):
    send, recv, half_send, half_recv, sib_send, sib_recv = sems
    c = here.c
    cut = held.shape[2] // 2

    def part(at, k):
        return held.at[c, here.corners[at], pl.ds(k * cut, cut)]

    def copy(i, at, k):
        return remote(part(at, k), part(at, k), send.at[i - 1, k], recv.at[i - 1, k], here.square[i])

    def onward(i, at):
        block = part(at, i - 1)
        return remote(block, block, half_send.at[i - 1], half_recv.at[i - 1], here.square[3 - i])

    def pass_on(i):
        block = held.at[c, here.corners[i]]
        return remote(block, block, sib_send.at[i], sib_recv.at[i], here.sibling)

    def passed(i):
        block = held.at[1 - c, here.corners[i]]
        return remote(block, block, sib_send.at[i], sib_recv.at[i], here.sibling)

    def finish():
        for i in (1, 2):
            for k in range(2):
                copy(i, 0, k).wait_send()
            onward(i, i).wait_send()
        for i in range(4):
            pass_on(i).wait_send()

    ends.append(finish)

    def start():
        for k in range(2):
            for i in (1, 2):
                copy(i, 0, (i - 1 + k) % 2).start()
        pass_on(0).start()

    def relay():
        for i in (1, 2):
            copy(i, i, i - 1).wait_recv()
            onward(i, i).start()
        for i in (1, 2):
            copy(i, i, 2 - i).wait_recv()
            pass_on(i).start()

    def last():
        for i in (1, 2):
            onward(i, 3).wait_recv()
        pass_on(3).start()

    def got(i):
        passed(i).wait_recv()

    return start, relay, last, got


def square_sems():
    return [DMA((2, 2))] * 2 + [DMA((2,))] * 2 + [DMA((4,))] * 2


def square_scratch():
    shape = (4, ROWS, WIDTH)
    return [buffer(LOW, *shape)] * 3 + [DMA((4,))] * 4


def square_sum(here, part, total, scratch):
    landed, ready, final, sib_send, sib_recv, send, recv = scratch
    c = here.c

    def swap(i):
        return remote(
            part(1 - c, here.corners[i]), landed.at[i], sib_send.at[i], sib_recv.at[i], here.sibling
        )

    def ship(i):
        return remote(ready.at[i], final.at[i], send.at[i], recv.at[i], here.square[i])

    def start(i):
        swap(i).start()

    def go(i):
        swap(i).wait_recv()
        value = part(c, here.corners[i])[...].astype(F32) + landed[i].astype(F32)
        if i:
            ready[i] = value.astype(LOW)
            ship(i).start()
        else:
            total[...] = value

    def end():
        for i in range(1, 4):
            ship(i).wait_recv()
        total[...] += final[1].astype(F32) + final[2].astype(F32) + final[3].astype(F32)
        for i in range(4):
            swap(i).wait_send()
        for i in range(1, 4):
            ship(i).wait_send()

    return start, go, end


def cross_scratch(rows, cols):
    return [buffer(LOW, 2, rows, cols)] + [buffer(LOW, rows, cols)] * 2 + [DMA((2,))] * 2 + [DMA((1,))] * 2


def cross_sum(here, part, total, scratch, ends):
    landed, ready, final, c_send, c_recv, x_send, x_recv = scratch
    g, x, c = here.g, here.x, here.c
    first = [
        remote(part.at[xx * 2 + 1 - c], landed.at[xx], c_send.at[xx], c_recv.at[xx], here.sibling)
        for xx in range(2)
    ]
    second = remote(ready, final, x_send.at[0], x_recv.at[0], here.beside)
    for copy in first:
        copy.start()
    yield
    for copy in first:
        copy.wait_recv()
    ready[...] = (part[(1 - x) * 2 + c].astype(F32) + landed[1 - x].astype(F32)).astype(LOW)
    second.start()
    yield
    second.wait_recv()
    value = part[g].astype(F32) + landed[x].astype(F32) + final[...].astype(F32)
    total[...] = value.astype(total.dtype).reshape(total.shape)

    def finish():
        for copy in first + [second]:
            copy.wait_send()

    ends.append(finish)
    yield


def pair_scratch(rows, cols, parts=1):
    return [buffer(LOW, parts, 2, rows, cols)] + [buffer(LOW, parts, rows, cols)] * 2 + [DMA((1,))] * 4


def pair_sum(here, part, total, scratch, ends):
    landed, ready, final, x_send, x_recv, z_send, z_recv = scratch
    x, half = here.x, here.half
    first = remote(part.at[1 - x], landed, x_send.at[0], x_recv.at[0], here.beside)
    second = remote(ready, final, z_send.at[0], z_recv.at[0], here.far)
    first.start()
    yield
    first.wait_recv()
    ready[...] = (part[x, :, 1 - half].astype(F32) + landed[:, 1 - half].astype(F32)).astype(LOW)
    second.start()
    yield
    second.wait_recv()
    value = part[x, :, half].astype(F32) + landed[:, half].astype(F32) + final[...].astype(F32)
    total[...] = value.astype(LOW).reshape(total.shape)

    def finish():
        first.wait_send()
        second.wait_send()

    ends.append(finish)
    yield


def spread_scratch(rows):
    return [buffer(LOW, 4, rows, WIDTH)] * 3 + [DMA((1,))] * 2 + [DMA((4,))] * 2


def spread_sum(here, part, total, scratch, ends):
    landed, ready, final, y_send, y_recv, z_send, z_recv = scratch
    z, y = here.z, here.y
    first = remote(part.at[:, 1 - y], landed, y_send.at[0], y_recv.at[0], here.across)

    def second(k):
        to = (z + k) % 4
        return remote(ready.at[to], final.at[k], z_send.at[k], z_recv.at[k], (here.g, to * 2 + y))

    first.start()
    yield
    first.wait_recv()
    ready[...] = (part[:, y].astype(F32) + landed[...].astype(F32)).astype(LOW)
    for k in (2, 1, 3):
        second(k).start()
    yield
    value = ready[z].astype(F32)
    for k in range(1, 4):
        second(k).wait_recv()
        value += final[k].astype(F32)
    total[...] = value

    def finish():
        first.wait_send()
        for k in range(1, 4):
            second(k).wait_send()

    ends.append(finish)
    yield


def trade_sems():
    return [DMA((1,))] * 2


def all_sent(here, seven, sems):
    remote(seven, seven, sems[0].at[0], sems[1].at[0], here.across).wait_send()


def all_came(here, seven, sems):
    remote(seven, seven, sems[0].at[0], sems[1].at[0], here.across).wait_recv()


def plane_trade(here, mine, theirs, sems, ends, stay=None):
    send, recv = sems

    def copy(k):
        device = here.at_shard(k)
        return remote(mine.at[device[1]], theirs.at[here.s], send.at[0], recv.at[0], device)

    for k in range(1, SHARDS):
        copy(k).start()
    if stay is None:
        theirs[here.s] = mine[here.s]
    else:
        stay.start()
    yield
    all_came(here, theirs.at[pl.ds(0, SHARDS - 1)], sems)

    def finish():
        all_sent(here, mine.at[pl.ds(0, SHARDS - 1)], sems)
        if stay is not None:
            stay.wait()

    ends.append(finish)
    yield


def centre(values):
    mean = jnp.mean(values, -1, keepdims=True)
    centred = values - mean
    variance = jnp.mean(centred * centred, -1, keepdims=True)
    inverse = lax.rsqrt(variance + eps_norm)
    return centred * inverse, inverse


def centre_back(e, normed, inverse, gain):
    scaled = e * gain
    mean_one = jnp.mean(scaled, -1, keepdims=True)
    mean_two = jnp.mean(scaled * normed, -1, keepdims=True)
    return inverse * (scaled - mean_one - normed * mean_two)


def wide(norm, row):
    return jnp.concatenate([norm[j, row : row + 1, :] for j in range(SHARDS)], 1)


def column(row):
    return jnp.broadcast_to(row, (LANES, LANES)).T


def scratch_plan():
    plan = dict(
        own_norm=buffer(F32, 8, LANES),
        own_sems=DMA((SHARDS,)),
        norm=buffer(F32, SHARDS, 8, LANES),
        norm_sems=trade_sems(),
        wq=buffer(LOW, SHARDS, GROUPS, 32, 3 * LANES),
        wq_sems=trade_sems() + [DMA((3,))] * 2,
        wo=buffer(LOW, SHARDS, GROUPS, 32, WIDTH),
        wo_sems=gather_sems(),
        wo_more=[DMA((SHARDS + 2,))] * 2,
        wu=buffer(LOW, SHARDS, 2, 64, HIDDEN),
        wu_sems=trade_sems() + [DMA((1,))] * 2,
        wd=buffer(LOW, 2, 2, ROWS, WIDTH),
        wd_sems=[DMA((2,))] * 2,
        a1=buffer(LOW, SHARDS, ROWS, WIDTH),
        a1_sems=gather_sems(),
        a2=buffer(LOW, 2, 4, ROWS, WIDTH),
        a2_sems=square_sems(),
        dz=buffer(LOW, 2, 4, ROWS, WIDTH),
        dz_sems=square_sems(),
        qkv=buffer(LOW, SHARDS, ROWS, 3 * LANES),
        probs=buffer(LOW, 2, SHARDS, ROWS, WIDTH),
        o_mine=buffer(LOW, SHARDS, ROWS, LANES),
        o_all=buffer(LOW, SHARDS, ROWS, LANES),
        o_sems=trade_sems(),
        n1=buffer(F32, ROWS, WIDTH),
        r1=buffer(F32, ROWS, LANES),
        h1=buffer(F32, ROWS, WIDTH),
        n2=buffer(F32, ROWS, WIDTH),
        r2=buffer(F32, ROWS, LANES),
        act=buffer(LOW, 2, 4, ROWS, HIDDEN),
        du=buffer(LOW, 2, 4, ROWS, HIDDEN),
        dact=buffer(F32, 2, 4, ROWS, HIDDEN),
        da2=buffer(LOW, SHARDS, ROWS, WIDTH),
        da2_sum=square_scratch(),
        e2=buffer(F32, ROWS, WIDTH),
        ffn=buffer(LOW, SHARDS, ROWS, WIDTH),
        ffn_sum=square_scratch(),
        block=buffer(F32, ROWS, WIDTH),
        dh1=buffer(F32, ROWS, WIDTH),
        do_mine=buffer(LOW, SHARDS, ROWS, LANES),
        do_all=buffer(LOW, SHARDS, ROWS, LANES),
        do_sems=trade_sems(),
        gk=buffer(F32, LANES, WIDTH),
        gv=buffer(F32, LANES, WIDTH),
        dqkv=buffer(LOW, SHARDS, ROWS, 3 * LANES),
        da1_sum=sum_scratch(ROWS),
        e1=buffer(F32, ROWS, WIDTH),
        gd=buffer(LOW, 2, 1, 2, ROWS, WIDTH),
        gd_sum=pair_scratch(ROWS, WIDTH),
        gd_total=buffer(LOW, ROWS, WIDTH),
        gd_sems=[DMA((1,))] * 2,
        gu=buffer(LOW, 2, 2, 2, ROWS, HIDDEN),
        gu_sum=pair_scratch(ROWS, HIDDEN, 2),
        gu_total=buffer(LOW, 2, 4, 32, HIDDEN),
        gu_sems=[DMA((2, 4)), DMA((2, 4))],
        go=buffer(LOW, GROUPS, 256, WIDTH),
        go_sum=cross_scratch(256, WIDTH),
        go_total=buffer(LOW, 4, 2, 32, WIDTH),
        go_plane=spread_scratch(32),
        gq=buffer(LOW, GROUPS, 256, 3 * LANES),
        gq_sum=cross_scratch(256, 3 * LANES),
        gq_total=buffer(LOW, SHARDS, 32, 3 * LANES),
        gq_sems=trade_sems(),
        np_mine=buffer(F32, SHARDS, 8, LANES),
        np_land=buffer(F32, GROUPS * SHARDS, 8, LANES),
        np_sems=trade_sems(),
        go_sum32=buffer(F32, 32, WIDTH),
        dx=buffer(F32, ROWS, WIDTH),
        out_sems=DMA((6,)),
    )
    return plan


def step_kernel(*refs):
    plan = scratch_plan()
    inputs, refs = refs[:9], refs[9:]
    outputs, refs = refs[:7], list(refs[7:])
    tok, cot, item_rows, live_rows, norm_weight, wqkv, wout, wup, wdown = inputs
    block_out, input_grad, gq_land, gu_land, out_sum, gd_land, norm_sum = outputs
    b = {}
    for name, kind in plan.items():
        many = isinstance(kind, list)
        got = [refs.pop(0) for _ in range(len(kind) if many else 1)]
        b[name] = got if many else got[0]

    here = Place()
    g, s, x, c, z, y, half, corner = (
        here.g, here.s, here.x, here.c, here.z, here.y, here.half, here.corner
    )
    ends = []
    quarter = pl.ds(pl.multiple_of(g * 32, 32), 32)
    beside_g = here.beside[0]
    wq, wo, wu, wd = b["wq"], b["wo"], b["wu"], b["wd"]
    wu_rows = pl.ds(pl.multiple_of(x * 64, 64), 64)

    def wu_columns(shard, j):
        return pl.ds(pl.multiple_of((shard % 4 + j * 4) * HIDDEN + c * 256, 256), 256)

    own_pairs = [
        (
            wqkv.at[quarter, pl.ds(pl.multiple_of(j * WIDTH + s * LANES, LANES), LANES)],
            wq.at[s, g, :, pl.ds(j * LANES, LANES)],
        )
        for j in range(3)
    ]
    own_pairs.append((wout.at[quarter, :], wo.at[s, g]))
    own_pairs += [(wup.at[wu_rows, wu_columns(s, j)], wu.at[s, x, :, pl.ds(j * 256, 256)]) for j in range(2)]
    own_pairs += [
        (wdown.at[pl.ds(pl.multiple_of(c * 256 + j * ROWS, ROWS), ROWS), :], wd.at[half, j]) for j in range(2)
    ]
    own_copies = [pltpu.make_async_copy(*pair, b["own_sems"].at[i]) for i, pair in enumerate(own_pairs)]
    for copy in own_copies:
        copy.start()
    greet_all(here)

    norm, own_norm = b["norm"], b["own_norm"]
    own_norm[...] = jnp.zeros_like(own_norm)
    own_norm[0:4, :] = norm_weight[...].astype(F32)
    norm[s] = own_norm[...]

    def norm_copy(k):
        send, recv = b["norm_sems"]
        return remote(own_norm, norm.at[s], send.at[0], recv.at[0], here.at_shard(k))

    def wq_copies(k):
        device = here.at_shard(k)
        send, recv = b["wq_sems"][:2]
        return [
            remote(
                wqkv.at[quarter, pl.ds(pl.multiple_of(j * WIDTH + device[1] * LANES, LANES), LANES)],
                wq.at[s, g, :, pl.ds(j * LANES, LANES)],
                send.at[0],
                recv.at[0],
                device,
            )
            for j in range(3)
        ]

    for k in range(1, SHARDS):
        norm_copy(k).start()
    for k in range(1, SHARDS):
        for copy in wq_copies(k):
            copy.start()
    n1, inverse = centre(tok[...].astype(F32))
    b["n1"][...] = n1
    b["r1"][...] = jnp.broadcast_to(inverse, (ROWS, LANES))
    a1, raw = b["a1"], b["ffn"]
    raw[s] = n1.astype(LOW)
    a1_step = plane_gather(here, lambda i: raw.at[i], b["a1_sems"], ends)
    next(a1_step)
    raw_sent = ends.pop()

    own_copies[3].wait()
    wo_send, wo_recv = b["wo_more"]

    def wo_beside(i, k):
        block = wo.at[i, k]
        return remote(block, block, wo_send.at[i], wo_recv.at[i], here.beside)

    def wo_came(i):
        wo_beside(i, g).start()

    wo_step = plane_gather(here, lambda i: wo.at[i, g], b["wo_sems"], ends, wo_came)
    next(wo_step)
    wo_core = [
        remote(wo.at[:, k], wo.at[:, k], wo_send.at[SHARDS + i], wo_recv.at[SHARDS + i], here.sibling)
        for i, k in enumerate((g, beside_g))
    ]

    wd_send, wd_recv = b["wd_sems"]
    wd_rows = pl.ds(pl.multiple_of(c * 256 + x * ROWS, ROWS), ROWS)
    wd_far = remote(wdown.at[wd_rows, :], wd.at[half, x], wd_send.at[0], wd_recv.at[0], here.far)
    wd_beside = remote(
        wd.at[1 - half, x], wd.at[1 - half, x], wd_send.at[1], wd_recv.at[1], here.beside
    )

    wu_send, wu_recv, wu_xsend, wu_xrecv = b["wu_sems"]

    def wu_copies(k):
        device = here.at_shard(k)
        return [
            remote(
                wup.at[wu_rows, wu_columns(device[1], j)],
                wu.at[s, x, :, pl.ds(j * 256, 256)],
                wu_send.at[0],
                wu_recv.at[0],
                device,
            )
            for j in range(2)
        ]

    wu_beside = remote(wu.at[:, x], wu.at[:, x], wu_xsend.at[0], wu_xrecv.at[0], here.beside)

    dz = b["dz"]
    own_live = column(live_rows[pl.ds(s, 1), :].astype(F32))
    dz[c, corner] = (cot[...].astype(F32) * jnp.concatenate([own_live] * SHARDS, 1)).astype(LOW)
    all_came(here, wq.at[pl.ds(0, SHARDS - 1), g], b["wq_sems"])
    wq_send, wq_recv = b["wq_sems"][2:]
    wq_beside = remote(wq.at[:, g], wq.at[:, g], wq_send.at[0], wq_recv.at[0], here.beside)
    wq_core = [
        remote(wq.at[:, k], wq.at[:, k], wq_send.at[1 + i], wq_recv.at[1 + i], here.sibling)
        for i, k in enumerate((g, beside_g))
    ]
    for copy in own_copies[:3]:
        copy.wait()
    wq_beside.start()
    wq_core[0].start()
    next(a1_step)
    next(wo_step)
    next(a1_step)
    next(wo_step)
    wq_beside.wait_recv()
    wq_core[1].start()
    wd_far.start()
    next(a1_step)
    next(wo_step)
    for copy in own_copies[4:]:
        copy.wait()

    for copy in wq_core:
        copy.wait_recv()
    all_came(here, norm.at[pl.ds(0, SHARDS - 1)], b["norm_sems"])
    qkv, probs = b["qkv"], b["probs"]
    gain, shift, weight = wide(norm, 0), wide(norm, 1), flat(wq[...])

    def project(yy):
        rows = []
        for zz in range(4):
            value = (raw[zz * 2 + yy].astype(F32) * gain + shift).astype(LOW)
            a1[zz * 2 + yy] = value
            rows.append(value)
        out = dot(jnp.concatenate(rows, 0), weight).astype(LOW)
        for zz in range(4):
            qkv[zz * 2 + yy] = out[zz * ROWS : (zz + 1) * ROWS]

    project(y)
    run(a1_step)
    for k in range(1, SHARDS):
        for copy in wu_copies(k):
            copy.start()
    dz_start, dz_relay, dz_last, dz_got = square_gather(here, dz, b["dz_sems"], ends)
    project(1 - y)
    keys = flat(qkv[:, :, LANES : 2 * LANES])
    values = flat(qkv[:, :, 2 * LANES :])
    key_items = jnp.concatenate(
        [jnp.where(live_rows[j : j + 1, :] > 0, item_rows[j : j + 1, :], -1) for j in range(SHARDS)], 1
    )
    lane = lax.broadcasted_iota(jnp.int32, (2 * ROWS, LANES), 1)
    mine = [lane < HEAD_DIM, lane >= HEAD_DIM]
    o_mine, o_all = b["o_mine"], b["o_all"]

    def o_copy(to):
        send, recv = b["o_sems"]
        return remote(o_mine.at[to], o_all.at[s], send.at[0], recv.at[0], (g, to))

    def attend(zz):
        pair = pl.ds(zz * 2, 2)
        queries = flat(qkv[pair, :, :LANES])
        items = jnp.concatenate([column(item_rows[pl.ds(zz * 2 + j, 1), :]) for j in range(2)], 0)
        allowed = jnp.concatenate([items] * SHARDS, 1) == key_items
        outs = []
        for h in range(2):
            scores = dot_nt(jnp.where(mine[h], queries, jnp.zeros_like(queries)), keys) * score_scale
            scores = jnp.where(allowed, scores, -1e30)
            peak = jnp.max(scores, -1, keepdims=True)
            expo = jnp.exp(scores - peak)
            chance = (expo * (1.0 / jnp.sum(expo, -1, keepdims=True))).astype(LOW)
            probs[h, pair] = chance.reshape(2, ROWS, WIDTH)
            outs.append(dot(chance, values))
        o_mine[pair] = jnp.where(mine[0], outs[0], outs[1]).astype(LOW).reshape(2, ROWS, LANES)

    for step in range(1, 4):
        zz = (z + step) % 4
        attend(zz)
        for j in range(2):
            to = zz * 2 + j
            o_copy(to).start()
        if step == 1:
            run(wo_step)
            wo_core[0].start()
    for i in range(SHARDS):
        wo_beside(i, beside_g).wait_recv()
    wo_core[1].start()
    attend(z)
    o_all[s] = o_mine[s]
    dz_start()
    o_copy(here.across[1]).start()
    wd_far.wait_recv()
    wd_beside.start()
    all_came(here, wu.at[pl.ds(0, SHARDS - 1), x], b["wu_sems"])
    wu_beside.start()
    dz_relay()
    all_came(here, o_all.at[pl.ds(0, SHARDS - 1)], b["o_sems"])
    for copy in wo_core:
        copy.wait_recv()

    attended = jnp.concatenate([o_all[j] for j in range(SHARDS)], 1)
    h1 = tok[...].astype(F32) + dot(attended, wo[...].reshape(WIDTH, WIDTH))
    b["h1"][...] = h1
    n2, inverse = centre(h1)
    b["n2"][...] = n2
    b["r2"][...] = jnp.broadcast_to(inverse, (ROWS, LANES))
    a2 = b["a2"]
    a2[c, corner] = (n2 * wide(norm, 2) + wide(norm, 3)).astype(LOW)
    a2_start, a2_relay, a2_last, a2_got = square_gather(here, a2, b["a2_sems"], ends)
    a2_start()
    dz_last()
    a2_relay()
    wu_beside.wait_recv()
    wd_beside.wait_recv()

    act, du, da2, dact = b["act"], b["du"], b["da2"], b["dact"]
    up = wu[...].reshape(WIDTH, HIDDEN)
    down = wd[...].reshape(HIDDEN, WIDTH)
    start, go, end = square_sum(here, lambda cc, at: da2.at[cc * 4 + at], b["e2"], b["da2_sum"])
    shape = (2, ROWS, HIDDEN)

    def feed(i):
        at = here.corners[i]
        u = dot(flat(a2[:, at]), up)
        half_erf = 0.5 + 0.5 * lax.erf(u * (0.5**0.5))
        act[:, at] = (u * half_erf).astype(LOW).reshape(shape)
        slope = half_erf + u * jnp.exp(-0.5 * u * u) * (1.0 / math.sqrt(2.0 * math.pi))
        grad = (flat(dact[:, at]) * slope).astype(LOW)
        du[:, at] = grad.reshape(shape)
        grad = dot_nt(grad, up).astype(LOW)
        for cc in range(2):
            da2[cc * 4 + at] = grad[cc * ROWS : (cc + 1) * ROWS]

    for i in range(4):
        dz_got(i)
    dact[...] = dot_nt(flat(dz[...]), down).reshape(dact.shape)
    a2_got(0)
    feed(0)
    start(0)
    a2_got(1)
    feed(1)
    start(1)
    a2_last()
    a2_got(2)
    feed(2)
    start(2)
    go(1)
    a2_got(3)
    feed(3)
    start(3)
    go(2)
    go(3)
    ffn = b["ffn"]
    f_start, f_go, f_end = square_sum(here, lambda cc, at: ffn.at[cc * 4 + at], b["block"], b["ffn_sum"])
    raw_sent()
    ffn[...] = dot(flat(act[...]), down).astype(LOW).reshape(ffn.shape)
    for i in range(4):
        f_start(i)
    gd = b["gd"]
    gd[...] = dot_tn(flat(act[...]), flat(dz[...])).astype(LOW).reshape(gd.shape)
    gd_step = pair_sum(here, gd, b["gd_total"], b["gd_sum"], ends)
    next(gd_step)
    gu = b["gu"]
    gu[...] = dot_tn(flat(a2[...]), flat(du[...])).astype(LOW).reshape(gu.shape)
    gu_step = pair_sum(here, gu, b["gu_total"], b["gu_sum"], ends)
    next(gu_step)
    go(0)
    end()

    e2, n2 = b["e2"][...], b["n2"][...]
    dh1 = centre_back(e2, n2, b["r2"][:, :1], wide(norm, 2)) + dz[c, corner].astype(F32)
    b["dh1"][...] = dh1
    low = dh1.astype(LOW)
    do_mine, do_all = b["do_mine"], b["do_all"]
    for k in range(SHARDS):
        do_mine[k] = dot_nt(low, wo[k].reshape(ROWS, WIDTH)).astype(LOW)
    do_step = plane_trade(here, do_mine, do_all, b["do_sems"], ends)
    next(do_step)
    go_part = b["go"]
    go_part[...] = dot_tn(attended, low).astype(LOW).reshape(go_part.shape)
    go_step = cross_sum(here, go_part, b["go_total"], b["go_sum"], ends)
    next(go_step)
    next(go_step)
    run(do_step)
    next(gd_step)
    for i in range(1, 4):
        f_go(i)
    f_go(0)

    gk, gv, dqkv = b["gk"], b["gv"], b["dqkv"]

    def back(zz, first):
        pair = pl.ds(zz * 2, 2)
        queries, outs = flat(qkv[pair, :, :LANES]), flat(do_all[pair])
        queries_t, outs_t = queries.T, outs.T
        grad_query, grad_key, grad_value = [], [], []
        for h in range(2):
            chance_low = flat(probs[h, pair])
            chance = chance_low.astype(F32)
            grad_chance = dot_nt(jnp.where(mine[h], outs, jnp.zeros_like(outs)), values)
            inner = jnp.sum(chance * grad_chance, -1, keepdims=True)
            grad_scores = (chance * (grad_chance - inner)).astype(LOW)
            lanes = slice(h * HEAD_DIM, (h + 1) * HEAD_DIM)
            grad_query.append(dot(grad_scores, keys))
            grad_key.append(dot(queries_t[lanes], grad_scores))
            grad_value.append(dot(outs_t[lanes], chance_low))
        grad_query = jnp.where(mine[0], grad_query[0], grad_query[1]) * score_scale
        dqkv[pair, :, :LANES] = grad_query.astype(LOW).reshape(2, ROWS, LANES)
        grad_key, grad_value = jnp.concatenate(grad_key, 0), jnp.concatenate(grad_value, 0)
        if first:
            gk[...], gv[...] = grad_key, grad_value
        else:
            gk[...] += grad_key
            gv[...] += grad_value

    back(0, True)
    back(1, False)
    next(gu_step)
    back(2, False)
    back(3, False)
    thirds = (SHARDS, ROWS, LANES)
    dqkv[:, :, LANES : 2 * LANES] = (gk[...].T * score_scale).astype(LOW).reshape(thirds)
    dqkv[:, :, 2 * LANES :] = gv[...].T.astype(LOW).reshape(thirds)

    da1 = da2

    def spread(zz):
        pair = pl.ds(zz * 2, 2)
        da1[pair] = dot_nt(flat(dqkv[pair]), weight).astype(LOW).reshape(2, ROWS, WIDTH)

    da1_step = plane_sum(here, da1, b["e1"], b["da1_sum"], ends, spread)
    next(da1_step)
    gq = b["gq"]
    gq[...] = dot_tn(flat(a1[...]), flat(dqkv[...])).astype(LOW).reshape(gq.shape)
    gq_step = cross_sum(here, gq, b["gq_total"], b["gq_sum"], ends)
    next(gq_step)
    owner = here.y * 4 + c * 2 + half
    holder = x * 2 + here.near
    stays = (holder == g) & (owner == s)
    gd_away = remote(
        b["gd_total"], gd_land, b["gd_sems"][0].at[0], b["gd_sems"][1].at[0], (holder, owner)
    )
    gu_total = b["gu_total"]

    def store(i, src, dst):
        return pltpu.make_async_copy(src, dst, b["out_sems"].at[i])

    gd_stay = store(0, b["gd_total"], gd_land)
    gu_stay = store(1, gu_total.at[c, corner], gu_land.at[c, corner])
    gq_stay = store(2, b["gq_total"].at[s], gq_land.at[s])
    gu_send, gu_recv = b["gu_sems"]

    def gu_copy(k, i):
        core = here.g if k == 0 else here.sibling[0]
        cc = c if k == 0 else 1 - c
        return remote(
            gu_total.at[cc, here.corners[i]],
            gu_land.at[c, corner],
            gu_send.at[k, i],
            gu_recv.at[k, i],
            (core, here.square[i][1]),
        )

    def gu_came(k, i):
        cc = c if k == 0 else 1 - c
        block = gu_land.at[cc, here.corners[i]]
        return remote(block, block, gu_send.at[k, i], gu_recv.at[k, i], here.sibling)

    others = [(k, i) for k in range(2) for i in range(4) if (k, i) != (0, 0)]

    def send_gd():
        run(gd_step)

        @pl.when(stays)
        def _():
            gd_stay.start()

        @pl.when(jnp.logical_not(stays))
        def _():
            gd_away.start()

    def send_gu():
        run(gu_step)
        gu_stay.start()
        for k, i in others:
            gu_copy(k, i).start()

    go_out = spread_sum(here, b["go_total"], b["go_sum32"], b["go_plane"], ends)
    gq_out = plane_trade(here, b["gq_total"], gq_land, b["gq_sems"], ends, gq_stay)

    def send_go():
        run(go_step)
        next(go_out)

    def send_gq():
        run(gq_step)
        next(gq_out)

    send_gd()
    next(gq_step)
    next(da1_step)
    send_gu()
    send_go()
    next(da1_step)
    send_gq()
    next(da1_step)
    next(go_out)
    next(da1_step)
    run(da1_step)

    e1, n1 = b["e1"][...], b["n1"][...]
    count = jnp.sum(live_rows[pl.ds(s, 1), :].astype(F32), 1, keepdims=True)
    part = jnp.concatenate(
        [
            jnp.sum(e1 * n1, 0, keepdims=True),
            jnp.sum(e1, 0, keepdims=True),
            jnp.sum(e2 * n2, 0, keepdims=True),
            jnp.sum(e2, 0, keepdims=True),
            jnp.broadcast_to(count, (4, WIDTH)),
        ],
        0,
    )
    np_mine, np_land = b["np_mine"], b["np_land"]
    n_send, n_recv = b["np_sems"]
    me, everyone = g * SHARDS + s, GROUPS * SHARDS
    for k in range(SHARDS):
        np_mine[k] = part[:, k * LANES : (k + 1) * LANES]

    def np_copy(k):
        to = (me + k) % everyone
        return remote(
            np_mine.at[to // 4], np_land.at[k], n_send.at[0], n_recv.at[0], (to // SHARDS, to % SHARDS)
        )

    def np_start(k, carry):
        np_copy(k).start()
        return carry

    lax.fori_loop(1, everyone, np_start, 0)
    np_land[0] = np_mine[me // 4]
    b["dx"][...] = centre_back(e1, n1, b["r1"][:, :1], wide(norm, 0)) + b["dh1"][...]
    dx_store = store(3, b["dx"], input_grad)
    dx_store.start()

    f_end()
    b["block"][...] += b["h1"][...]
    block_store = store(4, b["block"], block_out)
    block_store.start()
    run(go_out)
    out_store = store(5, b["go_sum32"], out_sum)
    out_store.start()
    for k, i in others:
        gu_came(k, i).wait_recv()
    gu_stay.wait()
    run(gq_out)

    @pl.when(stays)
    def _():
        gd_stay.wait()

    @pl.when(jnp.logical_not(stays))
    def _():
        gd_away.wait_recv()
        gd_away.wait_send()

    all_came(here, np_land.at[pl.ds(1, everyone - 1)], b["np_sems"])
    total = jnp.sum(np_land[...], 0)
    norm_sum[...] = pltpu.roll(total, LANES - (s % 4) * 32, 1)
    all_sent(here, np_land.at[pl.ds(1, everyone - 1)], b["np_sems"])
    for copy in (dx_store, block_store, out_store):
        copy.wait()
    all_sent(here, norm.at[pl.ds(0, SHARDS - 1)], b["norm_sems"])
    all_sent(here, wq.at[pl.ds(0, SHARDS - 1), g], b["wq_sems"])
    all_sent(here, wu.at[pl.ds(0, SHARDS - 1), x], b["wu_sems"])
    all_sent(here, o_all.at[pl.ds(0, SHARDS - 1)], b["o_sems"])
    for k, i in others:
        gu_copy(k, i).wait_send()
    for copy in (wq_beside, wd_far, wd_beside, wu_beside, *wq_core, *wo_core):
        copy.wait_send()
    for i in range(SHARDS):
        wo_beside(i, g).wait_send()
    for finish in ends:
        finish()


KERNEL_VMEM = 57 * 2**20
SIZES = ((32, 3 * WIDTH), (32, WIDTH), (32, 4 * WIDTH), (ROWS, WIDTH))
SUMS = (
    (LOW, (SHARDS, 32, 3 * LANES)),
    (F32, (32, WIDTH)),
    (LOW, (2, 4, 32, HIDDEN)),
    (LOW, (ROWS, WIDTH)),
)
KINDS = (F32, F32, F32, F32, LOW)
CHUNKS = ((1, 0, 32), (2, 0, 32), (0, 0, 32), (3, 0, ROWS))
AHEAD = 4


def pieces(i):
    if i == 0:
        return [
            (k * WIDTH + j * LANES, LANES, (j,), k * LANES) for j in range(SHARDS) for k in range(3)
        ]
    if i == 2:
        return [
            ((j * 4 + at) * HIDDEN + cc * 256, 256, (cc, at), j * 256)
            for cc in range(2)
            for at in range(4)
            for j in range(2)
        ]
    return [(first, 256, (), first) for first in range(0, WIDTH, 256)]


def adamw_kernel(rates, *refs):
    refs = list(refs)

    def take(n):
        got = refs[:n]
        del refs[:n]
        return got

    norm_sum, *norm_old = take(4)
    sums, olds, passed = take(4), [take(3) for _ in SIZES], take(2)
    norm_new = take(5)
    news, handed = [take(5) for _ in SIZES], take(2)
    held_sum, held_old, held_out = take(4), [take(3) for _ in SIZES], [take(5) for _ in SIZES]
    held_pass = take(2)
    sum_sem, in_sem, out_sem, pass_sem = take(4)
    sum_loads = [pltpu.make_async_copy(sums[i], held_sum[i], sum_sem.at[i]) for i in range(4)]
    loads, stores = [], []
    for n, (i, first, rows) in enumerate(CHUNKS):
        at = pl.ds(first, rows)
        loads.append(
            [
                pltpu.make_async_copy(src.at[at, :], dst.at[at, :], in_sem.at[n, j])
                for j, (src, dst) in enumerate(zip(olds[i], held_old[i]))
            ]
        )
        stores.append(
            [
                pltpu.make_async_copy(src.at[at, :], dst.at[at, :], out_sem.at[n, j])
                for j, (src, dst) in enumerate(zip(held_out[i], news[i]))
            ]
        )
    passes = [pltpu.make_async_copy(passed[i], held_pass[i], pass_sem.at[i]) for i in range(2)]
    hands = [pltpu.make_async_copy(held_pass[i], handed[i], pass_sem.at[2 + i]) for i in range(2)]

    def load(n):
        if n < len(CHUNKS):
            i, first, _ = CHUNKS[n]
            if first == 0:
                sum_loads[i].start()
            for copy in loads[n]:
                copy.start()

    for n in range(AHEAD):
        load(n)
    count = norm_sum[4:5, 0:1]
    results = adamw(norm_sum[0:4, 0:32], count, *[ref[...] for ref in norm_old], rates[4], 0.0)
    for ref, value in zip(norm_new, results):
        ref[...] = value
    inverse = 1.0 / count
    for n, (i, top, rows) in enumerate(CHUNKS):
        if top == 0:
            sum_loads[i].wait()
        for copy in loads[n]:
            copy.wait()
        load(n + AHEAD)
        if n + AHEAD == len(CHUNKS):
            for copy in passes:
                copy.start()
        step = min(rows, 32)

        def some(k, carry):
            at = pl.ds(pl.multiple_of(top + k * step, step), step)
            for first, width, index, start in pieces(i):
                lanes = slice(first, first + width)
                summed = held_sum[i][(*index, at, slice(start, start + width))].astype(F32) * inverse
                old = [ref[at, lanes] for ref in held_old[i]]
                results = adamw(summed, 1.0, *old, rates[i], 0.1)
                for ref, value in zip(held_out[i], results):
                    ref[at, lanes] = value
            return carry

        lax.fori_loop(0, rows // step, some, 0)
        for copy in stores[n]:
            copy.start()
    for k in range(2):
        passes[k].wait()
        hands[k].start()
    for copies in stores:
        for copy in copies:
            copy.wait()
    for copy in hands:
        copy.wait()


def shaped(kind, *shape):
    return jax.ShapeDtypeStruct(shape, kind)


def call_adamw(rates, norms, sums, olds, passed):
    return pl.pallas_call(
        functools.partial(adamw_kernel, rates),
        out_shape=[shaped(kind, *norms[1].shape) for kind in KINDS]
        + [shaped(kind, *size) for size in SIZES for kind in KINDS]
        + [shaped(F32, ROWS, WIDTH)] * 2,
        in_specs=[VMEM] * 4 + [ANY] * 18,
        out_specs=[VMEM] * 5 + [ANY] * 22,
        scratch_shapes=[buffer(kind, *shape) for kind, shape in SUMS]
        + [buffer(F32, *size) for size in SIZES for _ in range(3)]
        + [buffer(kind, *size) for size in SIZES for kind in KINDS]
        + [buffer(F32, ROWS, WIDTH)] * 2
        + [DMA((4,)), DMA((len(CHUNKS), 3)), DMA((len(CHUNKS), 5)), DMA((4,))],
        compiler_params=pltpu.CompilerParams(vmem_limit_bytes=KERNEL_VMEM),
    )(*norms, *sums, *olds, *passed)


def fast_body(
    tokens, cotangent, item_ids, live_mask, qkv_weight, out_weight, up_weight, down_weight, norm_weight,
    qkv_master, qkv_first, qkv_second, out_master, out_first, out_second, up_master, up_first, up_second,
    down_master, down_first, down_second, norm_master, norm_first, norm_second,
):
    rows = item_ids.shape[0]
    args = (
        tokens,
        cotangent,
        item_ids.reshape(SHARDS, ROWS),
        live_mask.reshape(SHARDS, ROWS),
        norm_weight,
        qkv_weight,
        out_weight,
        up_weight,
        down_weight,
    )
    scratch = []
    for kind in scratch_plan().values():
        scratch += kind if isinstance(kind, list) else [kind]
    block_out, input_grad, qkv_sum, up_sum, out_sum, down_sum, norm_sum = pl.pallas_call(
        step_kernel,
        out_shape=[
            shaped(F32, ROWS, WIDTH),
            shaped(F32, ROWS, WIDTH),
            shaped(LOW, SHARDS, 32, 3 * LANES),
            shaped(LOW, 2, 4, 32, HIDDEN),
            shaped(F32, 32, WIDTH),
            shaped(LOW, ROWS, WIDTH),
            shaped(F32, 8, LANES),
        ],
        in_specs=[VMEM] * 5 + [ANY] * 4,
        out_specs=[ANY] * 6 + [VMEM],
        scratch_shapes=scratch,
        compiler_params=pltpu.CompilerParams(
            collective_id=0, has_side_effects=True, vmem_limit_bytes=KERNEL_VMEM
        ),
    )(*args)
    model_width, hidden = tokens.shape[1], up_weight.shape[1]
    rates = (
        model_width ** (-0.5),
        math.sqrt(rows) / 64,
        model_width ** (-0.5),
        hidden ** (-0.5),
        0.4,
    )
    news = call_adamw(
        rates,
        (norm_sum, norm_master, norm_first, norm_second),
        (qkv_sum, out_sum, up_sum, down_sum),
        (
            qkv_master, qkv_first, qkv_second, out_master, out_first, out_second,
            up_master, up_first, up_second, down_master, down_first, down_second,
        ),
        (block_out, input_grad),
    )
    return (*news[25:], *news[5:25], *news[:5])


def suits(mesh):
    return mesh.shape["grp"] == GROUPS and mesh.shape["shard"] == SHARDS


def solution(mesh):
    placed = (
        P(("grp", "shard"), None),
        P(("grp", "shard"), None),
        P("grp"),
        P("grp"),
        P("shard", None),
        P("shard", None),
        P("shard", None),
        P("shard", None),
        P(None, "shard"),
        P(("grp", "shard"), None),
        P(("grp", "shard"), None),
        P(("grp", "shard"), None),
        P(("grp", "shard"), None),
        P(("grp", "shard"), None),
        P(("grp", "shard"), None),
        P(("grp", "shard"), None),
        P(("grp", "shard"), None),
        P(("grp", "shard"), None),
        P(("grp", "shard"), None),
        P(("grp", "shard"), None),
        P(("grp", "shard"), None),
        P(None, ("grp", "shard")),
        P(None, ("grp", "shard")),
        P(None, ("grp", "shard")),
    )
    return jax.shard_map(
        fast_body if suits(mesh) else body,
        mesh=mesh,
        in_specs=placed,
        out_specs=(
            P(("grp", "shard"), None),
            P(("grp", "shard"), None),
            P(("grp", "shard"), None),
            P(("grp", "shard"), None),
            P(("grp", "shard"), None),
            P(("grp", "shard"), None),
            P(("grp", "shard"), None),
            P(("grp", "shard"), None),
            P(("grp", "shard"), None),
            P(("grp", "shard"), None),
            P(("grp", "shard"), None),
            P(("grp", "shard"), None),
            P(("grp", "shard"), None),
            P(("grp", "shard"), None),
            P(("grp", "shard"), None),
            P(("grp", "shard"), None),
            P(("grp", "shard"), None),
            P(("grp", "shard"), None),
            P(("grp", "shard"), None),
            P(("grp", "shard"), None),
            P(("grp", "shard"), None),
            P(("grp", "shard"), None),
            P(None, ("grp", "shard")),
            P(None, ("grp", "shard")),
            P(None, ("grp", "shard")),
            P(None, ("grp", "shard")),
            P(None, ("grp", "shard")),
        ),
        check_vma=False,
    )
```

```python
import functools
import math

import jax
import jax.numpy as jnp
from jax import lax
from jax.experimental import pallas as pl
from jax.experimental.pallas import tpu as pltpu
from jax.sharding import PartitionSpec as P

HEADS = 16
HEAD_DIM = 64
STEP = 5


eps_norm = 1e-06
score_scale = 0.125


def exact_gelu(inputs):
    return jax.nn.gelu(inputs, approximate=False)


def outer_sum(left, right):
    return lax.dot_general(
        left, right, (((0,), (0,)), ((), ())), preferred_element_type=jnp.float32
    )


def back_dot(gradient, weight):
    return lax.dot_general(
        gradient, weight, (((1,), (1,)), ((), ())), preferred_element_type=jnp.float32
    )


def norm_forward(values, gain, shift):
    mean = jnp.mean(values, -1, keepdims=True)
    centred = values - mean
    variance = jnp.mean(centred * centred, -1, keepdims=True)
    inverse = lax.rsqrt(variance + eps_norm)
    normed = centred * inverse
    return (normed * gain + shift, normed, inverse)


def norm_backward(upstream, normed, inverse, gain):
    scaled = upstream * gain
    mean_one = jnp.mean(scaled, -1, keepdims=True)
    mean_two = jnp.mean(scaled * normed, -1, keepdims=True)
    return (
        inverse * (scaled - mean_one - normed * mean_two),
        jnp.sum(upstream * normed, 0),
        jnp.sum(upstream, 0),
    )


def block_scores(queries, query_items, key_heads, key_items, key_live):
    scores = (
        jnp.einsum("qhd,khd->qhk", queries, key_heads, preferred_element_type=jnp.float32)
        * score_scale
    )
    allowed = (query_items[:, None] == key_items[None, :]) & (key_live[None, :] > 0)
    return (scores, allowed[:, None, :])


def score_grads(
    queries, query_items, grad_out, log_total, grad_dot, key_heads, value_heads, key_items, key_live
):
    scores, allowed = block_scores(queries, query_items, key_heads, key_items, key_live)
    attention = jnp.where(allowed, jnp.exp(scores - log_total[..., None]), 0.0)
    grad_attention = jnp.einsum(
        "qhd,khd->qhk", grad_out, value_heads, preferred_element_type=jnp.float32
    )
    grad_scores = (attention * (grad_attention - grad_dot[..., None])).astype(jnp.bfloat16)
    return (grad_scores, attention.astype(jnp.bfloat16))


def key_terms(grad_scores, attention_low, queries, grad_out):
    grad_key = (
        jnp.einsum("qhk,qhd->khd", grad_scores, queries, preferred_element_type=jnp.float32)
        * score_scale
    )
    grad_value = jnp.einsum(
        "qhk,qhd->khd", attention_low, grad_out, preferred_element_type=jnp.float32
    )
    return (grad_key, grad_value)


def query_term(grad_scores, key_heads):
    return (
        jnp.einsum("qhk,khd->qhd", grad_scores, key_heads, preferred_element_type=jnp.float32)
        * score_scale
    )


def key_blocks(shard_piece, item_ids, live_mask):
    piece_rows = shard_piece.shape[0]
    block_rows = math.gcd(piece_rows, 512)
    block_count = piece_rows // block_rows
    heads = shard_piece.reshape(block_count, block_rows, 2, HEADS, HEAD_DIM)
    key_items = item_ids.reshape(block_count, block_rows)
    key_live = live_mask.reshape(block_count, block_rows)
    return (heads[:, :, 0], heads[:, :, 1], key_items, key_live, block_rows)


def attend_fold(queries, query_items, item_ids, live_mask, carried, shard_piece):
    key_heads, value_heads, key_items, key_live, block_rows = key_blocks(
        shard_piece, item_ids, live_mask
    )

    def attend_advance(running, current):
        running_max, running_sum, weighted_sum = running
        key_block, value_block, item_block, live_block = current
        scores, allowed = block_scores(queries, query_items, key_block, item_block, live_block)
        new_max = jnp.maximum(running_max, jnp.max(jnp.where(allowed, scores, -1e30), -1))
        attention = jnp.where(allowed, jnp.exp(scores - new_max[..., None]), 0.0)
        factor = jnp.exp(running_max - new_max)
        running_sum = running_sum * factor + jnp.sum(attention, -1)
        weighted_sum = weighted_sum * factor[..., None] + jnp.einsum(
            "qhk,khd->qhd",
            attention.astype(jnp.bfloat16),
            value_block,
            preferred_element_type=jnp.float32,
        )
        return ((new_max, running_sum, weighted_sum), None)

    carried, _ = lax.scan(attend_advance, carried, (key_heads, value_heads, key_items, key_live))
    return carried


def summed_fold(queries, query_items, grad_out, log_total, grad_dot, item_ids, live_mask):

    def fold_keys(carried, shard_piece, first_row):
        grad_query, grad_pairs = carried
        key_heads, value_heads, key_items, key_live, block_rows = key_blocks(
            shard_piece, item_ids, live_mask
        )

        def fold_advance(running, current):
            key_block, value_block, item_block, live_block = current
            grad_scores, attention_low = score_grads(
                queries,
                query_items,
                grad_out,
                log_total,
                grad_dot,
                key_block,
                value_block,
                item_block,
                live_block,
            )
            grad_key, grad_value = key_terms(grad_scores, attention_low, queries, grad_out)
            paired = jnp.concatenate(
                [grad_key.reshape(block_rows, -1), grad_value.reshape(block_rows, -1)], 1
            )
            return (running + query_term(grad_scores, key_block), paired)

        grad_query, pieces = lax.scan(
            fold_advance, grad_query, (key_heads, value_heads, key_items, key_live)
        )
        grad_pairs = pieces.reshape(shard_piece.shape[0], -1)
        return (grad_query, grad_pairs)

    return fold_keys


def adamw(summed, live_total, master, old_first, old_second, step_rate, shrink):
    gradient = summed / live_total
    moment = 0.5 * old_first + 0.5 * gradient
    square = 0.5 * old_second + 0.5 * gradient * gradient
    correction = 1.0 - 0.5**STEP
    updated = master - step_rate * (
        moment / correction / (jnp.sqrt(square / correction) + 1e-08) + shrink * master
    )
    return (gradient, moment, square, updated, updated.astype(jnp.bfloat16))


def body(
    tokens,
    cotangent,
    item_ids,
    live_mask,
    qkv_weight,
    out_weight,
    up_weight,
    down_weight,
    norm_weight,
    qkv_master,
    qkv_first,
    qkv_second,
    out_master,
    out_first,
    out_second,
    up_master,
    up_first,
    up_second,
    down_master,
    down_first,
    down_second,
    norm_master,
    norm_first,
    norm_second,
):
    local_rows = tokens.shape[0]
    model_width = tokens.shape[1]
    group_rows = item_ids.shape[0]
    offset = lax.axis_index("shard") * local_rows
    qkv_full, out_full, up_full, down_full, norm_full = (
        lax.all_gather(qkv_weight, "shard", axis=0, tiled=True),
        lax.all_gather(out_weight, "shard", axis=0, tiled=True),
        lax.all_gather(up_weight, "shard", axis=0, tiled=True),
        lax.all_gather(down_weight, "shard", axis=0, tiled=True),
        lax.all_gather(norm_weight, "shard", axis=1, tiled=True),
    )
    hidden = up_full.shape[1]
    norm_values = norm_full.astype(jnp.float32)
    live_rows = lax.dynamic_slice_in_dim(live_mask, offset, local_rows)
    query_items = lax.dynamic_slice_in_dim(item_ids, offset, local_rows)
    group_count = jnp.sum(live_mask).astype(jnp.float32)
    total_count = lax.psum(group_count, "grp")
    inputs = tokens.astype(jnp.float32)
    first_norm, normed_one, inverse_one = norm_forward(inputs, norm_values[0], norm_values[1])
    first_low = first_norm.astype(jnp.bfloat16)
    projected = jnp.dot(first_low, qkv_full, preferred_element_type=jnp.float32).astype(
        jnp.bfloat16
    )
    query_flat = projected[:, :model_width]
    queries = query_flat.reshape(local_rows, HEADS, HEAD_DIM)
    key_values = projected[:, model_width:]
    start_state = (
        jnp.full((local_rows, HEADS), -1e30, jnp.float32),
        jnp.zeros((local_rows, HEADS), jnp.float32),
        jnp.zeros((local_rows, HEADS, HEAD_DIM), jnp.float32),
    )
    running_max, running_sum, weighted_sum = attend_fold(
        queries,
        query_items,
        item_ids,
        live_mask,
        start_state,
        lax.all_gather(key_values, "shard", axis=0, tiled=True),
    )
    attended = weighted_sum / running_sum[..., None]
    log_total = running_max + jnp.log(running_sum)
    attended_low = attended.reshape(local_rows, model_width).astype(jnp.bfloat16)
    mixed = inputs + jnp.dot(attended_low, out_full, preferred_element_type=jnp.float32)
    second_norm, normed_two, inverse_two = norm_forward(mixed, norm_values[2], norm_values[3])
    second_low = second_norm.astype(jnp.bfloat16)
    expanded = jnp.dot(second_low, up_full, preferred_element_type=jnp.float32)
    activated, gelu_pull = jax.vjp(exact_gelu, expanded)
    activated_low = activated.astype(jnp.bfloat16)
    block_out = mixed + jnp.dot(activated_low, down_full, preferred_element_type=jnp.float32)
    upstream = cotangent.astype(jnp.float32) * live_rows.astype(jnp.float32)[:, None]
    upstream_low = upstream.astype(jnp.bfloat16)
    down_term = outer_sum(activated_low, upstream_low)
    (grad_expanded,) = gelu_pull(back_dot(upstream_low, down_full))
    expanded_low = grad_expanded.astype(jnp.bfloat16)
    up_term = outer_sum(second_low, expanded_low)
    grad_mixed, gain_two, shift_two = norm_backward(
        back_dot(expanded_low, up_full), normed_two, inverse_two, norm_values[2]
    )
    grad_mixed = grad_mixed + upstream
    mixed_low = grad_mixed.astype(jnp.bfloat16)
    out_term = outer_sum(attended_low, mixed_low)
    grad_flat = back_dot(mixed_low, out_full).astype(jnp.bfloat16)
    grad_attended = grad_flat.reshape(local_rows, HEADS, HEAD_DIM)
    grad_dot = jnp.sum(grad_attended.astype(jnp.float32) * attended, -1)
    zero_query = jnp.zeros((local_rows, HEADS, HEAD_DIM), jnp.float32)
    fold_back = summed_fold(
        queries, query_items, grad_attended, log_total, grad_dot, item_ids, live_mask
    )
    start_back = (zero_query, jnp.zeros((group_rows, 2 * model_width), jnp.float32))
    folded = fold_back(
        start_back, lax.all_gather(key_values, "shard", axis=0, tiled=True), jnp.int32(0)
    )
    grad_query, grad_pairs = folded
    grad_kv = lax.psum_scatter(
        grad_pairs.astype(jnp.bfloat16), "shard", scatter_dimension=0, tiled=True
    ).astype(jnp.float32)
    grad_projected = jnp.concatenate(
        [grad_query.reshape(local_rows, model_width), grad_kv], 1
    ).astype(jnp.bfloat16)
    qkv_term = outer_sum(first_low, grad_projected)
    grad_first, gain_one, shift_one = norm_backward(
        back_dot(grad_projected, qkv_full), normed_one, inverse_one, norm_values[0]
    )
    input_grad = grad_first + grad_mixed
    norm_term = jnp.stack([gain_one, shift_one, gain_two, shift_two])
    qkv_sum, out_sum, up_sum, down_sum, norm_sum = (
        lax.psum_scatter(qkv_term, ("grp", "shard"), scatter_dimension=0, tiled=True),
        lax.psum_scatter(out_term, ("grp", "shard"), scatter_dimension=0, tiled=True),
        lax.psum_scatter(up_term, ("grp", "shard"), scatter_dimension=0, tiled=True),
        lax.psum_scatter(down_term, ("grp", "shard"), scatter_dimension=0, tiled=True),
        lax.psum_scatter(norm_term, ("grp", "shard"), scatter_dimension=1, tiled=True),
    )
    qkv_grad, qkv_moment, qkv_square, qkv_fresh, qkv_copy = adamw(
        qkv_sum, total_count, qkv_master, qkv_first, qkv_second, model_width ** (-0.5), 0.1
    )
    out_grad, out_moment, out_square, out_fresh, out_copy = adamw(
        out_sum, total_count, out_master, out_first, out_second, math.sqrt(group_rows) / 64, 0.1
    )
    up_grad, up_moment, up_square, up_fresh, up_copy = adamw(
        up_sum, total_count, up_master, up_first, up_second, model_width ** (-0.5), 0.1
    )
    down_grad, down_moment, down_square, down_fresh, down_copy = adamw(
        down_sum, total_count, down_master, down_first, down_second, hidden ** (-0.5), 0.1
    )
    norm_grad, norm_moment, norm_square, norm_fresh, norm_copy = adamw(
        norm_sum, total_count, norm_master, norm_first, norm_second, 0.4, 0.0
    )
    return (
        block_out,
        input_grad,
        qkv_grad,
        qkv_moment,
        qkv_square,
        qkv_fresh,
        qkv_copy,
        out_grad,
        out_moment,
        out_square,
        out_fresh,
        out_copy,
        up_grad,
        up_moment,
        up_square,
        up_fresh,
        up_copy,
        down_grad,
        down_moment,
        down_square,
        down_fresh,
        down_copy,
        norm_grad,
        norm_moment,
        norm_square,
        norm_fresh,
        norm_copy,
    )


MESH = pl.DeviceIdType.MESH
F32, LOW = jnp.float32, jnp.bfloat16
VMEM = pl.BlockSpec(memory_space=pltpu.VMEM)
ANY = pl.BlockSpec(memory_space=pltpu.HBM)
SHARDS, GROUPS = 8, 4
WIDTH, ROWS, LANES = 1024, 128, 128
HIDDEN = 512
DMA = pltpu.SemaphoreType.DMA


class Place:
    def __init__(self):
        self.g, self.s = lax.axis_index("grp"), lax.axis_index("shard")
        self.z, self.y = self.s // 2, self.s % 2
        self.x, self.c = self.g // 2, self.g % 2
        self.half, self.near = self.z // 2, self.z % 2
        self.corner = self.near * 2 + self.y
        g, s = self.g, self.s
        over = 1 - 2 * self.y
        along = 2 - 4 * self.near
        self.across = (g, s + over)
        self.up = (g, s + 2)
        self.down = (g, s - 2)
        self.far = (g, (s + 4) % SHARDS)
        self.sibling = (g + 1 - 2 * self.c, s)
        self.beside = ((g + 2) % GROUPS, s)
        self.square = [(g, s), self.across, (g, s + along), (g, s + along + over)]
        self.corners = [
            self.corner,
            self.corner + over,
            (self.corner + 2) % 4,
            (self.corner + over + 2) % 4,
        ]

    def at_shard(self, k):
        return (self.g, (self.s + k) % SHARDS)


def remote(src, dst, send, recv, device):
    return pltpu.make_async_remote_copy(
        src_ref=src, dst_ref=dst, send_sem=send, recv_sem=recv, device_id=device, device_id_type=MESH
    )


def greet_all(here):
    barrier = pltpu.get_barrier_semaphore()
    me, everyone = here.g * SHARDS + here.s, GROUPS * SHARDS

    def greet(k, carry):
        other = (me + k) % everyone
        pl.semaphore_signal(
            barrier, inc=1, device_id=(other // SHARDS, other % SHARDS), device_id_type=MESH
        )
        return carry

    lax.fori_loop(1, everyone, greet, 0)
    pl.semaphore_wait(barrier, everyone - 1)


def flat(value):
    return value.reshape(-1, value.shape[-1])


def dot(left, right):
    return lax.dot_general(left, right, (((1,), (0,)), ((), ())), preferred_element_type=F32)


def dot_nt(left, right):
    return lax.dot_general(left, right, (((1,), (1,)), ((), ())), preferred_element_type=F32)


def dot_tn(left, right):
    return lax.dot_general(left, right, (((0,), (0,)), ((), ())), preferred_element_type=F32)


def run(*steps):
    for step in steps:
        for _ in step:
            pass


def buffer(kind, *shape):
    return pltpu.VMEM(shape, kind)


def gather_sems():
    return [DMA((3, 4)), DMA((SHARDS,))]


def plane_gather(here, block, sems, ends, came=None):
    send, recv = sems
    z, y = here.z, here.y

    def copy(lane, zz, yy):
        device = (here.across, here.up, here.down)[lane]
        i = zz * 2 + yy
        return remote(block(i), block(i), send.at[lane, zz], recv.at[i], device)

    def arrived(zz, yy):
        copy(0, zz, yy).wait_recv()
        if came is not None:
            came(zz * 2 + yy)

    def finish():
        for zz in range(4):
            copy(0, zz, y).wait_send()

            @pl.when((zz <= z) & (z < 3))
            def _():
                copy(1, zz, y).wait_send()

            @pl.when((zz >= z) & (z > 0))
            def _():
                copy(2, zz, y).wait_send()

    ends.append(finish)

    @pl.when(z < 3)
    def _():
        copy(1, z, y).start()

    @pl.when(z > 0)
    def _():
        copy(2, z, y).start()

    copy(0, z, y).start()
    if came is not None:
        came(z * 2 + y)
    yield
    for step in range(1, 4):

        @pl.when(z >= step)
        def _():
            zz = z - step
            arrived(zz, y)

            @pl.when(z < 3)
            def _():
                copy(1, zz, y).start()

            copy(0, zz, y).start()

        @pl.when(z + step <= 3)
        def _():
            zz = z + step
            arrived(zz, y)

            @pl.when(z > 0)
            def _():
                copy(2, zz, y).start()

            copy(0, zz, y).start()

        yield
    for zz in range(4):
        arrived(zz, 1 - y)
    yield


def sum_scratch(rows):
    shape = (4, rows, WIDTH)
    return [buffer(LOW, *shape), buffer(LOW, *shape), buffer(LOW, 2, *shape)] + [DMA((4,))] * 3 + [DMA((2, 4))]


def plane_sum(here, part, total, scratch, ends, prepare=None):
    landed, ready, relayed, y_send, y_recv, z_send, z_recv = scratch
    z, y = here.z, here.y
    order = [
        jnp.where(z < 2, 3, 0),
        jnp.where(z % 3 == 0, jnp.where(z == 0, 2, 1), jnp.where(z == 1, 2, 1)),
        jnp.where(z % 3 == 0, jnp.where(z == 0, 1, 2), jnp.where(z == 1, 0, 3)),
        z,
    ]
    first = [
        remote(part.at[zz * 2 + 1 - y], landed.at[i], y_send.at[i], y_recv.at[i], here.across)
        for i, zz in enumerate(order)
    ]

    def relay(lane, zz):
        device = (here.up, here.down)[lane]
        return remote(ready.at[zz], relayed.at[lane, zz], z_send.at[zz], z_recv.at[lane, zz], device)

    for i, zz in enumerate(order):
        if prepare is not None:
            prepare(zz)
        first[i].start()
    yield
    for i, zz in enumerate(order):
        first[i].wait_recv()
        if i < 3:
            ready[zz] = (part[zz * 2 + y].astype(F32) + landed[i].astype(F32)).astype(LOW)

            @pl.when(zz > z)
            def _():
                @pl.when(z > 0)
                def _():
                    relay(0, zz).wait_recv()
                    ready[zz] = (ready[zz].astype(F32) + relayed[0, zz].astype(F32)).astype(LOW)

                relay(0, zz).start()

            @pl.when(zz < z)
            def _():
                @pl.when(z < 3)
                def _():
                    relay(1, zz).wait_recv()
                    ready[zz] = (ready[zz].astype(F32) + relayed[1, zz].astype(F32)).astype(LOW)

                relay(1, zz).start()

        else:
            total[...] = part[zz * 2 + y].astype(F32) + landed[i].astype(F32)
        yield

    @pl.when(z > 0)
    def _():
        relay(0, z).wait_recv()
        total[...] += relayed[0, z].astype(F32)

    @pl.when(z < 3)
    def _():
        relay(1, z).wait_recv()
        total[...] += relayed[1, z].astype(F32)

    def finish():
        for copy in first:
            copy.wait_send()
        for zz in order[:3]:
            relay(0, zz).wait_send()

    ends.append(finish)
    yield


def square_gather(here, held, sems, ends):
    send, recv, half_send, half_recv, sib_send, sib_recv = sems
    c = here.c
    cut = held.shape[2] // 2

    def part(at, k):
        return held.at[c, here.corners[at], pl.ds(k * cut, cut)]

    def copy(i, at, k):
        return remote(part(at, k), part(at, k), send.at[i - 1, k], recv.at[i - 1, k], here.square[i])

    def onward(i, at):
        block = part(at, i - 1)
        return remote(block, block, half_send.at[i - 1], half_recv.at[i - 1], here.square[3 - i])

    def pass_on(i):
        block = held.at[c, here.corners[i]]
        return remote(block, block, sib_send.at[i], sib_recv.at[i], here.sibling)

    def passed(i):
        block = held.at[1 - c, here.corners[i]]
        return remote(block, block, sib_send.at[i], sib_recv.at[i], here.sibling)

    def finish():
        for i in (1, 2):
            for k in range(2):
                copy(i, 0, k).wait_send()
            onward(i, i).wait_send()
        for i in range(4):
            pass_on(i).wait_send()

    ends.append(finish)

    def start():
        for k in range(2):
            for i in (1, 2):
                copy(i, 0, (i - 1 + k) % 2).start()
        pass_on(0).start()

    def relay():
        for i in (1, 2):
            copy(i, i, i - 1).wait_recv()
            onward(i, i).start()
        for i in (1, 2):
            copy(i, i, 2 - i).wait_recv()
            pass_on(i).start()

    def last():
        for i in (1, 2):
            onward(i, 3).wait_recv()
        pass_on(3).start()

    def got(i):
        passed(i).wait_recv()

    return start, relay, last, got


def square_sems():
    return [DMA((2, 2))] * 2 + [DMA((2,))] * 2 + [DMA((4,))] * 2


def square_scratch():
    shape = (4, ROWS, WIDTH)
    return [buffer(LOW, *shape)] * 3 + [DMA((4,))] * 4


def square_sum(here, part, total, scratch):
    landed, ready, final, sib_send, sib_recv, send, recv = scratch
    c = here.c

    def swap(i):
        return remote(
            part(1 - c, here.corners[i]), landed.at[i], sib_send.at[i], sib_recv.at[i], here.sibling
        )

    def ship(i):
        return remote(ready.at[i], final.at[i], send.at[i], recv.at[i], here.square[i])

    def start(i):
        swap(i).start()

    def go(i):
        swap(i).wait_recv()
        value = part(c, here.corners[i])[...].astype(F32) + landed[i].astype(F32)
        if i:
            ready[i] = value.astype(LOW)
            ship(i).start()
        else:
            total[...] = value

    def end():
        for i in range(1, 4):
            ship(i).wait_recv()
        total[...] += final[1].astype(F32) + final[2].astype(F32) + final[3].astype(F32)
        for i in range(4):
            swap(i).wait_send()
        for i in range(1, 4):
            ship(i).wait_send()

    return start, go, end


def cross_scratch(rows, cols):
    return [buffer(LOW, 2, rows, cols)] + [buffer(LOW, rows, cols)] * 2 + [DMA((2,))] * 2 + [DMA((1,))] * 2


def cross_sum(here, part, total, scratch, ends):
    landed, ready, final, c_send, c_recv, x_send, x_recv = scratch
    g, x, c = here.g, here.x, here.c
    first = [
        remote(part.at[xx * 2 + 1 - c], landed.at[xx], c_send.at[xx], c_recv.at[xx], here.sibling)
        for xx in range(2)
    ]
    second = remote(ready, final, x_send.at[0], x_recv.at[0], here.beside)
    for copy in first:
        copy.start()
    yield
    for copy in first:
        copy.wait_recv()
    ready[...] = (part[(1 - x) * 2 + c].astype(F32) + landed[1 - x].astype(F32)).astype(LOW)
    second.start()
    yield
    second.wait_recv()
    value = part[g].astype(F32) + landed[x].astype(F32) + final[...].astype(F32)
    total[...] = value.astype(total.dtype).reshape(total.shape)

    def finish():
        for copy in first + [second]:
            copy.wait_send()

    ends.append(finish)
    yield


def pair_scratch(rows, cols, parts=1):
    return [buffer(LOW, parts, 2, rows, cols)] + [buffer(LOW, parts, rows, cols)] * 2 + [DMA((1,))] * 4


def pair_sum(here, part, total, scratch, ends):
    landed, ready, final, x_send, x_recv, z_send, z_recv = scratch
    x, half = here.x, here.half
    first = remote(part.at[1 - x], landed, x_send.at[0], x_recv.at[0], here.beside)
    second = remote(ready, final, z_send.at[0], z_recv.at[0], here.far)
    first.start()
    yield
    first.wait_recv()
    ready[...] = (part[x, :, 1 - half].astype(F32) + landed[:, 1 - half].astype(F32)).astype(LOW)
    second.start()
    yield
    second.wait_recv()
    value = part[x, :, half].astype(F32) + landed[:, half].astype(F32) + final[...].astype(F32)
    total[...] = value.astype(LOW).reshape(total.shape)

    def finish():
        first.wait_send()
        second.wait_send()

    ends.append(finish)
    yield


def spread_scratch(rows):
    return [buffer(LOW, 4, rows, WIDTH)] * 3 + [DMA((1,))] * 2 + [DMA((4,))] * 2


def spread_sum(here, part, total, scratch, ends):
    landed, ready, final, y_send, y_recv, z_send, z_recv = scratch
    z, y = here.z, here.y
    first = remote(part.at[:, 1 - y], landed, y_send.at[0], y_recv.at[0], here.across)

    def second(k):
        to = (z + k) % 4
        return remote(ready.at[to], final.at[k], z_send.at[k], z_recv.at[k], (here.g, to * 2 + y))

    first.start()
    yield
    first.wait_recv()
    ready[...] = (part[:, y].astype(F32) + landed[...].astype(F32)).astype(LOW)
    for k in (2, 1, 3):
        second(k).start()
    yield
    value = ready[z].astype(F32)
    for k in range(1, 4):
        second(k).wait_recv()
        value += final[k].astype(F32)
    total[...] = value

    def finish():
        first.wait_send()
        for k in range(1, 4):
            second(k).wait_send()

    ends.append(finish)
    yield


def trade_sems():
    return [DMA((1,))] * 2


def all_sent(here, seven, sems):
    remote(seven, seven, sems[0].at[0], sems[1].at[0], here.across).wait_send()


def all_came(here, seven, sems):
    remote(seven, seven, sems[0].at[0], sems[1].at[0], here.across).wait_recv()


def plane_trade(here, mine, theirs, sems, ends, stay=None, prepare=None):
    send, recv = sems

    def copy(k):
        device = here.at_shard(k)
        return remote(mine.at[device[1]], theirs.at[here.s], send.at[0], recv.at[0], device)

    for k in range(1, SHARDS):
        if prepare is not None:
            prepare(here.at_shard(k)[1])
        copy(k).start()
    if prepare is not None:
        prepare(here.s)
    if stay is None:
        theirs[here.s] = mine[here.s]
    else:
        stay.start()
    yield
    all_came(here, theirs.at[pl.ds(0, SHARDS - 1)], sems)

    def finish():
        all_sent(here, mine.at[pl.ds(0, SHARDS - 1)], sems)
        if stay is not None:
            stay.wait()

    ends.append(finish)
    yield


def centre(values):
    mean = jnp.mean(values, -1, keepdims=True)
    centred = values - mean
    variance = jnp.mean(centred * centred, -1, keepdims=True)
    inverse = lax.rsqrt(variance + eps_norm)
    return centred * inverse, inverse


def centre_back(e, normed, inverse, gain):
    scaled = e * gain
    mean_one = jnp.mean(scaled, -1, keepdims=True)
    mean_two = jnp.mean(scaled * normed, -1, keepdims=True)
    return inverse * (scaled - mean_one - normed * mean_two)


def wide(norm, row):
    return jnp.concatenate([norm[j, row : row + 1, :] for j in range(SHARDS)], 1)


def column(row):
    return jnp.broadcast_to(row, (LANES, LANES)).T


def scratch_plan():
    plan = dict(
        own_norm=buffer(F32, 8, LANES),
        own_sems=DMA((SHARDS,)),
        norm=buffer(F32, SHARDS, 8, LANES),
        norm_sems=trade_sems(),
        wq=buffer(LOW, SHARDS, GROUPS, 32, 3 * LANES),
        wq_sems=trade_sems() + [DMA((3,))] * 2,
        wo=buffer(LOW, SHARDS, GROUPS, 32, WIDTH),
        wo_sems=gather_sems(),
        wo_more=[DMA((SHARDS + 2,))] * 2,
        wu=buffer(LOW, SHARDS, 2, 64, HIDDEN),
        wu_sems=trade_sems() + [DMA((1,))] * 2,
        wd=buffer(LOW, 2, 2, ROWS, WIDTH),
        wd_sems=[DMA((2,))] * 2,
        a1=buffer(LOW, SHARDS, ROWS, WIDTH),
        a1_sems=gather_sems(),
        a2=buffer(LOW, 2, 4, ROWS, WIDTH),
        a2_sems=square_sems(),
        dz=buffer(LOW, 2, 4, ROWS, WIDTH),
        dz_sems=square_sems(),
        qkv=buffer(LOW, SHARDS, ROWS, 3 * LANES),
        probs=buffer(LOW, 2, SHARDS, ROWS, WIDTH),
        o_mine=buffer(LOW, SHARDS, ROWS, LANES),
        o_all=buffer(LOW, SHARDS, ROWS, LANES),
        o_sems=trade_sems(),
        n1=buffer(F32, ROWS, WIDTH),
        r1=buffer(F32, ROWS, LANES),
        h1=buffer(F32, ROWS, WIDTH),
        n2=buffer(F32, ROWS, WIDTH),
        r2=buffer(F32, ROWS, LANES),
        act=buffer(LOW, 2, 4, ROWS, HIDDEN),
        du=buffer(LOW, 2, 4, ROWS, HIDDEN),
        dact=buffer(F32, 2, 4, ROWS, HIDDEN),
        da2=buffer(LOW, SHARDS, ROWS, WIDTH),
        da2_sum=square_scratch(),
        e2=buffer(F32, ROWS, WIDTH),
        ffn=buffer(LOW, SHARDS, ROWS, WIDTH),
        ffn_sum=square_scratch(),
        block=buffer(F32, ROWS, WIDTH),
        dh1=buffer(F32, ROWS, WIDTH),
        do_mine=buffer(LOW, SHARDS, ROWS, LANES),
        do_all=buffer(LOW, SHARDS, ROWS, LANES),
        do_sems=trade_sems(),
        gk=buffer(F32, LANES, WIDTH),
        gv=buffer(F32, LANES, WIDTH),
        dqkv=buffer(LOW, SHARDS, ROWS, 3 * LANES),
        da1_sum=sum_scratch(ROWS),
        e1=buffer(F32, ROWS, WIDTH),
        gd=buffer(LOW, 2, 1, 2, ROWS, WIDTH),
        gd_sum=pair_scratch(ROWS, WIDTH),
        gd_total=buffer(LOW, ROWS, WIDTH),
        gd_sems=[DMA((1,))] * 2,
        gu=buffer(LOW, 2, 2, 2, ROWS, HIDDEN),
        gu_sum=pair_scratch(ROWS, HIDDEN, 2),
        gu_total=buffer(LOW, 2, 4, 32, HIDDEN),
        gu_sems=[DMA((2, 4)), DMA((2, 4))],
        go=buffer(LOW, GROUPS, 256, WIDTH),
        go_sum=cross_scratch(256, WIDTH),
        go_total=buffer(LOW, 4, 2, 32, WIDTH),
        go_plane=spread_scratch(32),
        gq=buffer(LOW, GROUPS, 256, 3 * LANES),
        gq_sum=cross_scratch(256, 3 * LANES),
        gq_total=buffer(LOW, SHARDS, 32, 3 * LANES),
        gq_sems=trade_sems(),
        np_mine=buffer(F32, SHARDS, 8, LANES),
        np_land=buffer(F32, GROUPS * SHARDS, 8, LANES),
        np_sems=trade_sems(),
        go_sum32=buffer(F32, 32, WIDTH),
        dx=buffer(F32, ROWS, WIDTH),
        out_sems=DMA((6,)),
    )
    return plan


def step_kernel(*refs):
    plan = scratch_plan()
    inputs, refs = refs[:9], refs[9:]
    outputs, refs = refs[:7], list(refs[7:])
    tok, cot, item_rows, live_rows, norm_weight, wqkv, wout, wup, wdown = inputs
    block_out, input_grad, gq_land, gu_land, out_sum, gd_land, norm_sum = outputs
    b = {}
    for name, kind in plan.items():
        many = isinstance(kind, list)
        got = [refs.pop(0) for _ in range(len(kind) if many else 1)]
        b[name] = got if many else got[0]

    here = Place()
    g, s, x, c, z, y, half, corner = (
        here.g, here.s, here.x, here.c, here.z, here.y, here.half, here.corner
    )
    ends = []
    quarter = pl.ds(pl.multiple_of(g * 32, 32), 32)
    beside_g = here.beside[0]
    wq, wo, wu, wd = b["wq"], b["wo"], b["wu"], b["wd"]
    wu_rows = pl.ds(pl.multiple_of(x * 64, 64), 64)

    def wu_columns(shard, j):
        return pl.ds(pl.multiple_of((shard % 4 + j * 4) * HIDDEN + c * 256, 256), 256)

    own_pairs = [
        (
            wqkv.at[quarter, pl.ds(pl.multiple_of(j * WIDTH + s * LANES, LANES), LANES)],
            wq.at[s, g, :, pl.ds(j * LANES, LANES)],
        )
        for j in range(3)
    ]
    own_pairs.append((wout.at[quarter, :], wo.at[s, g]))
    own_pairs += [(wup.at[wu_rows, wu_columns(s, j)], wu.at[s, x, :, pl.ds(j * 256, 256)]) for j in range(2)]
    own_pairs += [
        (wdown.at[pl.ds(pl.multiple_of(c * 256 + j * ROWS, ROWS), ROWS), :], wd.at[half, j]) for j in range(2)
    ]
    own_copies = [pltpu.make_async_copy(*pair, b["own_sems"].at[i]) for i, pair in enumerate(own_pairs)]
    for copy in own_copies:
        copy.start()
    greet_all(here)

    norm, own_norm = b["norm"], b["own_norm"]
    own_norm[...] = jnp.zeros_like(own_norm)
    own_norm[0:4, :] = norm_weight[...].astype(F32)
    norm[s] = own_norm[...]

    def norm_copy(k):
        send, recv = b["norm_sems"]
        return remote(own_norm, norm.at[s], send.at[0], recv.at[0], here.at_shard(k))

    def wq_copies(k):
        device = here.at_shard(k)
        send, recv = b["wq_sems"][:2]
        return [
            remote(
                wqkv.at[quarter, pl.ds(pl.multiple_of(j * WIDTH + device[1] * LANES, LANES), LANES)],
                wq.at[s, g, :, pl.ds(j * LANES, LANES)],
                send.at[0],
                recv.at[0],
                device,
            )
            for j in range(3)
        ]

    for k in range(1, SHARDS):
        norm_copy(k).start()
    for k in range(1, SHARDS):
        for copy in wq_copies(k):
            copy.start()
    n1, inverse = centre(tok[...].astype(F32))
    b["n1"][...] = n1
    b["r1"][...] = jnp.broadcast_to(inverse, (ROWS, LANES))
    a1, raw = b["a1"], b["ffn"]
    raw[s] = n1.astype(LOW)
    a1_step = plane_gather(here, lambda i: raw.at[i], b["a1_sems"], ends)
    next(a1_step)
    raw_sent = ends.pop()

    own_copies[3].wait()
    wo_send, wo_recv = b["wo_more"]

    def wo_beside(i, k):
        block = wo.at[i, k]
        return remote(block, block, wo_send.at[i], wo_recv.at[i], here.beside)

    def wo_came(i):
        wo_beside(i, g).start()

    wo_step = plane_gather(here, lambda i: wo.at[i, g], b["wo_sems"], ends, wo_came)
    next(wo_step)
    wo_core = [
        remote(wo.at[:, k], wo.at[:, k], wo_send.at[SHARDS + i], wo_recv.at[SHARDS + i], here.sibling)
        for i, k in enumerate((g, beside_g))
    ]

    wd_send, wd_recv = b["wd_sems"]
    wd_rows = pl.ds(pl.multiple_of(c * 256 + x * ROWS, ROWS), ROWS)
    wd_far = remote(wdown.at[wd_rows, :], wd.at[half, x], wd_send.at[0], wd_recv.at[0], here.far)
    wd_beside = remote(
        wd.at[1 - half, x], wd.at[1 - half, x], wd_send.at[1], wd_recv.at[1], here.beside
    )

    wu_send, wu_recv, wu_xsend, wu_xrecv = b["wu_sems"]

    def wu_copies(k):
        device = here.at_shard(k)
        return [
            remote(
                wup.at[wu_rows, wu_columns(device[1], j)],
                wu.at[s, x, :, pl.ds(j * 256, 256)],
                wu_send.at[0],
                wu_recv.at[0],
                device,
            )
            for j in range(2)
        ]

    wu_beside = remote(wu.at[:, x], wu.at[:, x], wu_xsend.at[0], wu_xrecv.at[0], here.beside)

    dz = b["dz"]
    own_live = column(live_rows[pl.ds(s, 1), :].astype(F32))
    dz[c, corner] = (cot[...].astype(F32) * jnp.concatenate([own_live] * SHARDS, 1)).astype(LOW)
    all_came(here, wq.at[pl.ds(0, SHARDS - 1), g], b["wq_sems"])
    wq_send, wq_recv = b["wq_sems"][2:]
    wq_beside = remote(wq.at[:, g], wq.at[:, g], wq_send.at[0], wq_recv.at[0], here.beside)
    wq_core = [
        remote(wq.at[:, k], wq.at[:, k], wq_send.at[1 + i], wq_recv.at[1 + i], here.sibling)
        for i, k in enumerate((g, beside_g))
    ]
    for copy in own_copies[:3]:
        copy.wait()
    wq_beside.start()
    wq_core[0].start()
    next(a1_step)
    next(wo_step)
    next(a1_step)
    next(wo_step)
    wq_beside.wait_recv()
    wq_core[1].start()
    wd_far.start()
    next(a1_step)
    next(wo_step)
    for copy in own_copies[4:]:
        copy.wait()

    for copy in wq_core:
        copy.wait_recv()
    all_came(here, norm.at[pl.ds(0, SHARDS - 1)], b["norm_sems"])
    qkv, probs = b["qkv"], b["probs"]
    gain, shift, weight = wide(norm, 0), wide(norm, 1), flat(wq[...])

    def project(yy):
        rows = []
        for zz in range(4):
            value = (raw[zz * 2 + yy].astype(F32) * gain + shift).astype(LOW)
            a1[zz * 2 + yy] = value
            rows.append(value)
        out = dot(jnp.concatenate(rows, 0), weight).astype(LOW)
        for zz in range(4):
            qkv[zz * 2 + yy] = out[zz * ROWS : (zz + 1) * ROWS]

    project(y)
    run(a1_step)
    for k in range(1, SHARDS):
        for copy in wu_copies(k):
            copy.start()
    dz_start, dz_relay, dz_last, dz_got = square_gather(here, dz, b["dz_sems"], ends)
    project(1 - y)
    keys = flat(qkv[:, :, LANES : 2 * LANES])
    values = flat(qkv[:, :, 2 * LANES :])
    key_items = jnp.concatenate(
        [jnp.where(live_rows[j : j + 1, :] > 0, item_rows[j : j + 1, :], -1) for j in range(SHARDS)], 1
    )
    lane = lax.broadcasted_iota(jnp.int32, (2 * ROWS, LANES), 1)
    mine = [lane < HEAD_DIM, lane >= HEAD_DIM]
    o_mine, o_all = b["o_mine"], b["o_all"]

    def o_copy(to):
        send, recv = b["o_sems"]
        return remote(o_mine.at[to], o_all.at[s], send.at[0], recv.at[0], (g, to))

    def attend(zz):
        pair = pl.ds(zz * 2, 2)
        queries = flat(qkv[pair, :, :LANES])
        items = jnp.concatenate([column(item_rows[pl.ds(zz * 2 + j, 1), :]) for j in range(2)], 0)
        allowed = jnp.concatenate([items] * SHARDS, 1) == key_items
        outs = []
        for h in range(2):
            scores = dot_nt(jnp.where(mine[h], queries, jnp.zeros_like(queries)), keys) * score_scale
            scores = jnp.where(allowed, scores, -1e30)
            peak = jnp.max(scores, -1, keepdims=True)
            expo = jnp.exp(scores - peak)
            chance = (expo * (1.0 / jnp.sum(expo, -1, keepdims=True))).astype(LOW)
            probs[h, pair] = chance.reshape(2, ROWS, WIDTH)
            outs.append(dot(chance, values))
        o_mine[pair] = jnp.where(mine[0], outs[0], outs[1]).astype(LOW).reshape(2, ROWS, LANES)

    for step in range(1, 4):
        zz = (z + step) % 4
        attend(zz)
        for j in range(2):
            to = zz * 2 + j
            o_copy(to).start()
        if step == 1:
            run(wo_step)
            wo_core[0].start()
    attend(z)
    o_all[s] = o_mine[s]
    dz_start()
    o_copy(here.across[1]).start()
    for i in range(SHARDS):
        wo_beside(i, beside_g).wait_recv()
    wo_core[1].start()
    wd_far.wait_recv()
    wd_beside.start()
    all_came(here, wu.at[pl.ds(0, SHARDS - 1), x], b["wu_sems"])
    wu_beside.start()
    dz_relay()
    all_came(here, o_all.at[pl.ds(0, SHARDS - 1)], b["o_sems"])
    for copy in wo_core:
        copy.wait_recv()

    attended = jnp.concatenate([o_all[j] for j in range(SHARDS)], 1)
    h1 = tok[...].astype(F32) + dot(attended, wo[...].reshape(WIDTH, WIDTH))
    b["h1"][...] = h1
    n2, inverse = centre(h1)
    b["n2"][...] = n2
    b["r2"][...] = jnp.broadcast_to(inverse, (ROWS, LANES))
    a2 = b["a2"]
    a2[c, corner] = (n2 * wide(norm, 2) + wide(norm, 3)).astype(LOW)
    a2_start, a2_relay, a2_last, a2_got = square_gather(here, a2, b["a2_sems"], ends)
    a2_start()
    dz_last()
    a2_relay()
    wu_beside.wait_recv()
    wd_beside.wait_recv()

    act, du, da2, dact = b["act"], b["du"], b["da2"], b["dact"]
    up = wu[...].reshape(WIDTH, HIDDEN)
    down = wd[...].reshape(HIDDEN, WIDTH)
    start, go, end = square_sum(here, lambda cc, at: da2.at[cc * 4 + at], b["e2"], b["da2_sum"])
    shape = (2, ROWS, HIDDEN)

    def feed(i):
        at = here.corners[i]
        u = dot(flat(a2[:, at]), up)
        half_erf = 0.5 + 0.5 * lax.erf(u * (0.5**0.5))
        act[:, at] = (u * half_erf).astype(LOW).reshape(shape)
        slope = half_erf + u * jnp.exp(-0.5 * u * u) * (1.0 / math.sqrt(2.0 * math.pi))
        grad = (flat(dact[:, at]) * slope).astype(LOW)
        du[:, at] = grad.reshape(shape)
        grad = dot_nt(grad, up).astype(LOW)
        for cc in range(2):
            da2[cc * 4 + at] = grad[cc * ROWS : (cc + 1) * ROWS]

    for i in range(4):
        dz_got(i)
    dact[...] = dot_nt(flat(dz[...]), down).reshape(dact.shape)
    a2_got(0)
    feed(0)
    start(0)
    a2_got(1)
    feed(1)
    start(1)
    a2_last()
    a2_got(2)
    feed(2)
    start(2)
    go(1)
    a2_got(3)
    feed(3)
    start(3)
    go(2)
    go(3)
    ffn = b["ffn"]
    f_start, f_go, f_end = square_sum(here, lambda cc, at: ffn.at[cc * 4 + at], b["block"], b["ffn_sum"])
    raw_sent()
    ffn[...] = dot(flat(act[...]), down).astype(LOW).reshape(ffn.shape)
    for i in range(4):
        f_start(i)
    gd = b["gd"]
    gd[...] = dot_tn(flat(act[...]), flat(dz[...])).astype(LOW).reshape(gd.shape)
    gd_step = pair_sum(here, gd, b["gd_total"], b["gd_sum"], ends)
    next(gd_step)
    gu = b["gu"]
    gu[...] = dot_tn(flat(a2[...]), flat(du[...])).astype(LOW).reshape(gu.shape)
    gu_step = pair_sum(here, gu, b["gu_total"], b["gu_sum"], ends)
    next(gu_step)
    go(0)
    end()

    e2, n2 = b["e2"][...], b["n2"][...]
    dh1 = centre_back(e2, n2, b["r2"][:, :1], wide(norm, 2)) + dz[c, corner].astype(F32)
    b["dh1"][...] = dh1
    low = dh1.astype(LOW)
    do_mine, do_all = b["do_mine"], b["do_all"]

    def head_rows(to):
        do_mine[to] = dot_nt(low, wo[to].reshape(ROWS, WIDTH)).astype(LOW)

    do_step = plane_trade(here, do_mine, do_all, b["do_sems"], ends, prepare=head_rows)
    next(do_step)
    go_part = b["go"]
    go_part[...] = dot_tn(attended, low).astype(LOW).reshape(go_part.shape)
    go_step = cross_sum(here, go_part, b["go_total"], b["go_sum"], ends)
    next(go_step)
    next(go_step)
    run(do_step)
    for i in range(1, 4):
        f_go(i)
    f_go(0)
    next(gd_step)

    gk, gv, dqkv = b["gk"], b["gv"], b["dqkv"]

    def back(zz, first):
        pair = pl.ds(zz * 2, 2)
        queries, outs = flat(qkv[pair, :, :LANES]), flat(do_all[pair])
        queries_t, outs_t = queries.T, outs.T
        grad_query, grad_key, grad_value = [], [], []
        for h in range(2):
            chance_low = flat(probs[h, pair])
            chance = chance_low.astype(F32)
            grad_chance = dot_nt(jnp.where(mine[h], outs, jnp.zeros_like(outs)), values)
            inner = jnp.sum(chance * grad_chance, -1, keepdims=True)
            grad_scores = (chance * (grad_chance - inner)).astype(LOW)
            lanes = slice(h * HEAD_DIM, (h + 1) * HEAD_DIM)
            grad_query.append(dot(grad_scores, keys))
            grad_key.append(dot(queries_t[lanes], grad_scores))
            grad_value.append(dot(outs_t[lanes], chance_low))
        grad_query = jnp.where(mine[0], grad_query[0], grad_query[1]) * score_scale
        dqkv[pair, :, :LANES] = grad_query.astype(LOW).reshape(2, ROWS, LANES)
        grad_key, grad_value = jnp.concatenate(grad_key, 0), jnp.concatenate(grad_value, 0)
        if first:
            gk[...], gv[...] = grad_key, grad_value
        else:
            gk[...] += grad_key
            gv[...] += grad_value

    back(0, True)
    back(1, False)
    next(gu_step)
    back(2, False)
    back(3, False)
    thirds = (SHARDS, ROWS, LANES)
    dqkv[:, :, LANES : 2 * LANES] = (gk[...].T * score_scale).astype(LOW).reshape(thirds)
    dqkv[:, :, 2 * LANES :] = gv[...].T.astype(LOW).reshape(thirds)

    da1 = da2

    def spread(zz):
        pair = pl.ds(zz * 2, 2)
        da1[pair] = dot_nt(flat(dqkv[pair]), weight).astype(LOW).reshape(2, ROWS, WIDTH)

    da1_step = plane_sum(here, da1, b["e1"], b["da1_sum"], ends, spread)
    next(da1_step)
    gq = b["gq"]
    gq[...] = dot_tn(flat(a1[...]), flat(dqkv[...])).astype(LOW).reshape(gq.shape)
    gq_step = cross_sum(here, gq, b["gq_total"], b["gq_sum"], ends)
    next(gq_step)
    owner = here.y * 4 + c * 2 + half
    holder = x * 2 + here.near
    stays = (holder == g) & (owner == s)
    gd_away = remote(
        b["gd_total"], gd_land, b["gd_sems"][0].at[0], b["gd_sems"][1].at[0], (holder, owner)
    )
    gu_total = b["gu_total"]

    def store(i, src, dst):
        return pltpu.make_async_copy(src, dst, b["out_sems"].at[i])

    gd_stay = store(0, b["gd_total"], gd_land)
    gu_stay = store(1, gu_total.at[c, corner], gu_land.at[c, corner])
    gq_stay = store(2, b["gq_total"].at[s], gq_land.at[s])
    gu_send, gu_recv = b["gu_sems"]

    def gu_copy(k, i):
        core = here.g if k == 0 else here.sibling[0]
        cc = c if k == 0 else 1 - c
        return remote(
            gu_total.at[cc, here.corners[i]],
            gu_land.at[c, corner],
            gu_send.at[k, i],
            gu_recv.at[k, i],
            (core, here.square[i][1]),
        )

    def gu_came(k, i):
        cc = c if k == 0 else 1 - c
        block = gu_land.at[cc, here.corners[i]]
        return remote(block, block, gu_send.at[k, i], gu_recv.at[k, i], here.sibling)

    others = [(k, i) for k in range(2) for i in range(4) if (k, i) != (0, 0)]

    def send_gd():
        run(gd_step)

        @pl.when(stays)
        def _():
            gd_stay.start()

        @pl.when(jnp.logical_not(stays))
        def _():
            gd_away.start()

    def send_gu():
        run(gu_step)
        gu_stay.start()
        for k, i in others:
            gu_copy(k, i).start()

    go_out = spread_sum(here, b["go_total"], b["go_sum32"], b["go_plane"], ends)
    gq_out = plane_trade(here, b["gq_total"], gq_land, b["gq_sems"], ends, gq_stay)

    def send_go():
        run(go_step)
        next(go_out)

    def send_gq():
        run(gq_step)
        next(gq_out)

    send_gd()
    next(gq_step)
    next(da1_step)
    send_gu()
    send_go()
    next(da1_step)
    send_gq()
    next(da1_step)
    next(go_out)
    next(da1_step)
    run(da1_step)

    e1, n1 = b["e1"][...], b["n1"][...]
    count = jnp.sum(live_rows[pl.ds(s, 1), :].astype(F32), 1, keepdims=True)
    part = jnp.concatenate(
        [
            jnp.sum(e1 * n1, 0, keepdims=True),
            jnp.sum(e1, 0, keepdims=True),
            jnp.sum(e2 * n2, 0, keepdims=True),
            jnp.sum(e2, 0, keepdims=True),
            jnp.broadcast_to(count, (4, WIDTH)),
        ],
        0,
    )
    np_mine, np_land = b["np_mine"], b["np_land"]
    n_send, n_recv = b["np_sems"]
    me, everyone = g * SHARDS + s, GROUPS * SHARDS
    for k in range(SHARDS):
        np_mine[k] = part[:, k * LANES : (k + 1) * LANES]

    def np_copy(k):
        to = (me + k) % everyone
        return remote(
            np_mine.at[to // 4], np_land.at[k], n_send.at[0], n_recv.at[0], (to // SHARDS, to % SHARDS)
        )

    def np_start(k, carry):
        np_copy(k).start()
        return carry

    lax.fori_loop(1, everyone, np_start, 0)
    np_land[0] = np_mine[me // 4]
    b["dx"][...] = centre_back(e1, n1, b["r1"][:, :1], wide(norm, 0)) + b["dh1"][...]
    dx_store = store(3, b["dx"], input_grad)
    dx_store.start()

    f_end()
    b["block"][...] += b["h1"][...]
    block_store = store(4, b["block"], block_out)
    block_store.start()
    run(go_out)
    out_store = store(5, b["go_sum32"], out_sum)
    out_store.start()
    for k, i in others:
        gu_came(k, i).wait_recv()
    gu_stay.wait()
    run(gq_out)

    @pl.when(stays)
    def _():
        gd_stay.wait()

    @pl.when(jnp.logical_not(stays))
    def _():
        gd_away.wait_recv()
        gd_away.wait_send()

    all_came(here, np_land.at[pl.ds(1, everyone - 1)], b["np_sems"])
    total = jnp.sum(np_land[...], 0)
    norm_sum[...] = pltpu.roll(total, LANES - (s % 4) * 32, 1)
    all_sent(here, np_land.at[pl.ds(1, everyone - 1)], b["np_sems"])
    for copy in (dx_store, block_store, out_store):
        copy.wait()
    all_sent(here, norm.at[pl.ds(0, SHARDS - 1)], b["norm_sems"])
    all_sent(here, wq.at[pl.ds(0, SHARDS - 1), g], b["wq_sems"])
    all_sent(here, wu.at[pl.ds(0, SHARDS - 1), x], b["wu_sems"])
    all_sent(here, o_all.at[pl.ds(0, SHARDS - 1)], b["o_sems"])
    for k, i in others:
        gu_copy(k, i).wait_send()
    for copy in (wq_beside, wd_far, wd_beside, wu_beside, *wq_core, *wo_core):
        copy.wait_send()
    for i in range(SHARDS):
        wo_beside(i, g).wait_send()
    for finish in ends:
        finish()


KERNEL_VMEM = 57 * 2**20
SIZES = ((32, 3 * WIDTH), (32, WIDTH), (32, 4 * WIDTH), (ROWS, WIDTH))
SUMS = (
    (LOW, (SHARDS, 32, 3 * LANES)),
    (F32, (32, WIDTH)),
    (LOW, (2, 4, 32, HIDDEN)),
    (LOW, (ROWS, WIDTH)),
)
KINDS = (F32, F32, F32, F32, LOW)
CHUNKS = ((1, 0, 32), (2, 0, 32), (0, 0, 32), (3, 0, ROWS))
AHEAD = 4


def pieces(i):
    if i == 0:
        return [
            (k * WIDTH + j * LANES, LANES, (j,), k * LANES) for j in range(SHARDS) for k in range(3)
        ]
    if i == 2:
        return [
            ((j * 4 + at) * HIDDEN + cc * 256, 256, (cc, at), j * 256)
            for cc in range(2)
            for at in range(4)
            for j in range(2)
        ]
    return [(first, 256, (), first) for first in range(0, WIDTH, 256)]


def adamw_kernel(rates, *refs):
    refs = list(refs)

    def take(n):
        got = refs[:n]
        del refs[:n]
        return got

    norm_sum, *norm_old = take(4)
    sums, olds, passed = take(4), [take(3) for _ in SIZES], take(2)
    norm_new = take(5)
    news, handed = [take(5) for _ in SIZES], take(2)
    held_sum, held_old, held_out = take(4), [take(3) for _ in SIZES], [take(5) for _ in SIZES]
    held_pass = take(2)
    sum_sem, in_sem, out_sem, pass_sem = take(4)
    sum_loads = [pltpu.make_async_copy(sums[i], held_sum[i], sum_sem.at[i]) for i in range(4)]
    loads, stores = [], []
    for n, (i, first, rows) in enumerate(CHUNKS):
        at = pl.ds(first, rows)
        loads.append(
            [
                pltpu.make_async_copy(src.at[at, :], dst.at[at, :], in_sem.at[n, j])
                for j, (src, dst) in enumerate(zip(olds[i], held_old[i]))
            ]
        )
        stores.append(
            [
                pltpu.make_async_copy(src.at[at, :], dst.at[at, :], out_sem.at[n, j])
                for j, (src, dst) in enumerate(zip(held_out[i], news[i]))
            ]
        )
    passes = [pltpu.make_async_copy(passed[i], held_pass[i], pass_sem.at[i]) for i in range(2)]
    hands = [pltpu.make_async_copy(held_pass[i], handed[i], pass_sem.at[2 + i]) for i in range(2)]

    def load(n):
        if n < len(CHUNKS):
            i, first, _ = CHUNKS[n]
            if first == 0:
                sum_loads[i].start()
            for copy in loads[n]:
                copy.start()

    for n in range(AHEAD):
        load(n)
    count = norm_sum[4:5, 0:1]
    results = adamw(norm_sum[0:4, 0:32], count, *[ref[...] for ref in norm_old], rates[4], 0.0)
    for ref, value in zip(norm_new, results):
        ref[...] = value
    inverse = 1.0 / count
    for n, (i, top, rows) in enumerate(CHUNKS):
        if top == 0:
            sum_loads[i].wait()
        for copy in loads[n]:
            copy.wait()
        load(n + AHEAD)
        if n + AHEAD == len(CHUNKS):
            for copy in passes:
                copy.start()
        step = min(rows, 32)

        def some(k, carry):
            at = pl.ds(pl.multiple_of(top + k * step, step), step)
            for first, width, index, start in pieces(i):
                lanes = slice(first, first + width)
                summed = held_sum[i][(*index, at, slice(start, start + width))].astype(F32) * inverse
                old = [ref[at, lanes] for ref in held_old[i]]
                results = adamw(summed, 1.0, *old, rates[i], 0.1)
                for ref, value in zip(held_out[i], results):
                    ref[at, lanes] = value
            return carry

        lax.fori_loop(0, rows // step, some, 0)
        for copy in stores[n]:
            copy.start()
    for k in range(2):
        passes[k].wait()
        hands[k].start()
    for copies in stores:
        for copy in copies:
            copy.wait()
    for copy in hands:
        copy.wait()


def shaped(kind, *shape):
    return jax.ShapeDtypeStruct(shape, kind)


def call_adamw(rates, norms, sums, olds, passed):
    return pl.pallas_call(
        functools.partial(adamw_kernel, rates),
        out_shape=[shaped(kind, *norms[1].shape) for kind in KINDS]
        + [shaped(kind, *size) for size in SIZES for kind in KINDS]
        + [shaped(F32, ROWS, WIDTH)] * 2,
        in_specs=[VMEM] * 4 + [ANY] * 18,
        out_specs=[VMEM] * 5 + [ANY] * 22,
        scratch_shapes=[buffer(kind, *shape) for kind, shape in SUMS]
        + [buffer(F32, *size) for size in SIZES for _ in range(3)]
        + [buffer(kind, *size) for size in SIZES for kind in KINDS]
        + [buffer(F32, ROWS, WIDTH)] * 2
        + [DMA((4,)), DMA((len(CHUNKS), 3)), DMA((len(CHUNKS), 5)), DMA((4,))],
        compiler_params=pltpu.CompilerParams(vmem_limit_bytes=KERNEL_VMEM),
    )(*norms, *sums, *olds, *passed)


def fast_body(
    tokens, cotangent, item_ids, live_mask, qkv_weight, out_weight, up_weight, down_weight, norm_weight,
    qkv_master, qkv_first, qkv_second, out_master, out_first, out_second, up_master, up_first, up_second,
    down_master, down_first, down_second, norm_master, norm_first, norm_second,
):
    rows = item_ids.shape[0]
    args = (
        tokens,
        cotangent,
        item_ids.reshape(SHARDS, ROWS),
        live_mask.reshape(SHARDS, ROWS),
        norm_weight,
        qkv_weight,
        out_weight,
        up_weight,
        down_weight,
    )
    scratch = []
    for kind in scratch_plan().values():
        scratch += kind if isinstance(kind, list) else [kind]
    block_out, input_grad, qkv_sum, up_sum, out_sum, down_sum, norm_sum = pl.pallas_call(
        step_kernel,
        out_shape=[
            shaped(F32, ROWS, WIDTH),
            shaped(F32, ROWS, WIDTH),
            shaped(LOW, SHARDS, 32, 3 * LANES),
            shaped(LOW, 2, 4, 32, HIDDEN),
            shaped(F32, 32, WIDTH),
            shaped(LOW, ROWS, WIDTH),
            shaped(F32, 8, LANES),
        ],
        in_specs=[VMEM] * 5 + [ANY] * 4,
        out_specs=[ANY] * 6 + [VMEM],
        scratch_shapes=scratch,
        compiler_params=pltpu.CompilerParams(
            collective_id=0, has_side_effects=True, vmem_limit_bytes=KERNEL_VMEM
        ),
    )(*args)
    model_width, hidden = tokens.shape[1], up_weight.shape[1]
    rates = (
        model_width ** (-0.5),
        math.sqrt(rows) / 64,
        model_width ** (-0.5),
        hidden ** (-0.5),
        0.4,
    )
    news = call_adamw(
        rates,
        (norm_sum, norm_master, norm_first, norm_second),
        (qkv_sum, out_sum, up_sum, down_sum),
        (
            qkv_master, qkv_first, qkv_second, out_master, out_first, out_second,
            up_master, up_first, up_second, down_master, down_first, down_second,
        ),
        (block_out, input_grad),
    )
    return (*news[25:], *news[5:25], *news[:5])


def suits(mesh):
    return mesh.shape["grp"] == GROUPS and mesh.shape["shard"] == SHARDS


def solution(mesh):
    placed = (
        P(("grp", "shard"), None),
        P(("grp", "shard"), None),
        P("grp"),
        P("grp"),
        P("shard", None),
        P("shard", None),
        P("shard", None),
        P("shard", None),
        P(None, "shard"),
        P(("grp", "shard"), None),
        P(("grp", "shard"), None),
        P(("grp", "shard"), None),
        P(("grp", "shard"), None),
        P(("grp", "shard"), None),
        P(("grp", "shard"), None),
        P(("grp", "shard"), None),
        P(("grp", "shard"), None),
        P(("grp", "shard"), None),
        P(("grp", "shard"), None),
        P(("grp", "shard"), None),
        P(("grp", "shard"), None),
        P(None, ("grp", "shard")),
        P(None, ("grp", "shard")),
        P(None, ("grp", "shard")),
    )
    return jax.shard_map(
        fast_body if suits(mesh) else body,
        mesh=mesh,
        in_specs=placed,
        out_specs=(
            P(("grp", "shard"), None),
            P(("grp", "shard"), None),
            P(("grp", "shard"), None),
            P(("grp", "shard"), None),
            P(("grp", "shard"), None),
            P(("grp", "shard"), None),
            P(("grp", "shard"), None),
            P(("grp", "shard"), None),
            P(("grp", "shard"), None),
            P(("grp", "shard"), None),
            P(("grp", "shard"), None),
            P(("grp", "shard"), None),
            P(("grp", "shard"), None),
            P(("grp", "shard"), None),
            P(("grp", "shard"), None),
            P(("grp", "shard"), None),
            P(("grp", "shard"), None),
            P(("grp", "shard"), None),
            P(("grp", "shard"), None),
            P(("grp", "shard"), None),
            P(("grp", "shard"), None),
            P(("grp", "shard"), None),
            P(None, ("grp", "shard")),
            P(None, ("grp", "shard")),
            P(None, ("grp", "shard")),
            P(None, ("grp", "shard")),
            P(None, ("grp", "shard")),
        ),
        check_vma=False,
    )
```
